512 devices in a mesh: gen: 32 (over z, y_lo), dat: 16 (over y_hi, x, core).
Axes of the slice: x: 4, y: 8 (y_hi: 2, y_lo: 4; y = y_hi * 4 + y_lo), z: 8, core: 2. Of those that a mesh axis runs over, the one named last changes fastest.
Arguments:
- gen_samples: bfloat16 [131072, 256], P(('gen', 'dat')), may hold values from -6 to 6
- data_samples: bfloat16 [12288, 256], P(('dat', 'gen')), may hold values from -6 to 6
- data_potential: float32 [12288], P(('dat', 'gen')), may hold values from -1 to 10
Outputs:
- gen_potential: float32 [131072], P(('gen', 'dat'))
- new_data_potential: float32 [12288], P(('dat', 'gen'))
The draws below stay inside these ranges and needn't reach their ends.
All inputs are finite; a program needn't handle non-finite values.
Results may differ from the reference program's by a relative error of at most 0.0003.
Values may be sent and summed in bfloat16 or wider, within the bound.
A program may use at most 64 MiB of HBM per device.

```python
import jax
import jax.numpy as jnp
from jax import lax

D = 256
NG = 131072
NM = 12288


def draw_data_potential(key, part):
    key = jax.random.fold_in(key, 7)
    first = jax.random.fold_in(key, 0)
    values = jax.random.uniform(first, (NM,), jnp.float32, -1.0, 1.0)
    return values


def shard_levels(rng, dims, cuts, least, high):
    level = 1.0
    for dim, blocks in cuts:
        steps = jax.random.uniform(jax.random.fold_in(jax.random.fold_in(rng, 6), dim), (blocks,), jnp.float32, least / len(cuts), high / len(cuts))
        level = level * jnp.repeat(jnp.exp(steps), dims[dim] // blocks).reshape((-1,) + (1,) * (len(dims) - 1 - dim))
    return level


def bell_draw(own_key, shape, scale, bound, pieces=(), held_as=jnp.bfloat16):
    values = scale * jax.random.normal(own_key, shape, jnp.float32)
    if pieces:
        values = values * shard_levels(own_key, shape, pieces, -0.22, 0.18)
    return jnp.clip(values, -bound, bound).astype(held_as)


def setup_inputs(seed: int = 0) -> dict:
    keys = jax.random.split(jax.random.key(seed), 4)
    return {
        "gen_samples": bell_draw(keys[0], (NG, D), 1.0, 6.0, ((0, 512),)),
        "data_samples": bell_draw(keys[1], (NM, D), 1.0, 6.0, ((0, 512),)),
        "data_potential": draw_data_potential(jax.random.fold_in(keys[3], 71), 0),
    }


EPS = 0.05


def reference(gen_samples, data_samples, data_potential):
    width = gen_samples.shape[1]
    sq_data = jnp.sum(data_samples.astype(jnp.float32) ** 2, axis=1)
    block = min(512, NG)
    count = NG // block
    gen_blocks = gen_samples.reshape(count, block, width)

    def block_cost(rows):
        sq_rows = jnp.sum(rows.astype(jnp.float32) ** 2, axis=1)
        cross = jnp.dot(rows, data_samples.T, preferred_element_type=jnp.float32)
        return (sq_rows[:, None] + sq_data[None, :] - 2.0 * cross) / width

    def row_pass(rows):
        scores = (data_potential[None, :] - block_cost(rows)) / EPS
        top = jnp.max(scores, axis=1)
        total = jnp.sum(jnp.exp(scores - top[:, None]), axis=1)
        return -EPS * (top + jnp.log(total) - jnp.log(jnp.float32(NM)))

    gen_potential = lax.map(row_pass, gen_blocks).reshape(NG)

    def column_pass(carry, item):
        rows, pot = item
        run_max, run_sum = carry
        scores = (pot[:, None] - block_cost(rows)) / EPS
        top = jnp.maximum(run_max, jnp.max(scores, axis=0))
        run_sum = run_sum * jnp.exp(run_max - top) + jnp.sum(jnp.exp(scores - top[None, :]), axis=0)
        return (top, run_sum), None

    start = (jnp.full((NM,), -1e30, jnp.float32), jnp.zeros((NM,), jnp.float32))
    (col_max, col_sum), _ = lax.scan(column_pass, start, (gen_blocks, gen_potential.reshape(count, block)))
    new_data_potential = -EPS * (col_max + jnp.log(col_sum) - jnp.log(jnp.float32(NG)))
    return gen_potential, new_data_potential
```

```python
import math

import jax
import jax.numpy as jnp
from jax import lax
from jax.experimental import pallas as pl
from jax.experimental.pallas import tpu as pltpu
from jax.sharding import PartitionSpec as P

EPS = 0.05
LOG2E = math.log2(math.e)
LN2 = math.log(2.0)
SCALE = LOG2E / EPS
LOW = -1e30
MESH = pl.DeviceIdType.MESH
F32 = jnp.float32
BF16 = jnp.bfloat16

NX, NY, NZ, NC = 4, 8, 8, 2
CHIPS = NY * NZ
ROWS = 256
COLS = 24
WIDTH = 256
HALF = WIDTH // 2
UNIT = 8
UCOLS = UNIT * COLS
KEEP = 1.0 / WIDTH


def hops(d):
    return min(d % 8, -d % 8)


LATTICE = sorted(
    [(p, q) for q in range(8) for p in range(8) if (p + 2 * q) % 4 == 0 and (p, q) != (0, 0)],
    key=lambda o: -(hops(o[0]) + hops(o[1])),
)


def squares(values):
    wide = values.astype(F32)
    wide = wide * wide
    high = wide.astype(BF16)
    low = (wide - high.astype(F32)).astype(BF16)
    ones = jnp.ones((8, WIDTH), BF16)
    dims = (((1,), (1,)), ((), ()))
    return lax.dot_general(ones, high, dims, preferred_element_type=F32) + lax.dot_general(
        ones, low, dims, preferred_element_type=F32
    )


def kernel(
    gen_hbm, data_ref, pot_ref, f_out, g_out,
    x_buf, own, sib, own_u, sib_u, stash, row_m, row_s, row_l, send_l, send_c, recv_c, final,
    local_sem, x_send, x_recv, one_send, one_recv, two_send, two_recv, sib_send, sib_recv,
    row_send, row_recv, col_send, col_recv, fin_send, fin_recv,
):
    gen = lax.axis_index("gen")
    dat = lax.axis_index("dat")
    x, c = (dat // 2) % NX, dat % 2
    y, z = (dat // 8) * 4 + gen % 4, gen // 4

    def device(x_, y_, z_, c_):
        return (z_ * 4 + y_ % 4, (y_ // 4) * 8 + x_ * 2 + c_)

    p, q = y + c * (z - y), z + c * (y - z)

    def in_plane(p_, q_):
        p_, q_ = p_ % 8, q_ % 8
        return device(x, p_ + c * (q_ - p_), q_ + c * (p_ - q_), c)

    def slot_of(p_, q_):
        return ((p_ + 2 * q_) % 4) * 16 + q_ * 2 + p_ // 4

    sibling = device(x, y, z, 1 - c)
    x_peers = [device((x + d) % NX, y, z, c) for d in (2, 1, 3)]
    near = [in_plane(p + 1, q), in_plane(p - 1, q), in_plane(p, q + 1), in_plane(p, q - 1)]
    group = [in_plane(p + dp, q + dq) for dp, dq in LATTICE]
    peers = group + near + x_peers + [sibling]

    barrier = pltpu.get_barrier_semaphore()
    for peer in peers:
        pl.semaphore_signal(barrier, inc=1, device_id=peer, device_id_type=MESH)

    load = pltpu.make_async_copy(gen_hbm, x_buf.at[x], local_sem)
    load.start()

    mine = slot_of(p, q)
    data = data_ref[...].astype(F32)
    own[mine] = jnp.concatenate([data[:, :HALF], data[:, HALF:]], axis=0).astype(BF16)
    term = (pot_ref[...] - squares(data_ref[...])[0:1, :] * KEEP) * SCALE
    own_u[mine] = jnp.concatenate([term, jnp.zeros((1, 128 - COLS), F32)], axis=1)
    row_m[...] = jnp.full(row_m.shape, LOW, F32)
    row_s[...] = jnp.zeros(row_s.shape, F32)

    pl.semaphore_wait(barrier, len(peers))

    def remote(src, dst, send, recv, peer):
        return pltpu.make_async_remote_copy(
            src_ref=src, dst_ref=dst, send_sem=send, recv_sem=recv, device_id=peer, device_id_type=MESH
        )

    for peer in group:
        remote(own.at[mine], own.at[mine], one_send.at[0], one_recv.at[0], peer).start()
        remote(own_u.at[mine], own_u.at[mine], one_send.at[1], one_recv.at[1], peer).start()
    for peer in x_peers:
        remote(gen_hbm, x_buf.at[x], x_send, x_recv, peer).start()

    one = [
        remote(own.at[pl.ds(0, 15)], own.at[pl.ds(0, 15)], one_send.at[0], one_recv.at[0], sibling),
        remote(own_u.at[pl.ds(0, 15)], own_u.at[pl.ds(0, 15)], one_send.at[1], one_recv.at[1], sibling),
    ]
    for copy in one:
        copy.wait_recv()

    kind = (p + 2 * q) % 4
    base = kind * 16

    def block(ref, start):
        return ref.at[pl.ds(start, UNIT)]

    def to_near(k, start, peer):
        return [
            remote(block(own, start), block(own, start), two_send.at[0, k], two_recv.at[0, k], peer),
            remote(block(own_u, start), block(own_u, start), two_send.at[1, k], two_recv.at[1, k], peer),
        ]

    def to_sibling(k, start):
        return [
            remote(block(own, start), block(sib, start), sib_send.at[0, k], sib_recv.at[0, k], sibling),
            remote(block(own_u, start), block(sib_u, start), sib_send.at[1, k], sib_recv.at[1, k], sibling),
        ]

    outgoing = (
        to_near(0, base, near[0]) + to_near(1, base, near[1])
        + to_near(2, base + 8, near[0]) + to_near(3, base + 8, near[1])
        + to_near(4, base, near[2]) + to_near(5, base + 8, near[3])
    )
    for copy in outgoing:
        copy.start()
    for k in range(2):
        for copy in to_sibling(k, base + 8 * k):
            copy.start()

    load.wait()
    gather_x = remote(x_buf.at[pl.ds(0, 3)], x_buf.at[pl.ds(0, 3)], x_send, x_recv, sibling)
    gather_x.wait_recv()

    lane = lax.broadcasted_iota(jnp.int32, (UNIT, COLS, 128), 2)
    sub = lax.broadcasted_iota(jnp.int32, (UNIT, COLS, 128), 1)
    on_diagonal = lane == sub

    def row_unit(data_blocks, terms, place):
        wide = data_blocks[...].astype(F32)
        first = wide[:, :COLS, :].reshape(UCOLS, HALF)
        second = wide[:, COLS:, :].reshape(UCOLS, HALF)
        cols = jnp.concatenate([first.astype(BF16), second.astype(BF16)], axis=1)
        spread = jnp.where(on_diagonal, jnp.broadcast_to(terms[...], (UNIT, COLS, 128)), 0.0)
        term_ = jnp.sum(spread, axis=2, keepdims=True).reshape(UCOLS, 1)
        for b in range(NX):
            lanes = slice(b * ROWS, (b + 1) * ROWS)
            cross = lax.dot_general(cols, x_buf[b], (((1,), (1,)), ((), ())), preferred_element_type=F32)
            scores = cross * (2.0 * KEEP * SCALE) + term_
            stash[pl.ds(place, UNIT), :, lanes] = scores.reshape(UNIT, COLS, ROWS)
            parts = scores.reshape(UCOLS // 8, 8, ROWS)
            old = row_m[:, lanes]
            top = jnp.maximum(old, jnp.max(parts, axis=0))
            row_m[:, lanes] = top
            row_s[:, lanes] = row_s[:, lanes] * jnp.exp2(old - top) + jnp.sum(
                jnp.exp2(parts - top[None]), axis=0
            )

    def own_unit(start):
        row_unit(block(own, start), block(own_u, start), start)

    def sib_unit(start):
        row_unit(block(sib, start), block(sib_u, start), CHIPS + start)

    sp, sq = q, p
    sib_kind = (sp + 2 * sq) % 4

    def arrival(k, kind_):
        far = k // 4
        which = (kind_ + (1 - far) * (2 * (k % 2) - 1) + 2 * far) % 4
        half = (1 - far) * (k // 2) + far * (k % 4)
        return which * 16 + half * 8

    def first_units(k, _):
        own_unit(base + 8 * k)
        return 0

    lax.fori_loop(0, 2, first_units, 0)

    def first_sib(k, _):
        for copy in to_sibling(k, sib_kind * 16 + 8 * k):
            copy.wait_recv()
        sib_unit(sib_kind * 16 + 8 * k)
        return 0

    lax.fori_loop(0, 2, first_sib, 0)

    def next_units(k, _):
        start = arrival(k, kind)
        for copy in to_near(k, start, near[0]):
            copy.wait_recv()
        for copy in to_sibling(k + 2, start):
            copy.start()
        own_unit(start)
        return 0

    lax.fori_loop(0, 6, next_units, 0)

    def next_sib(k, _):
        start = arrival(k, sib_kind)
        for copy in to_sibling(k + 2, start):
            copy.wait_recv()
        sib_unit(start)
        return 0

    lax.fori_loop(0, 6, next_sib, 0)

    m = row_m[...]
    top = jnp.max(m, axis=0, keepdims=True)
    total = jnp.sum(row_s[...] * jnp.exp2(m - top), axis=0, keepdims=True)
    row_l[x] = top + jnp.log2(total)
    for peer in x_peers:
        remote(row_l.at[x], row_l.at[x], row_send, row_recv, peer).start()
    gather_l = remote(row_l.at[pl.ds(0, 3)], row_l.at[pl.ds(0, 3)], row_send, row_recv, sibling)
    gather_l.wait_recv()
    parts = [row_l[b] for b in range(NX)]
    top = jnp.maximum(jnp.maximum(parts[0], parts[1]), jnp.maximum(parts[2], parts[3]))
    total = sum(jnp.exp2(part - top) for part in parts)
    whole = top + jnp.log2(total)
    for b in range(NX):
        send_l[b] = whole[:, b * ROWS : (b + 1) * ROWS]
    lifted = jnp.broadcast_to(whole, (8, NX * ROWS))

    lane2 = lax.broadcasted_iota(jnp.int32, (COLS, 128), 1)
    sub2 = lax.broadcasted_iota(jnp.int32, (COLS, 128), 0)
    at_own = lane2 == sub2
    at_sib = lane2 == sub2 + 64

    def col_scores(place):
        scores = stash[place].reshape(COLS // 8, 8, NX * ROWS) - lifted[None]
        pieces = [scores[:, :, i * 128 : (i + 1) * 128] for i in range(NX * ROWS // 128)]
        peak = pieces[0]
        for piece in pieces[1:]:
            peak = jnp.maximum(peak, piece)
        added = jnp.exp2(pieces[0] - peak)
        for piece in pieces[1:]:
            added = added + jnp.exp2(piece - peak)
        peak, added = peak.reshape(COLS, 128), added.reshape(COLS, 128)
        crest = jnp.max(peak, axis=1, keepdims=True)
        return crest + jnp.log2(jnp.sum(added * jnp.exp2(peak - crest), axis=1, keepdims=True))

    here = y * 8 + z

    def far_first(i):
        return (4 + (i % 2) * ((i + 1) // 2) - (1 - i % 2) * (i // 2)) % 8

    def columns(i, _):
        y_ = (y + far_first(i)) % 8
        for j in range(8):
            z_ = (z + far_first(j)) % 8
            p_, q_ = y_ + c * (z_ - y_), z_ + c * (y_ - z_)
            first = col_scores(slot_of(p_, q_))
            second = col_scores(CHIPS + slot_of(q_, p_))
            line = jnp.where(at_own, first, 0.0) + jnp.where(at_sib, second, 0.0)
            line = jnp.sum(line, axis=0, keepdims=True)
            there = y_ * 8 + z_
            if j < 7:
                send_c[there] = line
                remote(send_c.at[there], recv_c.at[here], col_send, col_recv, device(x, y_, z_, c)).start()
            else:

                @pl.when(i < 7)
                def _(line=line, there=there, y_=y_, z_=z_):
                    send_c[there] = line
                    remote(send_c.at[there], recv_c.at[here], col_send, col_recv, device(x, y_, z_, c)).start()

                @pl.when(i == 7)
                def _(line=line):
                    recv_c[here] = line

        return 0

    lax.fori_loop(0, 8, columns, 0)

    sq_rows = squares(x_buf[x])[0:1, :]
    f_out[...] = sq_rows * KEEP - (EPS * LN2) * send_l[x] + EPS * math.log(float(CHIPS * NX * NC * COLS))

    gather_c = remote(recv_c.at[pl.ds(0, CHIPS - 1)], recv_c.at[pl.ds(0, CHIPS - 1)], col_send, col_recv, sibling)
    gather_c.wait_recv()
    lines = recv_c[...]
    top = jnp.max(lines, axis=0)
    final[0] = top + jnp.log2(jnp.sum(jnp.exp2(lines - top[None]), axis=0))
    swap = remote(final.at[0], final.at[1], fin_send, fin_recv, sibling)
    swap.start()
    swap.wait_recv()
    ours, theirs = final[0][:, :COLS], final[1][:, 64 : 64 + COLS]
    top = jnp.maximum(ours, theirs)
    score = top + jnp.log2(jnp.exp2(ours - top) + jnp.exp2(theirs - top))
    g_out[...] = pot_ref[...] - (EPS * LN2) * score + EPS * (
        math.log(float(CHIPS * NX * NC * ROWS)) - math.log(float(CHIPS * NX * NC * COLS))
    )

    for copy in one + [gather_x, gather_l, gather_c, swap] + outgoing:
        copy.wait_send()

    def sent(k, _):
        for copy in to_sibling(k, 0):
            copy.wait_send()
        return 0

    lax.fori_loop(0, 8, sent, 0)


def per_device(gen_samples, data_samples, data_potential):
    vmem = pl.BlockSpec(memory_space=pltpu.VMEM)
    dma = pltpu.SemaphoreType.DMA
    f, g = pl.pallas_call(
        kernel,
        out_shape=(jax.ShapeDtypeStruct((1, ROWS), F32), jax.ShapeDtypeStruct((1, COLS), F32)),
        in_specs=[pl.BlockSpec(memory_space=pl.ANY), vmem, vmem],
        out_specs=(vmem, vmem),
        scratch_shapes=[
            pltpu.VMEM((NX, ROWS, WIDTH), BF16),
            pltpu.VMEM((CHIPS, 2 * COLS, HALF), BF16),
            pltpu.VMEM((CHIPS, 2 * COLS, HALF), BF16),
            pltpu.VMEM((CHIPS, 1, 128), F32),
            pltpu.VMEM((CHIPS, 1, 128), F32),
            pltpu.VMEM((2 * CHIPS, COLS, NX * ROWS), F32),
            pltpu.VMEM((8, NX * ROWS), F32),
            pltpu.VMEM((8, NX * ROWS), F32),
            pltpu.VMEM((NX, 1, NX * ROWS), F32),
            pltpu.VMEM((NX, 1, ROWS), F32),
            pltpu.VMEM((CHIPS, 1, 128), F32),
            pltpu.VMEM((CHIPS, 1, 128), F32),
            pltpu.VMEM((2, 1, 128), F32),
            dma, dma, dma,
            dma((2,)), dma((2,)), dma((2, 6)), dma((2, 6)), dma((2, 8)), dma((2, 8)),
            dma, dma, dma, dma, dma, dma,
        ],
        compiler_params=pltpu.CompilerParams(
            collective_id=0, has_side_effects=True, vmem_limit_bytes=40 * 2**20
        ),
    )(gen_samples, data_samples, data_potential.reshape(1, COLS))
    return f.reshape(ROWS), g.reshape(COLS)


def solution(mesh):
    in_specs = (P(("gen", "dat"), None), P(("dat", "gen"), None), P(("dat", "gen")))
    out_specs = (P(("gen", "dat")), P(("dat", "gen")))
    return jax.shard_map(
        per_device, mesh=mesh, in_specs=in_specs, out_specs=out_specs, check_vma=False
    )
```

```python
import math

import jax
import jax.numpy as jnp
from jax import lax
from jax.experimental import pallas as pl
from jax.experimental.pallas import tpu as pltpu
from jax.sharding import PartitionSpec as P

EPS = 0.05
LOG2E = math.log2(math.e)
LN2 = math.log(2.0)
SCALE = LOG2E / EPS
LOW = -1e30
MESH = pl.DeviceIdType.MESH
F32 = jnp.float32
BF16 = jnp.bfloat16

NX, NY, NZ, NC = 4, 8, 8, 2
CHIPS = NY * NZ
ROWS = 256
COLS = 24
WIDTH = 256
HALF = WIDTH // 2
UNIT = 16
UCOLS = UNIT * COLS
KEEP = 1.0 / WIDTH


def hops(d):
    return min(d % 8, -d % 8)


LATTICE = sorted(
    [(p, q) for q in range(8) for p in range(8) if (p + 2 * q) % 4 == 0 and (p, q) != (0, 0)],
    key=lambda o: -(hops(o[0]) + hops(o[1])),
)


def squares(values):
    wide = values.astype(F32)
    wide = wide * wide
    high = wide.astype(BF16)
    low = (wide - high.astype(F32)).astype(BF16)
    ones = jnp.ones((8, WIDTH), BF16)
    dims = (((1,), (1,)), ((), ()))
    return lax.dot_general(ones, high, dims, preferred_element_type=F32) + lax.dot_general(
        ones, low, dims, preferred_element_type=F32
    )


def kernel(
    gen_hbm, data_hbm, pot_hbm, f_out, g_out,
    x_buf, data_buf, pot_buf, sq_buf, blocks, terms, stash, row_m, row_s, row_l, send_l,
    peak_a, added_a, peak_b, added_b, send_q, recv_q, send_p, recv_p, final,
    local_sem, x_send, x_recv, one_send, one_recv, two_send, two_recv, sib_send, sib_recv,
    row_send, row_recv, q_send, q_recv, p_send, p_recv, fin_send, fin_recv,
):
    gen = lax.axis_index("gen")
    dat = lax.axis_index("dat")
    x, c = (dat // 2) % NX, dat % 2
    y, z = (dat // 8) * 4 + gen % 4, gen // 4

    def device(x_, y_, z_, c_):
        return (z_ * 4 + y_ % 4, (y_ // 4) * 8 + x_ * 2 + c_)

    p, q = y + c * (z - y), z + c * (y - z)

    def in_plane(p_, q_):
        p_, q_ = p_ % 8, q_ % 8
        return device(x, p_ + c * (q_ - p_), q_ + c * (p_ - q_), c)

    def slot_of(p_, q_):
        return ((p_ + 2 * q_) % 4) * 16 + q_ * 2 + p_ // 4

    sibling = device(x, y, z, 1 - c)
    x_peers = [device((x + d) % NX, y, z, c) for d in (2, 1, 3)]
    near = [in_plane(p + 1, q), in_plane(p - 1, q), in_plane(p, q + 1), in_plane(p, q - 1)]
    group = [in_plane(p + dp, q + dq) for dp, dq in LATTICE]

    loads = [
        pltpu.make_async_copy(data_hbm, data_buf, local_sem.at[0]),
        pltpu.make_async_copy(pot_hbm, pot_buf, local_sem.at[1]),
        pltpu.make_async_copy(gen_hbm, x_buf.at[x], local_sem.at[2]),
    ]
    for copy in loads:
        copy.start()

    peers = group + near + x_peers + [sibling]
    barrier = pltpu.get_barrier_semaphore()
    for peer in peers:
        pl.semaphore_signal(barrier, inc=1, device_id=peer, device_id_type=MESH)

    mine = slot_of(p, q)
    for copy in loads[:2]:
        copy.wait()
    data = data_buf[...].astype(F32)
    blocks[mine] = jnp.concatenate([data[:, :HALF], data[:, HALF:]], axis=0).astype(BF16)
    term = (pot_buf[...] - squares(data_buf[...])[0:1, :] * KEEP) * SCALE
    terms[mine] = jnp.concatenate([term, jnp.zeros((1, 128 - COLS), F32)], axis=1)

    pl.semaphore_wait(barrier, len(peers))

    def remote(src, dst, send, recv, peer):
        return pltpu.make_async_remote_copy(
            src_ref=src, dst_ref=dst, send_sem=send, recv_sem=recv, device_id=peer, device_id_type=MESH
        )

    for peer in group:
        remote(blocks.at[mine], blocks.at[mine], one_send.at[0], one_recv.at[0], peer).start()
    for peer in x_peers:
        remote(gen_hbm, x_buf.at[x], x_send, x_recv, peer).start()
    for peer in group:
        remote(terms.at[mine], terms.at[mine], one_send.at[1], one_recv.at[1], peer).start()

    row_m[...] = jnp.full(row_m.shape, LOW, F32)
    row_s[...] = jnp.zeros(row_s.shape, F32)
    loads[2].wait()
    sq_buf[...] = squares(x_buf[x])[0:1, :]

    one = [
        remote(ref.at[pl.ds(0, 15)], ref.at[pl.ds(0, 15)], one_send.at[i], one_recv.at[i], sibling)
        for i, ref in enumerate((blocks, terms))
    ]
    for copy in one:
        copy.wait_recv()

    kind, sib_kind = (p + 2 * q) % 4, (q + 2 * p) % 4

    def to_near(k, start, count, peer):
        return [
            remote(ref.at[pl.ds(start, count)], ref.at[pl.ds(start, count)], two_send.at[i, k], two_recv.at[i, k], peer)
            for i, ref in enumerate((blocks, terms))
        ]

    def to_sibling(k, start):
        return [
            remote(ref.at[pl.ds(start, 16)], ref.at[pl.ds(CHIPS + start, 16)], sib_send.at[i, k], sib_recv.at[i, k], sibling)
            for i, ref in enumerate((blocks, terms))
        ]

    base = kind * 16
    outgoing = (
        to_near(2, base, 8, near[2]) + to_near(3, base + 8, 8, near[3])
        + to_near(0, base, 16, near[0]) + to_near(1, base, 16, near[1])
    )
    for copy in outgoing:
        copy.start()
    for copy in to_sibling(0, base):
        copy.start()

    gather_x = remote(x_buf.at[pl.ds(0, 3)], x_buf.at[pl.ds(0, 3)], x_send, x_recv, sibling)
    gather_x.wait_recv()

    def place(k, kind_):
        return ((kind_ + 2 * k + 3 * (k // 2)) % 4) * 16

    lane = lax.broadcasted_iota(jnp.int32, (UNIT, COLS, 128), 2)
    sub = lax.broadcasted_iota(jnp.int32, (UNIT, COLS, 128), 1)
    on_diagonal = lane == sub

    def row_unit(step, _):
        k, other = step // 2, step % 2
        mine_at, sib_at = place(k, kind), place(k, sib_kind)

        @pl.when(step == 2)
        def _():
            for copy in to_near(2, base, 8, near[2]) + to_near(3, base, 8, near[3]):
                copy.wait_recv()

        @pl.when((step >= 4) & (other == 0))
        def _():
            for copy in to_near(k - 2, base, 16, near[0]):
                copy.wait_recv()

        @pl.when((step >= 2) & (other == 0))
        def _():
            for copy in to_sibling(k, mine_at):
                copy.start()

        @pl.when(other == 1)
        def _():
            for copy in to_sibling(k, sib_at):
                copy.wait_recv()

        start = mine_at + other * (CHIPS + sib_at - mine_at)
        wide = blocks[pl.ds(start, UNIT)].astype(F32)
        first = wide[:, :COLS, :].reshape(UCOLS, HALF)
        second = wide[:, COLS:, :].reshape(UCOLS, HALF)
        cols = jnp.concatenate([first.astype(BF16), second.astype(BF16)], axis=1)
        spread = jnp.where(on_diagonal, jnp.broadcast_to(terms[pl.ds(start, UNIT)], (UNIT, COLS, 128)), 0.0)
        term_ = jnp.sum(spread, axis=2, keepdims=True).reshape(UCOLS, 1)
        for b in range(NX):
            lanes = slice(b * ROWS, (b + 1) * ROWS)
            cross = lax.dot_general(cols, x_buf[b], (((1,), (1,)), ((), ())), preferred_element_type=F32)
            scores = cross * (2.0 * KEEP * SCALE) + term_
            stash[pl.ds(start, UNIT), :, lanes] = scores.reshape(UNIT, COLS, ROWS)
            parts = scores.reshape(UCOLS // 8, 8, ROWS)
            old = row_m[:, lanes]
            top = jnp.maximum(old, jnp.max(parts, axis=0))
            row_m[:, lanes] = top
            row_s[:, lanes] = row_s[:, lanes] * jnp.exp2(old - top) + jnp.sum(
                jnp.exp2(parts - top[None]), axis=0
            )
        return 0

    lax.fori_loop(0, 8, row_unit, 0)

    m = row_m[...]
    top = jnp.max(m, axis=0, keepdims=True)
    total = jnp.sum(row_s[...] * jnp.exp2(m - top), axis=0, keepdims=True)
    row_l[x] = top + jnp.log2(total)
    for peer in x_peers:
        remote(row_l.at[x], row_l.at[x], row_send, row_recv, peer).start()
    gather_l = remote(row_l.at[pl.ds(0, 3)], row_l.at[pl.ds(0, 3)], row_send, row_recv, sibling)
    gather_l.wait_recv()
    parts = [row_l[b] for b in range(NX)]
    top = jnp.maximum(jnp.maximum(parts[0], parts[1]), jnp.maximum(parts[2], parts[3]))
    total = sum(jnp.exp2(part - top) for part in parts)
    whole = top + jnp.log2(total)
    for b in range(NX):
        send_l[b] = whole[:, b * ROWS : (b + 1) * ROWS]
    lifted = jnp.broadcast_to(whole, (8, NX * ROWS))

    def line_of(i):
        return (q + 4 + (i % 2) * ((i + 1) // 2) - (1 - i % 2) * (i // 2)) % 8

    def line_parts(q_, peak_ref, added_ref):
        for h in range(2):
            for j in range(8):
                at = slot_of(j, q_) if h == 0 else CHIPS + slot_of(q_, j)
                scores = stash[at].reshape(COLS // 8, 8, NX * ROWS) - lifted[None]
                pieces = [scores[:, :, i * 128 : (i + 1) * 128] for i in range(NX * ROWS // 128)]
                peak = pieces[0]
                for piece in pieces[1:]:
                    peak = jnp.maximum(peak, piece)
                added = jnp.exp2(pieces[0] - peak)
                for piece in pieces[1:]:
                    added = added + jnp.exp2(piece - peak)
                to = (h * 8 + j) * COLS
                peak_ref[to : to + COLS, :] = peak.reshape(COLS, 128)
                added_ref[to : to + COLS, :] = added.reshape(COLS, 128)

    def line_sums(peak_ref, added_ref):
        peak, added = jnp.transpose(peak_ref[...]), jnp.transpose(added_ref[...])
        crest = jnp.max(peak, axis=0, keepdims=True)
        return crest + jnp.log2(jnp.sum(added * jnp.exp2(peak - crest), axis=0, keepdims=True))

    def line_send(q_, peak_ref, added_ref):
        send_q[q_] = line_sums(peak_ref, added_ref)
        remote(send_q.at[q_], recv_q.at[q], q_send, q_recv, in_plane(p, q_)).start()

    a, b = (peak_a, added_a), (peak_b, added_b)
    line_parts(line_of(0), *a)

    def lines(i, _):
        line_parts(line_of(2 * i + 1), *b)
        line_send(line_of(2 * i), *a)
        line_parts(line_of(2 * i + 2), *a)
        line_send(line_of(2 * i + 1), *b)
        return 0

    lax.fori_loop(0, 3, lines, 0)
    line_parts(q, *b)
    line_send(line_of(6), *a)
    recv_q[q] = line_sums(*b)

    f_out[...] = sq_buf[...] * KEEP - (EPS * LN2) * send_l[x] + EPS * math.log(float(CHIPS * NX * NC * COLS))

    def combined(values):
        top = jnp.max(values, axis=0)
        return top + jnp.log2(jnp.sum(jnp.exp2(values - top[None]), axis=0))

    gather_q = remote(recv_q.at[pl.ds(0, 7)], recv_q.at[pl.ds(0, 7)], q_send, q_recv, sibling)
    gather_q.wait_recv()
    line = combined(recv_q[...])
    send_p[...] = line
    recv_p[p] = line
    for d in (4, 3, 5, 2, 6, 1, 7):
        remote(send_p, recv_p.at[p], p_send, p_recv, in_plane(p + d, q)).start()
    gather_p = remote(recv_p.at[pl.ds(0, 7)], recv_p.at[pl.ds(0, 7)], p_send, p_recv, sibling)
    gather_p.wait_recv()
    line = combined(recv_p[...])

    def segment(first):
        return sum(
            jnp.where(p == j, line[:, first + j * COLS : first + (j + 1) * COLS], 0.0) for j in range(8)
        )

    ours, theirs = segment(0), segment(8 * COLS)
    final[0] = jnp.concatenate([theirs, jnp.zeros((1, 128 - COLS), F32)], axis=1)
    swap = remote(final.at[0], final.at[1], fin_send, fin_recv, sibling)
    swap.start()
    swap.wait_recv()
    theirs = final[1][:, :COLS]
    top = jnp.maximum(ours, theirs)
    score = top + jnp.log2(jnp.exp2(ours - top) + jnp.exp2(theirs - top))
    g_out[...] = pot_buf[...] - (EPS * LN2) * score + EPS * (
        math.log(float(CHIPS * NX * NC * ROWS)) - math.log(float(CHIPS * NX * NC * COLS))
    )

    for copy in one + [gather_x, gather_l, gather_q, gather_p, swap] + outgoing:
        copy.wait_send()
    for k in range(4):
        for copy in to_sibling(k, 0):
            copy.wait_send()


def per_device(gen_samples, data_samples, data_potential):
    hbm = pl.BlockSpec(memory_space=pltpu.HBM)
    vmem = pl.BlockSpec(memory_space=pltpu.VMEM)
    dma = pltpu.SemaphoreType.DMA
    span = 2 * 8 * COLS
    f, g = pl.pallas_call(
        kernel,
        out_shape=(jax.ShapeDtypeStruct((1, ROWS), F32), jax.ShapeDtypeStruct((1, COLS), F32)),
        in_specs=[hbm, hbm, hbm],
        out_specs=(vmem, vmem),
        scratch_shapes=[
            pltpu.VMEM((NX, ROWS, WIDTH), BF16),
            pltpu.VMEM((COLS, WIDTH), BF16),
            pltpu.VMEM((1, COLS), F32),
            pltpu.VMEM((1, ROWS), F32),
            pltpu.VMEM((2 * CHIPS, 2 * COLS, HALF), BF16),
            pltpu.VMEM((2 * CHIPS, 1, 128), F32),
            pltpu.VMEM((2 * CHIPS, COLS, NX * ROWS), F32),
            pltpu.VMEM((8, NX * ROWS), F32),
            pltpu.VMEM((8, NX * ROWS), F32),
            pltpu.VMEM((NX, 1, NX * ROWS), F32),
            pltpu.VMEM((NX, 1, ROWS), F32),
            pltpu.VMEM((span, 128), F32),
            pltpu.VMEM((span, 128), F32),
            pltpu.VMEM((span, 128), F32),
            pltpu.VMEM((span, 128), F32),
            pltpu.VMEM((8, 1, span), F32),
            pltpu.VMEM((8, 1, span), F32),
            pltpu.VMEM((1, span), F32),
            pltpu.VMEM((8, 1, span), F32),
            pltpu.VMEM((2, 1, 128), F32),
            dma((3,)), dma, dma,
            dma((2,)), dma((2,)), dma((2, 4)), dma((2, 4)), dma((2, 4)), dma((2, 4)),
            dma, dma, dma, dma, dma, dma, dma, dma,
        ],
        compiler_params=pltpu.CompilerParams(
            collective_id=0, has_side_effects=True, vmem_limit_bytes=40 * 2**20
        ),
    )(*[
        pltpu.with_memory_space_constraint(array, pltpu.HBM)
        for array in (gen_samples, data_samples, data_potential.reshape(1, COLS))
    ])
    return f.reshape(ROWS), g.reshape(COLS)


def solution(mesh):
    in_specs = (P(("gen", "dat"), None), P(("dat", "gen"), None), P(("dat", "gen")))
    out_specs = (P(("gen", "dat")), P(("dat", "gen")))
    return jax.shard_map(
        per_device, mesh=mesh, in_specs=in_specs, out_specs=out_specs, check_vma=False
    )
```

```python
import math

import jax
import jax.numpy as jnp
from jax import lax
from jax.experimental import pallas as pl
from jax.experimental.pallas import tpu as pltpu
from jax.sharding import PartitionSpec as P

EPS = 0.05
LOG2E = math.log2(math.e)
LN2 = math.log(2.0)
SCALE = LOG2E / EPS
LOW = -1e30
MESH = pl.DeviceIdType.MESH
F32 = jnp.float32
BF16 = jnp.bfloat16

NX, NY, NZ, NC = 4, 8, 8, 2
CHIPS = NY * NZ
ROWS = 256
COLS = 24
WIDTH = 256
HALF = WIDTH // 2
UNIT = 16
UCOLS = UNIT * COLS
KEEP = 1.0 / WIDTH


def hops(d):
    return min(d % 8, -d % 8)


FAR_FIRST = (4, 3, 5, 2, 6, 1, 7, 0)

LATTICE = sorted(
    [(p, q) for q in range(8) for p in range(8) if (p + 2 * q) % 4 == 0 and (p, q) != (0, 0)],
    key=lambda o: -(hops(o[0]) + hops(o[1])),
)


def squares(values):
    wide = values.astype(F32)
    wide = wide * wide
    high = wide.astype(BF16)
    low = (wide - high.astype(F32)).astype(BF16)
    ones = jnp.ones((8, WIDTH), BF16)
    dims = (((1,), (1,)), ((), ()))
    return lax.dot_general(ones, high, dims, preferred_element_type=F32) + lax.dot_general(
        ones, low, dims, preferred_element_type=F32
    )


def kernel(
    gen_hbm, data_hbm, pot_hbm, f_out, g_out,
    x_buf, data_buf, pot_buf, sq_buf, blocks, terms, stash, row_m, row_s, row_l, send_l,
    peak_a, added_a, peak_b, added_b, send_c, recv_c, final,
    local_sem, x_send, x_recv, one_send, one_recv, two_send, two_recv, sib_send, sib_recv,
    row_send, row_recv, col_send, col_recv, fin_send, fin_recv,
):
    gen = lax.axis_index("gen")
    dat = lax.axis_index("dat")
    x, c = (dat // 2) % NX, dat % 2
    y, z = (dat // 8) * 4 + gen % 4, gen // 4

    def device(x_, y_, z_, c_):
        return (z_ * 4 + y_ % 4, (y_ // 4) * 8 + x_ * 2 + c_)

    p, q = y + c * (z - y), z + c * (y - z)

    def in_plane(p_, q_):
        p_, q_ = p_ % 8, q_ % 8
        return device(x, p_ + c * (q_ - p_), q_ + c * (p_ - q_), c)

    def slot_of(p_, q_):
        return ((p_ + 2 * q_) % 4) * 16 + q_ * 2 + p_ // 4

    sibling = device(x, y, z, 1 - c)
    x_peers = [device((x + d) % NX, y, z, c) for d in (2, 1, 3)]
    near = [in_plane(p + 1, q), in_plane(p - 1, q), in_plane(p, q + 1), in_plane(p, q - 1)]
    group = [in_plane(p + dp, q + dq) for dp, dq in LATTICE]

    loads = [
        pltpu.make_async_copy(data_hbm, data_buf, local_sem.at[0]),
        pltpu.make_async_copy(pot_hbm, pot_buf, local_sem.at[1]),
        pltpu.make_async_copy(gen_hbm, x_buf.at[x], local_sem.at[2]),
    ]
    for copy in loads:
        copy.start()

    peers = group + near + x_peers + [sibling]
    barrier = pltpu.get_barrier_semaphore()
    for peer in peers:
        pl.semaphore_signal(barrier, inc=1, device_id=peer, device_id_type=MESH)

    mine = slot_of(p, q)
    for copy in loads[:2]:
        copy.wait()
    data = data_buf[...].astype(F32)
    blocks[mine] = jnp.concatenate([data[:, :HALF], data[:, HALF:]], axis=0).astype(BF16)
    term = (pot_buf[...] - squares(data_buf[...])[0:1, :] * KEEP) * SCALE
    terms[mine] = jnp.concatenate([term, jnp.zeros((1, 128 - COLS), F32)], axis=1)

    pl.semaphore_wait(barrier, len(peers))

    def remote(src, dst, send, recv, peer):
        return pltpu.make_async_remote_copy(
            src_ref=src, dst_ref=dst, send_sem=send, recv_sem=recv, device_id=peer, device_id_type=MESH
        )

    for peer in group:
        remote(blocks.at[mine], blocks.at[mine], one_send.at[0], one_recv.at[0], peer).start()
    for peer in x_peers:
        remote(gen_hbm, x_buf.at[x], x_send, x_recv, peer).start()
    for peer in group:
        remote(terms.at[mine], terms.at[mine], one_send.at[1], one_recv.at[1], peer).start()

    row_m[...] = jnp.full(row_m.shape, LOW, F32)
    row_s[...] = jnp.zeros(row_s.shape, F32)
    loads[2].wait()
    sq_buf[...] = squares(x_buf[x])[0:1, :]

    one = [
        remote(ref.at[pl.ds(0, 15)], ref.at[pl.ds(0, 15)], one_send.at[i], one_recv.at[i], sibling)
        for i, ref in enumerate((blocks, terms))
    ]
    for copy in one:
        copy.wait_recv()

    kind, sib_kind = (p + 2 * q) % 4, (q + 2 * p) % 4

    def to_near(k, start, count, peer):
        return [
            remote(ref.at[pl.ds(start, count)], ref.at[pl.ds(start, count)], two_send.at[i, k], two_recv.at[i, k], peer)
            for i, ref in enumerate((blocks, terms))
        ]

    def to_sibling(k, start, count):
        return [
            remote(
                ref.at[pl.ds(start, count)], ref.at[pl.ds(CHIPS + start, count)],
                sib_send.at[i, k], sib_recv.at[i, k], sibling,
            )
            for i, ref in enumerate((blocks, terms))
        ]

    base, sib_base = kind * 16, sib_kind * 16
    outgoing = (
        to_near(0, base, 8, near[2]) + to_near(1, base + 8, 8, near[3])
        + to_near(2, base, 8, near[0]) + to_near(3, base, 8, near[1])
        + to_near(4, base + 8, 8, near[0]) + to_near(5, base + 8, 8, near[1])
    )
    for copy in outgoing:
        copy.start()
    for copy in to_sibling(0, base, 16):
        copy.start()

    gather_x = remote(x_buf.at[pl.ds(0, 3)], x_buf.at[pl.ds(0, 3)], x_send, x_recv, sibling)
    gather_x.wait_recv()

    def place(k, kind_):
        return ((kind_ + 2 * k + 3 * (k // 2)) % 4) * 16

    lane = lax.broadcasted_iota(jnp.int32, (UNIT, COLS, 128), 2)
    sub = lax.broadcasted_iota(jnp.int32, (UNIT, COLS, 128), 1)
    on_diagonal = lane == sub

    def row_unit(start):
        wide = blocks[pl.ds(start, UNIT)].astype(F32)
        first = wide[:, :COLS, :].reshape(UCOLS, HALF)
        second = wide[:, COLS:, :].reshape(UCOLS, HALF)
        cols = jnp.concatenate([first.astype(BF16), second.astype(BF16)], axis=1)
        spread = jnp.where(on_diagonal, jnp.broadcast_to(terms[pl.ds(start, UNIT)], (UNIT, COLS, 128)), 0.0)
        term_ = jnp.sum(spread, axis=2, keepdims=True).reshape(UCOLS, 1)
        for b in range(NX):
            lanes = slice(b * ROWS, (b + 1) * ROWS)
            cross = lax.dot_general(cols, x_buf[b], (((1,), (1,)), ((), ())), preferred_element_type=F32)
            scores = cross * (2.0 * KEEP * SCALE) + term_
            stash[pl.ds(start, UNIT), :, lanes] = scores.reshape(UNIT, COLS, ROWS)
            parts = scores.reshape(UCOLS // 8, 8, ROWS)
            old = row_m[:, lanes]
            top = jnp.maximum(old, jnp.max(parts, axis=0))
            row_m[:, lanes] = top
            row_s[:, lanes] = row_s[:, lanes] * jnp.exp2(old - top) + jnp.sum(
                jnp.exp2(parts - top[None]), axis=0
            )

    def first_units(step, _):
        @pl.when(step == 1)
        def _():
            for copy in to_sibling(0, sib_base, 16):
                copy.wait_recv()

        row_unit(base + step * (CHIPS + sib_base - base))
        return 0

    lax.fori_loop(0, 2, first_units, 0)

    def next_units(step, _):
        k, other = step % 3 + 1, step // 3
        opposite, below, above = (place(i, kind) for i in (1, 2, 3))

        @pl.when(step == 0)
        def _():
            for copy in to_near(0, opposite, 8, near[2]) + to_near(1, opposite, 8, near[3]):
                copy.wait_recv()
            for copy in to_sibling(1, opposite, 16):
                copy.start()

        @pl.when(step == 1)
        def _():
            for half in range(2):
                for i, start in ((2, below), (3, above)):
                    for copy in to_near(i + 2 * half, start, 8, near[0]):
                        copy.wait_recv()
                    for copy in to_sibling(i + 2 * half, start + 8 * half, 8):
                        copy.start()

        @pl.when(step == 3)
        def _():
            for copy in to_sibling(1, opposite, 16):
                copy.wait_recv()

        @pl.when(step == 4)
        def _():
            for copy in to_sibling(2, below, 8) + to_sibling(4, below, 8):
                copy.wait_recv()

        @pl.when(step == 5)
        def _():
            for copy in to_sibling(3, above, 8) + to_sibling(5, above, 8):
                copy.wait_recv()

        mine_at, sib_at = place(k, kind), place(k, sib_kind)
        row_unit(mine_at + other * (CHIPS + sib_at - mine_at))
        return 0

    lax.fori_loop(0, 6, next_units, 0)

    m = row_m[...]
    top = jnp.max(m, axis=0, keepdims=True)
    total = jnp.sum(row_s[...] * jnp.exp2(m - top), axis=0, keepdims=True)
    row_l[x] = top + jnp.log2(total)
    for peer in x_peers:
        remote(row_l.at[x], row_l.at[x], row_send, row_recv, peer).start()
    gather_l = remote(row_l.at[pl.ds(0, 3)], row_l.at[pl.ds(0, 3)], row_send, row_recv, sibling)
    gather_l.wait_recv()
    parts = [row_l[b] for b in range(NX)]
    top = jnp.maximum(jnp.maximum(parts[0], parts[1]), jnp.maximum(parts[2], parts[3]))
    total = sum(jnp.exp2(part - top) for part in parts)
    whole = top + jnp.log2(total)
    for b in range(NX):
        send_l[b] = whole[:, b * ROWS : (b + 1) * ROWS]
    lifted = jnp.broadcast_to(whole, (8, NX * ROWS))

    def line_of(i):
        return (q + 4 + (i % 2) * ((i + 1) // 2) - (1 - i % 2) * (i // 2)) % 8

    def line_parts(q_, peak_ref, added_ref):
        for h in range(2):
            for j in range(8):
                at = slot_of(j, q_) if h == 0 else CHIPS + slot_of(q_, j)
                scores = stash[at].reshape(COLS // 8, 8, NX * ROWS) - lifted[None]
                pieces = [scores[:, :, i * 128 : (i + 1) * 128] for i in range(NX * ROWS // 128)]
                peak = pieces[0]
                for piece in pieces[1:]:
                    peak = jnp.maximum(peak, piece)
                added = jnp.exp2(pieces[0] - peak)
                for piece in pieces[1:]:
                    added = added + jnp.exp2(piece - peak)
                to = (h * 8 + j) * COLS
                peak_ref[to : to + COLS, :] = peak.reshape(COLS, 128)
                added_ref[to : to + COLS, :] = added.reshape(COLS, 128)

    def line_sums(peak_ref, added_ref):
        peak, added = jnp.transpose(peak_ref[...]), jnp.transpose(added_ref[...])
        crest = jnp.max(peak, axis=0, keepdims=True)
        return crest + jnp.log2(jnp.sum(added * jnp.exp2(peak - crest), axis=0, keepdims=True))

    def line_send(q_, peak_ref, added_ref):
        send_c[q_] = line_sums(peak_ref, added_ref)
        for d in FAR_FIRST:
            remote(send_c.at[q_], recv_c.at[here], col_send, col_recv, in_plane(p + d, q_)).start()

    here = p * 8 + q
    a, b = (peak_a, added_a), (peak_b, added_b)
    line_parts(line_of(0), *a)

    def lines(i, _):
        line_parts(line_of(2 * i + 1), *b)
        line_send(line_of(2 * i), *a)
        line_parts(line_of(2 * i + 2), *a)
        line_send(line_of(2 * i + 1), *b)
        return 0

    lax.fori_loop(0, 3, lines, 0)
    line_parts(q, *b)
    line_send(line_of(6), *a)
    sums = line_sums(*b)
    send_c[q] = sums
    for d in FAR_FIRST[:-1]:
        remote(send_c.at[q], recv_c.at[here], col_send, col_recv, in_plane(p + d, q)).start()
    recv_c[here] = sums

    f_out[...] = sq_buf[...] * KEEP - (EPS * LN2) * send_l[x] + EPS * math.log(float(CHIPS * NX * NC * COLS))

    def combined(values):
        top = jnp.max(values, axis=0)
        return top + jnp.log2(jnp.sum(jnp.exp2(values - top[None]), axis=0))

    gather_c = remote(recv_c.at[pl.ds(0, CHIPS - 1)], recv_c.at[pl.ds(0, CHIPS - 1)], col_send, col_recv, sibling)
    gather_c.wait_recv()
    line = combined(recv_c[...])

    def segment(first):
        return sum(
            jnp.where(p == j, line[:, first + j * COLS : first + (j + 1) * COLS], 0.0) for j in range(8)
        )

    ours, theirs = segment(0), segment(8 * COLS)
    final[0] = jnp.concatenate([theirs, jnp.zeros((1, 128 - COLS), F32)], axis=1)
    swap = remote(final.at[0], final.at[1], fin_send, fin_recv, sibling)
    swap.start()
    swap.wait_recv()
    theirs = final[1][:, :COLS]
    top = jnp.maximum(ours, theirs)
    score = top + jnp.log2(jnp.exp2(ours - top) + jnp.exp2(theirs - top))
    g_out[...] = pot_buf[...] - (EPS * LN2) * score + EPS * (
        math.log(float(CHIPS * NX * NC * ROWS)) - math.log(float(CHIPS * NX * NC * COLS))
    )

    for copy in one + [gather_x, gather_l, gather_c, swap] + outgoing:
        copy.wait_send()
    for k, count in enumerate((16, 16, 8, 8, 8, 8)):
        for copy in to_sibling(k, 0, count):
            copy.wait_send()


def per_device(gen_samples, data_samples, data_potential):
    hbm = pl.BlockSpec(memory_space=pltpu.HBM)
    vmem = pl.BlockSpec(memory_space=pltpu.VMEM)
    dma = pltpu.SemaphoreType.DMA
    span = 2 * 8 * COLS
    f, g = pl.pallas_call(
        kernel,
        out_shape=(jax.ShapeDtypeStruct((1, ROWS), F32), jax.ShapeDtypeStruct((1, COLS), F32)),
        in_specs=[hbm, hbm, hbm],
        out_specs=(vmem, vmem),
        scratch_shapes=[
            pltpu.VMEM((NX, ROWS, WIDTH), BF16),
            pltpu.VMEM((COLS, WIDTH), BF16),
            pltpu.VMEM((1, COLS), F32),
            pltpu.VMEM((1, ROWS), F32),
            pltpu.VMEM((2 * CHIPS, 2 * COLS, HALF), BF16),
            pltpu.VMEM((2 * CHIPS, 1, 128), F32),
            pltpu.VMEM((2 * CHIPS, COLS, NX * ROWS), F32),
            pltpu.VMEM((8, NX * ROWS), F32),
            pltpu.VMEM((8, NX * ROWS), F32),
            pltpu.VMEM((NX, 1, NX * ROWS), F32),
            pltpu.VMEM((NX, 1, ROWS), F32),
            pltpu.VMEM((span, 128), F32),
            pltpu.VMEM((span, 128), F32),
            pltpu.VMEM((span, 128), F32),
            pltpu.VMEM((span, 128), F32),
            pltpu.VMEM((8, 1, span), F32),
            pltpu.VMEM((CHIPS, 1, span), F32),
            pltpu.VMEM((2, 1, 128), F32),
            dma((3,)), dma, dma,
            dma((2,)), dma((2,)), dma((2, 6)), dma((2, 6)), dma((2, 6)), dma((2, 6)),
            dma, dma, dma, dma, dma, dma,
        ],
        compiler_params=pltpu.CompilerParams(
            collective_id=0, has_side_effects=True, vmem_limit_bytes=40 * 2**20
        ),
    )(*[
        pltpu.with_memory_space_constraint(array, pltpu.HBM)
        for array in (gen_samples, data_samples, data_potential.reshape(1, COLS))
    ])
    return f.reshape(ROWS), g.reshape(COLS)


def solution(mesh):
    in_specs = (P(("gen", "dat"), None), P(("dat", "gen"), None), P(("dat", "gen")))
    out_specs = (P(("gen", "dat")), P(("dat", "gen")))
    return jax.shard_map(
        per_device, mesh=mesh, in_specs=in_specs, out_specs=out_specs, check_vma=False
    )
```

```python
import math

import jax
import jax.numpy as jnp
from jax import lax
from jax.experimental import pallas as pl
from jax.experimental.pallas import tpu as pltpu
from jax.sharding import PartitionSpec as P

EPS = 0.05
LOG2E = math.log2(math.e)
LN2 = math.log(2.0)
SCALE = LOG2E / EPS
LOW = -1e30
MESH = pl.DeviceIdType.MESH
F32 = jnp.float32
BF16 = jnp.bfloat16

NX, NY, NZ, NC = 4, 8, 8, 2
CHIPS = NY * NZ
ROWS = 256
COLS = 24
WIDTH = 256
HALF = WIDTH // 2
KEEP = 1.0 / WIDTH


def hops(d):
    return min(d % 8, -d % 8)


FAR_FIRST = (4, 3, 5, 2, 6, 1, 7, 0)

NEAR0 = [(0, 0), (0, 2), (0, -2), (2, 1), (2, -1), (-2, 1), (-2, -1), (0, 4)]
FAR0 = [(4, 0), (2, 3), (2, -3), (-2, 3), (-2, -3), (4, 2), (4, -2), (4, 4)]
NEAR2 = ([(0, 1), (2, 2), (-2, 2), (2, 0)], [(0, -1), (2, -2), (-2, -2), (-2, 0)])
FAR2 = ([(0, 3), (4, 1), (4, 3), (2, 4)], [(0, -3), (4, -1), (4, -3), (-2, 4)])


def shifted(offsets, dp, dq):
    return [(a + dp, b + dq) for a, b in offsets]


ORDER = (
    NEAR0 + FAR0
    + shifted(NEAR0, 1, 0) + NEAR2[0] + NEAR2[1] + shifted(NEAR0, -1, 0)
    + shifted(FAR0, 1, 0) + FAR2[0] + FAR2[1] + shifted(FAR0, -1, 0)
)
SLOT = {(a % 8, b % 8): slot for slot, (a, b) in enumerate(ORDER)}


def slot_of(dp, dq):
    return SLOT[dp % 8, dq % 8]


def squares(values):
    wide = values.astype(F32)
    wide = wide * wide
    high = wide.astype(BF16)
    low = (wide - high.astype(F32)).astype(BF16)
    ones = jnp.ones((8, WIDTH), BF16)
    dims = (((1,), (1,)), ((), ()))
    return lax.dot_general(ones, high, dims, preferred_element_type=F32) + lax.dot_general(
        ones, low, dims, preferred_element_type=F32
    )


def kernel(
    gen_hbm, data_hbm, pot_hbm, f_out, g_out,
    x_buf, data_buf, pot_buf, sq_buf, blocks, terms, stash, row_m, row_s, row_l, send_l,
    peak_a, added_a, peak_b, added_b, send_c, recv_c, final,
    local_sem, x_send, x_recv, one_send, one_recv, two_send, two_recv, sib_send, sib_recv,
    row_send, row_recv, col_send, col_recv, fin_send, fin_recv,
):
    gen = lax.axis_index("gen")
    dat = lax.axis_index("dat")
    x, c = (dat // 2) % NX, dat % 2
    y, z = (dat // 8) * 4 + gen % 4, gen // 4

    def device(x_, y_, z_, c_):
        return (z_ * 4 + y_ % 4, (y_ // 4) * 8 + x_ * 2 + c_)

    p, q = y + c * (z - y), z + c * (y - z)

    def in_plane(p_, q_):
        p_, q_ = p_ % 8, q_ % 8
        return device(x, p_ + c * (q_ - p_), q_ + c * (p_ - q_), c)

    sibling = device(x, y, z, 1 - c)
    x_peers = [device((x + d) % NX, y, z, c) for d in (2, 1, 3)]
    near = [in_plane(p + 1, q), in_plane(p - 1, q), in_plane(p, q + 1), in_plane(p, q - 1)]
    group = [in_plane(p + dp, q + dq) for dp, dq in reversed((NEAR0 + FAR0)[1:])]

    loads = [
        pltpu.make_async_copy(data_hbm, data_buf, local_sem.at[0]),
        pltpu.make_async_copy(pot_hbm, pot_buf, local_sem.at[1]),
        pltpu.make_async_copy(gen_hbm, x_buf.at[x], local_sem.at[2]),
    ]
    for copy in loads:
        copy.start()

    peers = group + near + x_peers + [sibling]
    barrier = pltpu.get_barrier_semaphore()
    for peer in peers:
        pl.semaphore_signal(barrier, inc=1, device_id=peer, device_id_type=MESH)

    for copy in loads[:2]:
        copy.wait()
    data = data_buf[...].astype(F32)
    blocks[0] = jnp.concatenate([data[:, :HALF], data[:, HALF:]], axis=0).astype(BF16)
    term = (pot_buf[...] - squares(data_buf[...])[0:1, :] * KEEP) * SCALE
    terms[0] = jnp.concatenate([term, jnp.zeros((1, 128 - COLS), F32)], axis=1)

    pl.semaphore_wait(barrier, len(peers))

    def remote(src, dst, send, recv, peer):
        return pltpu.make_async_remote_copy(
            src_ref=src, dst_ref=dst, send_sem=send, recv_sem=recv, device_id=peer, device_id_type=MESH
        )

    def to_group(i, ref):
        for dp, dq in reversed((NEAR0 + FAR0)[1:]):
            far = int((dp, dq) in FAR0)
            remote(
                ref.at[0], ref.at[slot_of(dp, dq)], one_send.at[i, far], one_recv.at[i, far], in_plane(p - dp, q - dq)
            ).start()

    to_group(0, blocks)
    for peer in x_peers:
        remote(gen_hbm, x_buf.at[x], x_send, x_recv, peer).start()
    to_group(1, terms)

    row_m[...] = jnp.full(row_m.shape, LOW, F32)
    row_s[...] = jnp.zeros(row_s.shape, F32)
    loads[2].wait()
    sq_buf[...] = squares(x_buf[x])[0:1, :]

    refs = (blocks, terms)

    def from_group(far):
        return [
            remote(ref.at[pl.ds(0, 7 + far)], ref.at[pl.ds(0, 7 + far)], one_send.at[i, far], one_recv.at[i, far], sibling)
            for i, ref in enumerate(refs)
        ]

    def to_near(k, far, count, src, dst, peer):
        return [
            remote(
                ref.at[pl.ds(src, count)], ref.at[pl.ds(dst, count)],
                two_send.at[i, k, far], two_recv.at[i, k, far], peer,
            )
            for i, ref in enumerate(refs)
        ]

    def send_near(far):
        first = 16 + 24 * far
        for k, slots in ((0, first), (1, first + 16)):
            for copy in to_near(k, far, 8, 8 * far, slots, near[1 - k]):
                copy.start()
        for side, ways in enumerate((NEAR2, FAR2)[far]):
            for dp, dq in ways:
                held = slot_of(dp, dq + 2 * side - 1)
                for copy in to_near(2 + side, far, 1, held, slot_of(dp, dq), near[3 - side]):
                    copy.start()

    def from_near(far):
        counts = (8, 8, 4, 4)
        return sum((to_near(k, far, count, 0, 0, sibling) for k, count in enumerate(counts)), [])

    def to_sibling(k, start, count):
        return [
            remote(
                ref.at[pl.ds(start, count)], ref.at[pl.ds(CHIPS + start, count)],
                sib_send.at[i, k], sib_recv.at[i, k], sibling,
            )
            for i, ref in enumerate(refs)
        ]

    passed_on = [to_sibling(0, 0, 8), to_sibling(1, 8, 8), to_sibling(2, 16, 24), to_sibling(3, 40, 24)]
    for far in range(2):
        for copy in from_group(far):
            copy.wait_recv()
        send_near(far)
        for copy in passed_on[far]:
            copy.start()

    gather_x = remote(x_buf.at[pl.ds(0, 3)], x_buf.at[pl.ds(0, 3)], x_send, x_recv, sibling)
    gather_x.wait_recv()

    def row_unit(start, count):
        wide = blocks[pl.ds(start, count)].astype(F32)
        first = wide[:, :COLS, :].reshape(count * COLS, HALF)
        second = wide[:, COLS:, :].reshape(count * COLS, HALF)
        cols = jnp.concatenate([first.astype(BF16), second.astype(BF16)], axis=1)
        shape = (count, COLS, 128)
        on_diagonal = lax.broadcasted_iota(jnp.int32, shape, 2) == lax.broadcasted_iota(jnp.int32, shape, 1)
        spread = jnp.where(on_diagonal, jnp.broadcast_to(terms[pl.ds(start, count)], shape), 0.0)
        term_ = jnp.sum(spread, axis=2, keepdims=True).reshape(count * COLS, 1)
        for b in range(NX):
            lanes = slice(b * ROWS, (b + 1) * ROWS)
            cross = lax.dot_general(cols, x_buf[b], (((1,), (1,)), ((), ())), preferred_element_type=F32)
            scores = cross * (2.0 * KEEP * SCALE) + term_
            stash[pl.ds(start, count), :, lanes] = scores.reshape(count, COLS, ROWS)
            parts = scores.reshape(count * COLS // 8, 8, ROWS)
            old = row_m[:, lanes]
            top = jnp.maximum(old, jnp.max(parts, axis=0))
            row_m[:, lanes] = top
            row_s[:, lanes] = row_s[:, lanes] * jnp.exp2(old - top) + jnp.sum(
                jnp.exp2(parts - top[None]), axis=0
            )

    def first_units(step, _):
        @pl.when(step == 1)
        def _():
            for copy in from_near(0):
                copy.wait_recv()
            for copy in passed_on[2]:
                copy.start()
            for copy in passed_on[0] + passed_on[1]:
                copy.wait_recv()

        row_unit(CHIPS * step, 16)
        return 0

    lax.fori_loop(0, 2, first_units, 0)

    def next_units(step, _):
        @pl.when(step == 1)
        def _():
            for copy in passed_on[2]:
                copy.wait_recv()

        @pl.when(step == 2)
        def _():
            for copy in from_near(1):
                copy.wait_recv()
            for copy in passed_on[3]:
                copy.start()

        @pl.when(step == 3)
        def _():
            for copy in passed_on[3]:
                copy.wait_recv()

        row_unit(16 + 24 * (step // 2) + CHIPS * (step % 2), 24)
        return 0

    lax.fori_loop(0, 4, next_units, 0)

    m = row_m[...]
    top = jnp.max(m, axis=0, keepdims=True)
    total = jnp.sum(row_s[...] * jnp.exp2(m - top), axis=0, keepdims=True)
    row_l[x] = top + jnp.log2(total)
    for peer in x_peers:
        remote(row_l.at[x], row_l.at[x], row_send, row_recv, peer).start()
    gather_l = remote(row_l.at[pl.ds(0, 3)], row_l.at[pl.ds(0, 3)], row_send, row_recv, sibling)
    gather_l.wait_recv()
    parts = [row_l[b] for b in range(NX)]
    top = jnp.maximum(jnp.maximum(parts[0], parts[1]), jnp.maximum(parts[2], parts[3]))
    total = sum(jnp.exp2(part - top) for part in parts)
    whole = top + jnp.log2(total)
    for b in range(NX):
        send_l[b] = whole[:, b * ROWS : (b + 1) * ROWS]
    lifted = jnp.broadcast_to(whole, (8, NX * ROWS))

    def line_parts(dq, peak_ref, added_ref):
        for h in range(2):
            for j in range(8):
                at = slot_of(j, dq) if h == 0 else CHIPS + slot_of(dq, j)
                scores = stash[at].reshape(COLS // 8, 8, NX * ROWS) - lifted[None]
                pieces = [scores[:, :, i * 128 : (i + 1) * 128] for i in range(NX * ROWS // 128)]
                peak = pieces[0]
                for piece in pieces[1:]:
                    peak = jnp.maximum(peak, piece)
                added = jnp.exp2(pieces[0] - peak)
                for piece in pieces[1:]:
                    added = added + jnp.exp2(piece - peak)
                to = (h * 8 + j) * COLS
                peak_ref[to : to + COLS, :] = peak.reshape(COLS, 128)
                added_ref[to : to + COLS, :] = added.reshape(COLS, 128)

    def line_sums(peak_ref, added_ref):
        peak, added = jnp.transpose(peak_ref[...]), jnp.transpose(added_ref[...])
        crest = jnp.max(peak, axis=0, keepdims=True)
        return crest + jnp.log2(jnp.sum(added * jnp.exp2(peak - crest), axis=0, keepdims=True))

    def line_send(dq, peak_ref, added_ref):
        sums = line_sums(peak_ref, added_ref)
        send_c[dq] = sums
        for dp in FAR_FIRST:
            if (dp, dq) == (0, 0):
                recv_c[0] = sums
            else:
                seen = (-dp % 8) * 8 + -dq % 8
                remote(send_c.at[dq], recv_c.at[seen], col_send, col_recv, in_plane(p + dp, q + dq)).start()

    room = ((peak_a, added_a), (peak_b, added_b))
    line_parts(FAR_FIRST[0], *room[0])
    for i in range(8):
        if i < 7:
            line_parts(FAR_FIRST[i + 1], *room[(i + 1) % 2])
        line_send(FAR_FIRST[i], *room[i % 2])

    f_out[...] = sq_buf[...] * KEEP - (EPS * LN2) * send_l[x] + EPS * math.log(float(CHIPS * NX * NC * COLS))

    def combined(values):
        top = jnp.max(values, axis=0)
        return top + jnp.log2(jnp.sum(jnp.exp2(values - top[None]), axis=0))

    gather_c = remote(recv_c.at[pl.ds(0, CHIPS - 1)], recv_c.at[pl.ds(0, CHIPS - 1)], col_send, col_recv, sibling)
    gather_c.wait_recv()

    sums = [combined(recv_c[pl.ds(8 * dp, 8)]) for dp in range(8)]

    def segment(first):
        parts = [sums[dp][:, first + (-dp % 8) * COLS :][:, :COLS] for dp in range(8)]
        top = parts[0]
        for part in parts[1:]:
            top = jnp.maximum(top, part)
        return top + jnp.log2(sum(jnp.exp2(part - top) for part in parts))

    ours, theirs = segment(0), segment(8 * COLS)
    final[0] = jnp.concatenate([theirs, jnp.zeros((1, 128 - COLS), F32)], axis=1)
    swap = remote(final.at[0], final.at[1], fin_send, fin_recv, sibling)
    swap.start()
    swap.wait_recv()
    theirs = final[1][:, :COLS]
    top = jnp.maximum(ours, theirs)
    score = top + jnp.log2(jnp.exp2(ours - top) + jnp.exp2(theirs - top))
    g_out[...] = pot_buf[...] - (EPS * LN2) * score + EPS * (
        math.log(float(CHIPS * NX * NC * ROWS)) - math.log(float(CHIPS * NX * NC * COLS))
    )

    for copy in [gather_x, gather_l, gather_c, swap]:
        copy.wait_send()
    for far in range(2):
        for copy in from_group(far) + from_near(far):
            copy.wait_send()
    for copy in sum(passed_on, []):
        copy.wait_send()


def per_device(gen_samples, data_samples, data_potential):
    hbm = pl.BlockSpec(memory_space=pltpu.HBM)
    vmem = pl.BlockSpec(memory_space=pltpu.VMEM)
    dma = pltpu.SemaphoreType.DMA
    span = 2 * 8 * COLS
    f, g = pl.pallas_call(
        kernel,
        out_shape=(jax.ShapeDtypeStruct((1, ROWS), F32), jax.ShapeDtypeStruct((1, COLS), F32)),
        in_specs=[hbm, hbm, hbm],
        out_specs=(vmem, vmem),
        scratch_shapes=[
            pltpu.VMEM((NX, ROWS, WIDTH), BF16),
            pltpu.VMEM((COLS, WIDTH), BF16),
            pltpu.VMEM((1, COLS), F32),
            pltpu.VMEM((1, ROWS), F32),
            pltpu.VMEM((2 * CHIPS, 2 * COLS, HALF), BF16),
            pltpu.VMEM((2 * CHIPS, 1, 128), F32),
            pltpu.VMEM((2 * CHIPS, COLS, NX * ROWS), F32),
            pltpu.VMEM((8, NX * ROWS), F32),
            pltpu.VMEM((8, NX * ROWS), F32),
            pltpu.VMEM((NX, 1, NX * ROWS), F32),
            pltpu.VMEM((NX, 1, ROWS), F32),
            pltpu.VMEM((span, 128), F32),
            pltpu.VMEM((span, 128), F32),
            pltpu.VMEM((span, 128), F32),
            pltpu.VMEM((span, 128), F32),
            pltpu.VMEM((8, 1, span), F32),
            pltpu.VMEM((CHIPS, 1, span), F32),
            pltpu.VMEM((2, 1, 128), F32),
            dma((3,)), dma, dma,
            dma((2, 2)), dma((2, 2)), dma((2, 4, 2)), dma((2, 4, 2)), dma((2, 4)), dma((2, 4)),
            dma, dma, dma, dma, dma, dma,
        ],
        compiler_params=pltpu.CompilerParams(
            collective_id=0, has_side_effects=True, vmem_limit_bytes=40 * 2**20
        ),
    )(*[
        pltpu.with_memory_space_constraint(array, pltpu.HBM)
        for array in (gen_samples, data_samples, data_potential.reshape(1, COLS))
    ])
    return f.reshape(ROWS), g.reshape(COLS)


def solution(mesh):
    in_specs = (P(("gen", "dat"), None), P(("dat", "gen"), None), P(("dat", "gen")))
    out_specs = (P(("gen", "dat")), P(("dat", "gen")))
    return jax.shard_map(
        per_device, mesh=mesh, in_specs=in_specs, out_specs=out_specs, check_vma=False
    )
```

```python
import math

import jax
import jax.numpy as jnp
from jax import lax
from jax.experimental import pallas as pl
from jax.experimental.pallas import tpu as pltpu
from jax.sharding import PartitionSpec as P

EPS = 0.05
LOG2E = math.log2(math.e)
LN2 = math.log(2.0)
SCALE = LOG2E / EPS
LOW = -1e30
MESH = pl.DeviceIdType.MESH
F32 = jnp.float32
BF16 = jnp.bfloat16

NX, NY, NZ, NC = 4, 8, 8, 2
CHIPS = NY * NZ
ROWS = 256
COLS = 24
WIDTH = 256
HALF = WIDTH // 2
LINE = 8 * NC * COLS
KEEP = 1.0 / WIDTH


def hops(d):
    return min(d % 8, -d % 8)


FAR_FIRST = (4, 3, 5, 2, 6, 1, 7, 0)

NEAR0 = [(0, 0), (0, 2), (0, -2), (2, 1), (2, -1), (-2, 1), (-2, -1), (0, 4)]
FAR0 = [(4, 0), (2, 3), (2, -3), (-2, 3), (-2, -3), (4, 2), (4, -2), (4, 4)]
NEAR2 = ([(0, 1), (2, 2), (-2, 2), (2, 0)], [(0, -1), (2, -2), (-2, -2), (-2, 0)])
FAR2 = ([(0, 3), (4, 1), (4, 3), (2, 4)], [(0, -3), (4, -1), (4, -3), (-2, 4)])


def shifted(offsets, dp, dq):
    return [(a + dp, b + dq) for a, b in offsets]


ORDER = (
    NEAR0 + FAR0
    + shifted(NEAR0, 1, 0) + NEAR2[0] + NEAR2[1] + shifted(NEAR0, -1, 0)
    + shifted(FAR0, 1, 0) + FAR2[0] + FAR2[1] + shifted(FAR0, -1, 0)
)
SLOT = {(a % 8, b % 8): slot for slot, (a, b) in enumerate(ORDER)}


def slot_of(dp, dq):
    return SLOT[dp % 8, dq % 8]


def squares(values):
    wide = values.astype(F32)
    wide = wide * wide
    high = wide.astype(BF16)
    low = (wide - high.astype(F32)).astype(BF16)
    ones = jnp.ones((8, WIDTH), BF16)
    dims = (((1,), (1,)), ((), ()))
    return lax.dot_general(ones, high, dims, preferred_element_type=F32) + lax.dot_general(
        ones, low, dims, preferred_element_type=F32
    )


def kernel(
    gen_hbm, data_hbm, pot_hbm, f_out, g_out,
    x_buf, data_buf, pot_buf, sq_buf, blocks, terms, stash, row_m, row_s, row_l, send_l,
    line_a, line_b, send_c, recv_c, final,
    local_sem, x_send, x_recv, one_send, one_recv, two_send, two_recv, sib_send, sib_recv,
    row_send, row_recv, col_send, col_recv, fin_send, fin_recv,
):
    gen = lax.axis_index("gen")
    dat = lax.axis_index("dat")
    x, c = (dat // 2) % NX, dat % 2
    y, z = (dat // 8) * 4 + gen % 4, gen // 4

    def device(x_, y_, z_, c_):
        return (z_ * 4 + y_ % 4, (y_ // 4) * 8 + x_ * 2 + c_)

    p, q = y + c * (z - y), z + c * (y - z)

    def in_plane(p_, q_):
        p_, q_ = p_ % 8, q_ % 8
        return device(x, p_ + c * (q_ - p_), q_ + c * (p_ - q_), c)

    sibling = device(x, y, z, 1 - c)
    x_peers = [device((x + d) % NX, y, z, c) for d in (2, 1, 3)]
    near = [in_plane(p + 1, q), in_plane(p - 1, q), in_plane(p, q + 1), in_plane(p, q - 1)]
    group = [in_plane(p + dp, q + dq) for dp, dq in reversed((NEAR0 + FAR0)[1:])]

    loads = [
        pltpu.make_async_copy(data_hbm, data_buf, local_sem.at[0]),
        pltpu.make_async_copy(pot_hbm, pot_buf, local_sem.at[1]),
        pltpu.make_async_copy(gen_hbm, x_buf.at[x], local_sem.at[2]),
    ]
    for copy in loads:
        copy.start()

    peers = group + near + x_peers + [sibling]
    barrier = pltpu.get_barrier_semaphore()
    for peer in peers:
        pl.semaphore_signal(barrier, inc=1, device_id=peer, device_id_type=MESH)

    for copy in loads[:2]:
        copy.wait()
    data = data_buf[...].astype(F32)
    blocks[0] = jnp.concatenate([data[:, :HALF], data[:, HALF:]], axis=0).astype(BF16)
    term = (pot_buf[...] - squares(data_buf[...])[0:1, :] * KEEP) * SCALE
    terms[0] = jnp.concatenate([term, jnp.zeros((1, 128 - COLS), F32)], axis=1)

    pl.semaphore_wait(barrier, len(peers))

    def remote(src, dst, send, recv, peer):
        return pltpu.make_async_remote_copy(
            src_ref=src, dst_ref=dst, send_sem=send, recv_sem=recv, device_id=peer, device_id_type=MESH
        )

    def to_group(i, ref):
        for dp, dq in reversed((NEAR0 + FAR0)[1:]):
            far = int((dp, dq) in FAR0)
            remote(
                ref.at[0], ref.at[slot_of(dp, dq)], one_send.at[i, far], one_recv.at[i, far], in_plane(p - dp, q - dq)
            ).start()

    to_group(0, blocks)
    for peer in x_peers:
        remote(gen_hbm, x_buf.at[x], x_send, x_recv, peer).start()
    to_group(1, terms)

    row_m[...] = jnp.full(row_m.shape, LOW, F32)
    row_s[...] = jnp.zeros(row_s.shape, F32)
    loads[2].wait()
    sq_buf[...] = squares(x_buf[x])[0:1, :]

    refs = (blocks, terms)

    def from_group(far):
        return [
            remote(ref.at[pl.ds(0, 7 + far)], ref.at[pl.ds(0, 7 + far)], one_send.at[i, far], one_recv.at[i, far], sibling)
            for i, ref in enumerate(refs)
        ]

    def to_near(k, far, count, src, dst, peer):
        return [
            remote(
                ref.at[pl.ds(src, count)], ref.at[pl.ds(dst, count)],
                two_send.at[i, k, far], two_recv.at[i, k, far], peer,
            )
            for i, ref in enumerate(refs)
        ]

    def send_near(far):
        first = 16 + 24 * far
        for k, slots in ((0, first), (1, first + 16)):
            for copy in to_near(k, far, 8, 8 * far, slots, near[1 - k]):
                copy.start()
        for side, ways in enumerate((NEAR2, FAR2)[far]):
            for dp, dq in ways:
                held = slot_of(dp, dq + 2 * side - 1)
                for copy in to_near(2 + side, far, 1, held, slot_of(dp, dq), near[3 - side]):
                    copy.start()

    def from_near(far):
        counts = (8, 8, 4, 4)
        return sum((to_near(k, far, count, 0, 0, sibling) for k, count in enumerate(counts)), [])

    def to_sibling(k, start, count):
        return [
            remote(
                ref.at[pl.ds(start, count)], ref.at[pl.ds(CHIPS + start, count)],
                sib_send.at[i, k], sib_recv.at[i, k], sibling,
            )
            for i, ref in enumerate(refs)
        ]

    passed_on = [to_sibling(0, 0, 8), to_sibling(1, 8, 8), to_sibling(2, 16, 24), to_sibling(3, 40, 24)]
    for far in range(2):
        for copy in from_group(far):
            copy.wait_recv()
        send_near(far)
        for copy in passed_on[far]:
            copy.start()

    gather_x = remote(x_buf.at[pl.ds(0, 3)], x_buf.at[pl.ds(0, 3)], x_send, x_recv, sibling)
    gather_x.wait_recv()

    def row_unit(start, count):
        wide = blocks[pl.ds(start, count)].astype(F32)
        first = wide[:, :COLS, :].reshape(count * COLS, HALF)
        second = wide[:, COLS:, :].reshape(count * COLS, HALF)
        cols = jnp.concatenate([first.astype(BF16), second.astype(BF16)], axis=1)
        shape = (count, COLS, 128)
        on_diagonal = lax.broadcasted_iota(jnp.int32, shape, 2) == lax.broadcasted_iota(jnp.int32, shape, 1)
        spread = jnp.where(on_diagonal, jnp.broadcast_to(terms[pl.ds(start, count)], shape), 0.0)
        term_ = jnp.sum(spread, axis=2, keepdims=True).reshape(count * COLS, 1)
        for b in range(NX):
            lanes = slice(b * ROWS, (b + 1) * ROWS)
            cross = lax.dot_general(cols, x_buf[b], (((1,), (1,)), ((), ())), preferred_element_type=F32)
            scores = cross * (2.0 * KEEP * SCALE) + term_
            stash[pl.ds(start, count), :, lanes] = scores.reshape(count, COLS, ROWS)
            parts = scores.reshape(count * COLS // 8, 8, ROWS)
            old = row_m[:, lanes]
            top = jnp.maximum(old, jnp.max(parts, axis=0))
            row_m[:, lanes] = top
            row_s[:, lanes] = row_s[:, lanes] * jnp.exp2(old - top) + jnp.sum(
                jnp.exp2(parts - top[None]), axis=0
            )

    def first_units(step, _):
        @pl.when(step == 1)
        def _():
            for copy in from_near(0):
                copy.wait_recv()
            for copy in passed_on[2]:
                copy.start()
            for copy in passed_on[0] + passed_on[1]:
                copy.wait_recv()

        row_unit(CHIPS * step, 16)
        return 0

    lax.fori_loop(0, 2, first_units, 0)

    def next_units(step, _):
        @pl.when(step == 1)
        def _():
            for copy in passed_on[2]:
                copy.wait_recv()

        @pl.when(step == 2)
        def _():
            for copy in from_near(1):
                copy.wait_recv()
            for copy in passed_on[3]:
                copy.start()

        @pl.when(step == 3)
        def _():
            for copy in passed_on[3]:
                copy.wait_recv()

        row_unit(16 + 24 * (step // 2) + CHIPS * (step % 2), 24)
        return 0

    lax.fori_loop(0, 4, next_units, 0)

    m = row_m[...]
    top = jnp.max(m, axis=0, keepdims=True)
    total = jnp.sum(row_s[...] * jnp.exp2(m - top), axis=0, keepdims=True)
    row_l[x] = top + jnp.log2(total)
    for peer in x_peers:
        remote(row_l.at[x], row_l.at[x], row_send, row_recv, peer).start()
    gather_l = remote(row_l.at[pl.ds(0, 3)], row_l.at[pl.ds(0, 3)], row_send, row_recv, sibling)
    gather_l.wait_recv()
    parts = [row_l[b] for b in range(NX)]
    top = jnp.maximum(jnp.maximum(parts[0], parts[1]), jnp.maximum(parts[2], parts[3]))
    total = sum(jnp.exp2(part - top) for part in parts)
    whole = top + jnp.log2(total)
    for b in range(NX):
        send_l[b] = whole[:, b * ROWS : (b + 1) * ROWS]
    lifted = jnp.broadcast_to(whole, (8, NX * ROWS))

    def line_parts(dq, line_ref):
        for h in range(2):
            for j in range(8):
                at = slot_of(j, dq) if h == 0 else CHIPS + slot_of(dq, j)
                scores = stash[at].reshape(COLS // 8, 8, NX * ROWS) - lifted[None]
                pieces = [scores[:, :, i * 128 : (i + 1) * 128] for i in range(NX * ROWS // 128)]
                peak = pieces[0]
                for piece in pieces[1:]:
                    peak = jnp.maximum(peak, piece)
                added = jnp.exp2(pieces[0] - peak)
                for piece in pieces[1:]:
                    added = added + jnp.exp2(piece - peak)
                to = (2 * j + h) * COLS
                line_ref[to : to + COLS, :] = (peak + jnp.log2(added)).reshape(COLS, 128)

    def combined(values):
        top = jnp.max(values, axis=0)
        return top + jnp.log2(jnp.sum(jnp.exp2(values - top[None]), axis=0))

    def tiles_of(j):
        first = 2 * COLS * j // 128
        return first, (2 * COLS * (j + 1) - 1) // 128 - first + 1

    def line_send(dq, line_ref):
        values = jnp.transpose(line_ref[...])
        top = jnp.max(values, axis=0, keepdims=True)
        sums = top + jnp.log2(jnp.sum(jnp.exp2(values - top), axis=0, keepdims=True))
        for t in range(LINE // 128):
            send_c[dq, t] = sums[:, 128 * t : 128 * (t + 1)]
        for dp in FAR_FIRST:
            first, count = tiles_of(dp)
            if (dp, dq) == (0, 0):
                recv_c[0] = sums[:, :128]
            else:
                seen = 2 * ((-dp % 8) * 8 + -dq % 8)
                remote(
                    send_c.at[dq, pl.ds(first, count)], recv_c.at[pl.ds(seen, count)],
                    col_send, col_recv, in_plane(p + dp, q + dq),
                ).start()

    room = (line_a, line_b)
    line_parts(FAR_FIRST[0], room[0])
    for i in range(8):
        if i < 7:
            line_parts(FAR_FIRST[i + 1], room[(i + 1) % 2])
        line_send(FAR_FIRST[i], room[i % 2])

    f_out[...] = sq_buf[...] * KEEP - (EPS * LN2) * send_l[x] + EPS * math.log(float(CHIPS * NX * NC * COLS))

    tiles = 8 * sum(tiles_of(j)[1] for j in range(8)) - 1
    gather_c = remote(recv_c.at[pl.ds(0, tiles)], recv_c.at[pl.ds(0, tiles)], col_send, col_recv, sibling)
    gather_c.wait_recv()

    parts = []
    for dp in range(8):
        j = -dp % 8
        first, count = tiles_of(j)
        tiles = [
            combined(jnp.concatenate([recv_c[pl.ds(2 * (8 * dp + dq) + t, 1)] for dq in range(8)], axis=0))
            for t in range(count)
        ]
        row = jnp.concatenate(tiles, axis=1)
        start = 2 * COLS * j - 128 * first
        parts.append(row[:, start : start + 2 * COLS])
    top = parts[0]
    for part in parts[1:]:
        top = jnp.maximum(top, part)
    both = top + jnp.log2(sum(jnp.exp2(part - top) for part in parts))
    ours, theirs = both[:, :COLS], both[:, COLS:]
    final[0] = jnp.concatenate([theirs, jnp.zeros((1, 128 - COLS), F32)], axis=1)
    swap = remote(final.at[0], final.at[1], fin_send, fin_recv, sibling)
    swap.start()
    swap.wait_recv()
    theirs = final[1][:, :COLS]
    top = jnp.maximum(ours, theirs)
    score = top + jnp.log2(jnp.exp2(ours - top) + jnp.exp2(theirs - top))
    g_out[...] = pot_buf[...] - (EPS * LN2) * score + EPS * (
        math.log(float(CHIPS * NX * NC * ROWS)) - math.log(float(CHIPS * NX * NC * COLS))
    )

    for copy in [gather_x, gather_l, gather_c, swap]:
        copy.wait_send()
    for far in range(2):
        for copy in from_group(far) + from_near(far):
            copy.wait_send()
    for copy in sum(passed_on, []):
        copy.wait_send()


def per_device(gen_samples, data_samples, data_potential):
    hbm = pl.BlockSpec(memory_space=pltpu.HBM)
    vmem = pl.BlockSpec(memory_space=pltpu.VMEM)
    dma = pltpu.SemaphoreType.DMA
    f, g = pl.pallas_call(
        kernel,
        out_shape=(jax.ShapeDtypeStruct((1, ROWS), F32), jax.ShapeDtypeStruct((1, COLS), F32)),
        in_specs=[hbm, hbm, hbm],
        out_specs=(vmem, vmem),
        scratch_shapes=[
            pltpu.VMEM((NX, ROWS, WIDTH), BF16),
            pltpu.VMEM((COLS, WIDTH), BF16),
            pltpu.VMEM((1, COLS), F32),
            pltpu.VMEM((1, ROWS), F32),
            pltpu.VMEM((2 * CHIPS, 2 * COLS, HALF), BF16),
            pltpu.VMEM((2 * CHIPS, 1, 128), F32),
            pltpu.VMEM((2 * CHIPS, COLS, NX * ROWS), F32),
            pltpu.VMEM((8, NX * ROWS), F32),
            pltpu.VMEM((8, NX * ROWS), F32),
            pltpu.VMEM((NX, 1, NX * ROWS), F32),
            pltpu.VMEM((NX, 1, ROWS), F32),
            pltpu.VMEM((LINE, 128), F32),
            pltpu.VMEM((LINE, 128), F32),
            pltpu.VMEM((8, LINE // 128, 1, 128), F32),
            pltpu.VMEM((2 * CHIPS, 1, 128), F32),
            pltpu.VMEM((2, 1, 128), F32),
            dma((3,)), dma, dma,
            dma((2, 2)), dma((2, 2)), dma((2, 4, 2)), dma((2, 4, 2)), dma((2, 4)), dma((2, 4)),
            dma, dma, dma, dma, dma, dma,
        ],
        compiler_params=pltpu.CompilerParams(
            collective_id=0, has_side_effects=True, vmem_limit_bytes=40 * 2**20
        ),
    )(*[
        pltpu.with_memory_space_constraint(array, pltpu.HBM)
        for array in (gen_samples, data_samples, data_potential.reshape(1, COLS))
    ])
    return f.reshape(ROWS), g.reshape(COLS)


def solution(mesh):
    in_specs = (P(("gen", "dat"), None), P(("dat", "gen"), None), P(("dat", "gen")))
    out_specs = (P(("gen", "dat")), P(("dat", "gen")))
    return jax.shard_map(
        per_device, mesh=mesh, in_specs=in_specs, out_specs=out_specs, check_vma=False
    )
```

```python
import math

import jax
import jax.numpy as jnp
from jax import lax
from jax.experimental import pallas as pl
from jax.experimental.pallas import tpu as pltpu
from jax.sharding import PartitionSpec as P

EPS = 0.05
LOG2E = math.log2(math.e)
LN2 = math.log(2.0)
SCALE = LOG2E / EPS
LOW = -1e30
MESH = pl.DeviceIdType.MESH
F32 = jnp.float32
BF16 = jnp.bfloat16

NX, NY, NZ, NC = 4, 8, 8, 2
CHIPS = NY * NZ
ROWS = 256
COLS = 24
WIDTH = 256
HALF = WIDTH // 2
LINE = 8 * NC * COLS
KEEP = 1.0 / WIDTH


def hops(d):
    return min(d % 8, -d % 8)


FAR_FIRST = (4, 3, 5, 2, 6, 1, 7, 0)

NEAR0 = [(0, 0), (0, 2), (0, -2), (2, 1), (2, -1), (-2, 1), (-2, -1), (0, 4)]
FAR0 = [(4, 0), (2, 3), (2, -3), (-2, 3), (-2, -3)]
NEAR2 = ([(0, 1), (2, 2), (-2, 2), (2, 0)], [(0, -1), (2, -2), (-2, -2), (-2, 0)])
FAR2 = ([(0, 3), (4, 1), (2, 4)], [(0, -3), (4, -1), (-2, 4)])


def shifted(offsets, dp, dq):
    return [(a + dp, b + dq) for a, b in offsets]


def folded(offset):
    return tuple((d + 3) % 8 - 3 for d in offset)


FIRST = NEAR0 + FAR0
ORDER = (
    FIRST
    + shifted(NEAR0, 1, 0) + shifted(NEAR0, -1, 0) + NEAR2[0] + NEAR2[1]
    + shifted(FAR0, 1, 0) + shifted(FAR0, -1, 0) + FAR2[0] + FAR2[1]
)
REST = sorted({folded((a, b)) for a in range(8) for b in range(8)} - {folded(o) for o in ORDER})
SLOT = {(a % 8, b % 8): slot for slot, (a, b) in enumerate(ORDER + REST)}


def holders(offsets):
    chosen = {}
    for offset in offsets:
        ways = [folded((offset[0] - a, offset[1] - b)) for a, b in FIRST]
        used = list(chosen.values())
        chosen[offset] = min(ways, key=lambda way: (abs(way[0]) + abs(way[1]), used.count(way), way))
    return chosen


HOLDER = holders(REST)


def slot_of(dp, dq):
    return SLOT[dp % 8, dq % 8]


def squares(values):
    wide = values.astype(F32)
    wide = wide * wide
    high = wide.astype(BF16)
    low = (wide - high.astype(F32)).astype(BF16)
    ones = jnp.ones((8, WIDTH), BF16)
    dims = (((1,), (1,)), ((), ()))
    return lax.dot_general(ones, high, dims, preferred_element_type=F32) + lax.dot_general(
        ones, low, dims, preferred_element_type=F32
    )


def kernel(
    gen_hbm, data_hbm, pot_hbm, f_out, g_out,
    x_buf, data_buf, pot_buf, sq_buf, blocks, terms, stash, row_m, row_s, row_l, send_l,
    line_a, line_b, send_c, recv_c, final,
    local_sem, x_send, x_recv, one_send, one_recv, two_send, two_recv, sib_send, sib_recv,
    row_send, row_recv, col_send, col_recv, fin_send, fin_recv,
):
    gen = lax.axis_index("gen")
    dat = lax.axis_index("dat")
    x, c = (dat // 2) % NX, dat % 2
    y, z = (dat // 8) * 4 + gen % 4, gen // 4

    def device(x_, y_, z_, c_):
        return (z_ * 4 + y_ % 4, (y_ // 4) * 8 + x_ * 2 + c_)

    p, q = y + c * (z - y), z + c * (y - z)

    def in_plane(p_, q_):
        p_, q_ = p_ % 8, q_ % 8
        return device(x, p_ + c * (q_ - p_), q_ + c * (p_ - q_), c)

    sibling = device(x, y, z, 1 - c)
    x_peers = [device((x + d) % NX, y, z, c) for d in (2, 1, 3)]
    near = [in_plane(p + 1, q), in_plane(p - 1, q), in_plane(p, q + 1), in_plane(p, q - 1)]
    around = {(1, 0), (-1, 0), (0, 1), (0, -1)}
    others = sorted(({folded(o) for o in FIRST[1:]} | set(HOLDER.values())) - around, key=lambda o: -abs(o[0]) - abs(o[1]))
    group = [in_plane(p + dp, q + dq) for dp, dq in others]

    loads = [
        pltpu.make_async_copy(data_hbm, data_buf, local_sem.at[0]),
        pltpu.make_async_copy(pot_hbm, pot_buf, local_sem.at[1]),
        pltpu.make_async_copy(gen_hbm, x_buf.at[x], local_sem.at[2]),
    ]
    for copy in loads:
        copy.start()

    peers = group + near + x_peers + [sibling]
    barrier = pltpu.get_barrier_semaphore()
    for peer in peers:
        pl.semaphore_signal(barrier, inc=1, device_id=peer, device_id_type=MESH)

    for copy in loads[:2]:
        copy.wait()
    data = data_buf[...].astype(F32)
    blocks[0] = jnp.concatenate([data[:, :HALF], data[:, HALF:]], axis=0).astype(BF16)
    term = (pot_buf[...] - squares(data_buf[...])[0:1, :] * KEEP) * SCALE
    terms[0] = jnp.concatenate([term, jnp.zeros((1, 128 - COLS), F32)], axis=1)

    pl.semaphore_wait(barrier, len(peers))

    def remote(src, dst, send, recv, peer):
        return pltpu.make_async_remote_copy(
            src_ref=src, dst_ref=dst, send_sem=send, recv_sem=recv, device_id=peer, device_id_type=MESH
        )

    def to_group(i, ref):
        for dp, dq in reversed(FIRST[1:]):
            far = int((dp, dq) in FAR0)
            remote(
                ref.at[0], ref.at[slot_of(dp, dq)], one_send.at[i, far], one_recv.at[i, far], in_plane(p - dp, q - dq)
            ).start()

    to_group(0, blocks)
    for peer in x_peers:
        remote(gen_hbm, x_buf.at[x], x_send, x_recv, peer).start()
    to_group(1, terms)

    row_m[...] = jnp.full(row_m.shape, LOW, F32)
    row_s[...] = jnp.zeros(row_s.shape, F32)
    loads[2].wait()
    sq_buf[...] = squares(x_buf[x])[0:1, :]

    refs = (blocks, terms)

    def from_group(far):
        return [
            remote(
                ref.at[pl.ds(0, (7, 5)[far])], ref.at[pl.ds(0, (7, 5)[far])],
                one_send.at[i, far], one_recv.at[i, far], sibling,
            )
            for i, ref in enumerate(refs)
        ]

    def to_near(k, far, count, src, dst, peer):
        return [
            remote(
                ref.at[pl.ds(src, count)], ref.at[pl.ds(dst, count)],
                two_send.at[i, k, far], two_recv.at[i, k, far], peer,
            )
            for i, ref in enumerate(refs)
        ]

    def send_near(far):
        count = (8, 5)[far]
        for k in range(2):
            for copy in to_near(k, far, count, 8 * far, (13, 37)[far] + k * count, near[1 - k]):
                copy.start()
        for side, ways in enumerate((NEAR2, FAR2)[far]):
            for dp, dq in ways:
                held = slot_of(dp, dq + 2 * side - 1)
                for copy in to_near(2 + side, far, 1, held, slot_of(dp, dq), near[3 - side]):
                    copy.start()
        if far:
            for (dp, dq), (hp, hq) in HOLDER.items():
                for copy in to_near(4, far, 1, slot_of(dp - hp, dq - hq), slot_of(dp, dq), in_plane(p - hp, q - hq)):
                    copy.start()

    def from_near(k, far):
        return to_near(k, far, (8, 8, 4, 4, 0)[k] if not far else (5, 5, 3, 3, len(REST))[k], 0, 0, sibling)

    def to_sibling(k, start, count):
        return [
            remote(
                ref.at[pl.ds(start, count)], ref.at[pl.ds(CHIPS + start, count)],
                sib_send.at[i, k], sib_recv.at[i, k], sibling,
            )
            for i, ref in enumerate(refs)
        ]

    pieces = ((37, 5), (42, 5), (47, 3), (50, 3), (53, len(REST)))
    passed_on = [to_sibling(0, 0, 8), to_sibling(1, 8, 5), to_sibling(2, 13, 24)]
    last_on = [to_sibling(3 + k, *piece) for k, piece in enumerate(pieces)]
    for far in range(2):
        for copy in from_group(far):
            copy.wait_recv()
        send_near(far)
        for copy in passed_on[far]:
            copy.start()

    gather_x = remote(x_buf.at[pl.ds(0, 3)], x_buf.at[pl.ds(0, 3)], x_send, x_recv, sibling)
    gather_x.wait_recv()

    def row_unit(start, count):
        wide = blocks[pl.ds(start, count)].astype(F32)
        first = wide[:, :COLS, :].reshape(count * COLS, HALF)
        second = wide[:, COLS:, :].reshape(count * COLS, HALF)
        cols = jnp.concatenate([first.astype(BF16), second.astype(BF16)], axis=1)
        shape = (count, COLS, 128)
        on_diagonal = lax.broadcasted_iota(jnp.int32, shape, 2) == lax.broadcasted_iota(jnp.int32, shape, 1)
        spread = jnp.where(on_diagonal, jnp.broadcast_to(terms[pl.ds(start, count)], shape), 0.0)
        term_ = jnp.sum(spread, axis=2, keepdims=True).reshape(count * COLS, 1)
        for b in range(NX):
            lanes = slice(b * ROWS, (b + 1) * ROWS)
            cross = lax.dot_general(cols, x_buf[b], (((1,), (1,)), ((), ())), preferred_element_type=F32)
            scores = cross * (2.0 * KEEP * SCALE) + term_
            stash[pl.ds(start, count), :, lanes] = scores.reshape(count, COLS, ROWS)
            parts = scores.reshape(count * COLS // 8, 8, ROWS)
            old = row_m[:, lanes]
            top = jnp.maximum(old, jnp.max(parts, axis=0))
            row_m[:, lanes] = top
            row_s[:, lanes] = row_s[:, lanes] * jnp.exp2(old - top) + jnp.sum(
                jnp.exp2(parts - top[None]), axis=0
            )

    def first_units(step, _):
        @pl.when(step == 1)
        def _():
            for k in range(4):
                for copy in from_near(k, 0):
                    copy.wait_recv()
            for copy in passed_on[2]:
                copy.start()
            for copy in passed_on[0] + passed_on[1]:
                copy.wait_recv()

        row_unit(CHIPS * step, 13)
        return 0

    lax.fori_loop(0, 2, first_units, 0)

    def next_units(step, _):
        @pl.when(step == 1)
        def _():
            for copy in passed_on[2]:
                copy.wait_recv()

        row_unit(13 + CHIPS * step, 24)
        return 0

    lax.fori_loop(0, 2, next_units, 0)

    def last_units(step, _):
        @pl.when(step == 0)
        def _():
            for k in range(5):
                for copy in from_near(k, 1):
                    copy.wait_recv()
                for copy in last_on[k]:
                    copy.start()

        @pl.when(step == 1)
        def _():
            for copy in sum(last_on, []):
                copy.wait_recv()

        row_unit(37 + CHIPS * step, 27)
        return 0

    lax.fori_loop(0, 2, last_units, 0)

    m = row_m[...]
    top = jnp.max(m, axis=0, keepdims=True)
    total = jnp.sum(row_s[...] * jnp.exp2(m - top), axis=0, keepdims=True)
    row_l[x] = top + jnp.log2(total)
    for peer in x_peers:
        remote(row_l.at[x], row_l.at[x], row_send, row_recv, peer).start()
    gather_l = remote(row_l.at[pl.ds(0, 3)], row_l.at[pl.ds(0, 3)], row_send, row_recv, sibling)
    gather_l.wait_recv()
    parts = [row_l[b] for b in range(NX)]
    top = jnp.maximum(jnp.maximum(parts[0], parts[1]), jnp.maximum(parts[2], parts[3]))
    total = sum(jnp.exp2(part - top) for part in parts)
    whole = top + jnp.log2(total)
    for b in range(NX):
        send_l[b] = whole[:, b * ROWS : (b + 1) * ROWS]
    lifted = jnp.broadcast_to(whole, (8, NX * ROWS))

    def line_parts(dq, line_ref):
        for h in range(2):
            for j in range(8):
                at = slot_of(j, dq) if h == 0 else CHIPS + slot_of(dq, j)
                scores = stash[at].reshape(COLS // 8, 8, NX * ROWS) - lifted[None]
                pieces = [scores[:, :, i * 128 : (i + 1) * 128] for i in range(NX * ROWS // 128)]
                peak = pieces[0]
                for piece in pieces[1:]:
                    peak = jnp.maximum(peak, piece)
                added = jnp.exp2(pieces[0] - peak)
                for piece in pieces[1:]:
                    added = added + jnp.exp2(piece - peak)
                to = (2 * j + h) * COLS
                line_ref[to : to + COLS, :] = (peak + jnp.log2(added)).reshape(COLS, 128)

    def combined(values):
        top = jnp.max(values, axis=0)
        return top + jnp.log2(jnp.sum(jnp.exp2(values - top[None]), axis=0))

    def tiles_of(j):
        first = 2 * COLS * j // 128
        return first, (2 * COLS * (j + 1) - 1) // 128 - first + 1

    def line_send(dq, line_ref):
        values = jnp.transpose(line_ref[...])
        top = jnp.max(values, axis=0, keepdims=True)
        sums = top + jnp.log2(jnp.sum(jnp.exp2(values - top), axis=0, keepdims=True))
        for t in range(LINE // 128):
            send_c[dq, t] = sums[:, 128 * t : 128 * (t + 1)]
        for dp in FAR_FIRST:
            first, count = tiles_of(dp)
            if (dp, dq) == (0, 0):
                recv_c[0] = sums[:, :128]
            else:
                seen = 2 * ((-dp % 8) * 8 + -dq % 8)
                remote(
                    send_c.at[dq, pl.ds(first, count)], recv_c.at[pl.ds(seen, count)],
                    col_send, col_recv, in_plane(p + dp, q + dq),
                ).start()

    room = (line_a, line_b)
    line_parts(FAR_FIRST[0], room[0])
    for i in range(8):
        if i < 7:
            line_parts(FAR_FIRST[i + 1], room[(i + 1) % 2])
        line_send(FAR_FIRST[i], room[i % 2])

    f_out[...] = sq_buf[...] * KEEP - (EPS * LN2) * send_l[x] + EPS * math.log(float(CHIPS * NX * NC * COLS))

    tiles = 8 * sum(tiles_of(j)[1] for j in range(8)) - 1
    gather_c = remote(recv_c.at[pl.ds(0, tiles)], recv_c.at[pl.ds(0, tiles)], col_send, col_recv, sibling)
    gather_c.wait_recv()

    parts = []
    for dp in range(8):
        j = -dp % 8
        first, count = tiles_of(j)
        tiles = [
            combined(jnp.concatenate([recv_c[pl.ds(2 * (8 * dp + dq) + t, 1)] for dq in range(8)], axis=0))
            for t in range(count)
        ]
        row = jnp.concatenate(tiles, axis=1)
        start = 2 * COLS * j - 128 * first
        parts.append(row[:, start : start + 2 * COLS])
    top = parts[0]
    for part in parts[1:]:
        top = jnp.maximum(top, part)
    both = top + jnp.log2(sum(jnp.exp2(part - top) for part in parts))
    ours, theirs = both[:, :COLS], both[:, COLS:]
    final[0] = jnp.concatenate([theirs, jnp.zeros((1, 128 - COLS), F32)], axis=1)
    swap = remote(final.at[0], final.at[1], fin_send, fin_recv, sibling)
    swap.start()
    swap.wait_recv()
    theirs = final[1][:, :COLS]
    top = jnp.maximum(ours, theirs)
    score = top + jnp.log2(jnp.exp2(ours - top) + jnp.exp2(theirs - top))
    g_out[...] = pot_buf[...] - (EPS * LN2) * score + EPS * (
        math.log(float(CHIPS * NX * NC * ROWS)) - math.log(float(CHIPS * NX * NC * COLS))
    )

    for copy in [gather_x, gather_l, gather_c, swap]:
        copy.wait_send()
    for far in range(2):
        for copy in from_group(far) + sum((from_near(k, far) for k in range(4 + far)), []):
            copy.wait_send()
    for copy in sum(passed_on + last_on, []):
        copy.wait_send()


def per_device(gen_samples, data_samples, data_potential):
    hbm = pl.BlockSpec(memory_space=pltpu.HBM)
    vmem = pl.BlockSpec(memory_space=pltpu.VMEM)
    dma = pltpu.SemaphoreType.DMA
    f, g = pl.pallas_call(
        kernel,
        out_shape=(jax.ShapeDtypeStruct((1, ROWS), F32), jax.ShapeDtypeStruct((1, COLS), F32)),
        in_specs=[hbm, hbm, hbm],
        out_specs=(vmem, vmem),
        scratch_shapes=[
            pltpu.VMEM((NX, ROWS, WIDTH), BF16),
            pltpu.VMEM((COLS, WIDTH), BF16),
            pltpu.VMEM((1, COLS), F32),
            pltpu.VMEM((1, ROWS), F32),
            pltpu.VMEM((2 * CHIPS, 2 * COLS, HALF), BF16),
            pltpu.VMEM((2 * CHIPS, 1, 128), F32),
            pltpu.VMEM((2 * CHIPS, COLS, NX * ROWS), F32),
            pltpu.VMEM((8, NX * ROWS), F32),
            pltpu.VMEM((8, NX * ROWS), F32),
            pltpu.VMEM((NX, 1, NX * ROWS), F32),
            pltpu.VMEM((NX, 1, ROWS), F32),
            pltpu.VMEM((LINE, 128), F32),
            pltpu.VMEM((LINE, 128), F32),
            pltpu.VMEM((8, LINE // 128, 1, 128), F32),
            pltpu.VMEM((2 * CHIPS, 1, 128), F32),
            pltpu.VMEM((2, 1, 128), F32),
            dma((3,)), dma, dma,
            dma((2, 2)), dma((2, 2)), dma((2, 5, 2)), dma((2, 5, 2)), dma((2, 8)), dma((2, 8)),
            dma, dma, dma, dma, dma, dma,
        ],
        compiler_params=pltpu.CompilerParams(
            collective_id=0, has_side_effects=True, vmem_limit_bytes=40 * 2**20
        ),
    )(*[
        pltpu.with_memory_space_constraint(array, pltpu.HBM)
        for array in (gen_samples, data_samples, data_potential.reshape(1, COLS))
    ])
    return f.reshape(ROWS), g.reshape(COLS)


def solution(mesh):
    in_specs = (P(("gen", "dat"), None), P(("dat", "gen"), None), P(("dat", "gen")))
    out_specs = (P(("gen", "dat")), P(("dat", "gen")))
    return jax.shard_map(
        per_device, mesh=mesh, in_specs=in_specs, out_specs=out_specs, check_vma=False
    )
```

```python
import math

import jax
import jax.numpy as jnp
from jax import lax
from jax.experimental import pallas as pl
from jax.experimental.pallas import tpu as pltpu
from jax.sharding import PartitionSpec as P

EPS = 0.05
LOG2E = math.log2(math.e)
LN2 = math.log(2.0)
SCALE = LOG2E / EPS
LOW = -1e30
MESH = pl.DeviceIdType.MESH
F32 = jnp.float32
BF16 = jnp.bfloat16

NX, NY, NZ, NC = 4, 8, 8, 2
CHIPS = NY * NZ
ROWS = 256
COLS = 24
WIDTH = 256
HALF = WIDTH // 2
LINE = 8 * NC * COLS
KEEP = 1.0 / WIDTH


def hops(d):
    return min(d % 8, -d % 8)


FAR_FIRST = (4, 3, 5, 2, 6, 1, 7, 0)

NEAR0 = [(0, 0), (0, 2), (0, -2), (2, 1), (2, -1), (-2, 1), (-2, -1), (0, 4)]
FAR0 = [(4, 0), (2, 3), (2, -3), (-2, 3), (-2, -3)]
NEAR2 = ([(0, 1), (2, 2), (-2, 2), (2, 0)], [(0, -1), (2, -2), (-2, -2), (-2, 0)])
FAR2 = ([(0, 3), (4, 1), (2, 4)], [(0, -3), (4, -1), (-2, 4)])


def shifted(offsets, dp, dq):
    return [(a + dp, b + dq) for a, b in offsets]


def folded(offset):
    return tuple((d + 3) % 8 - 3 for d in offset)


FIRST = NEAR0 + FAR0
ORDER = (
    FIRST
    + shifted(NEAR0, 1, 0) + shifted(NEAR0, -1, 0) + NEAR2[0] + NEAR2[1]
    + shifted(FAR0, 1, 0) + shifted(FAR0, -1, 0) + FAR2[0] + FAR2[1]
)
REST = sorted({folded((a, b)) for a in range(8) for b in range(8)} - {folded(o) for o in ORDER})
SLOT = {(a % 8, b % 8): slot for slot, (a, b) in enumerate(ORDER + REST)}


def holders(offsets):
    chosen = {}
    for offset in offsets:
        ways = [folded((offset[0] - a, offset[1] - b)) for a, b in FIRST]
        used = list(chosen.values())
        chosen[offset] = min(ways, key=lambda way: (abs(way[0]) + abs(way[1]), used.count(way), way))
    return chosen


HOLDER = holders(REST)


def slot_of(dp, dq):
    return SLOT[dp % 8, dq % 8]


def squares(values):
    wide = values.astype(F32)
    wide = wide * wide
    high = wide.astype(BF16)
    low = (wide - high.astype(F32)).astype(BF16)
    ones = jnp.ones((8, WIDTH), BF16)
    dims = (((1,), (1,)), ((), ()))
    return lax.dot_general(ones, high, dims, preferred_element_type=F32) + lax.dot_general(
        ones, low, dims, preferred_element_type=F32
    )


def kernel(
    gen_hbm, data_hbm, pot_hbm, f_out, g_out,
    x_buf, gen_buf, data_buf, pot_buf, sq_buf, blocks, terms, stash, row_m, row_s, row_l,
    line_a, line_b, send_c, recv_c, final,
    local_sem, x_send, x_recv, one_send, one_recv, two_send, two_recv, sib_send, sib_recv,
    row_send, row_recv, col_send, col_recv, fin_send, fin_recv,
):
    gen = lax.axis_index("gen")
    dat = lax.axis_index("dat")
    x, c = (dat // 2) % NX, dat % 2
    y, z = (dat // 8) * 4 + gen % 4, gen // 4

    def device(x_, y_, z_, c_):
        return (z_ * 4 + y_ % 4, (y_ // 4) * 8 + x_ * 2 + c_)

    p, q = y + c * (z - y), z + c * (y - z)

    def in_plane(p_, q_):
        p_, q_ = p_ % 8, q_ % 8
        return device(x, p_ + c * (q_ - p_), q_ + c * (p_ - q_), c)

    sibling = device(x, y, z, 1 - c)
    x_peers = {d: device((x + d) % NX, y, z, c) for d in (1, 3, 2)}
    near = [in_plane(p + 1, q), in_plane(p - 1, q), in_plane(p, q + 1), in_plane(p, q - 1)]
    around = {(1, 0), (-1, 0), (0, 1), (0, -1)}
    others = sorted(({folded(o) for o in FIRST[1:]} | set(HOLDER.values())) - around, key=lambda o: -abs(o[0]) - abs(o[1]))
    group = [in_plane(p + dp, q + dq) for dp, dq in others]

    loads = [
        pltpu.make_async_copy(data_hbm, data_buf, local_sem.at[0]),
        pltpu.make_async_copy(pot_hbm, pot_buf, local_sem.at[1]),
        pltpu.make_async_copy(gen_hbm, gen_buf, local_sem.at[2]),
    ]
    for copy in loads:
        copy.start()

    peers = group + near + list(x_peers.values()) + [sibling]
    barrier = pltpu.get_barrier_semaphore()
    for peer in peers:
        pl.semaphore_signal(barrier, inc=1, device_id=peer, device_id_type=MESH)

    for copy in loads[:2]:
        copy.wait()
    data = data_buf[...].astype(F32)
    blocks[0] = jnp.concatenate([data[:, :HALF], data[:, HALF:]], axis=0).astype(BF16)
    term = (pot_buf[...] - squares(data_buf[...])[0:1, :] * KEEP) * SCALE
    terms[0] = jnp.concatenate([term, jnp.zeros((1, 128 - COLS), F32)], axis=1)

    loads[2].wait()
    columns = jnp.transpose(gen_buf[...].astype(F32))
    sq_buf[...] = jnp.sum(columns * columns, axis=0, keepdims=True)
    x_buf[0] = columns.astype(BF16)

    pl.semaphore_wait(barrier, len(peers))

    def remote(src, dst, send, recv, peer):
        return pltpu.make_async_remote_copy(
            src_ref=src, dst_ref=dst, send_sem=send, recv_sem=recv, device_id=peer, device_id_type=MESH
        )

    def to_group(i, ref):
        for dp, dq in reversed(FIRST[1:]):
            far = int((dp, dq) in FAR0)
            remote(
                ref.at[0], ref.at[slot_of(dp, dq)], one_send.at[i, far], one_recv.at[i, far], in_plane(p - dp, q - dq)
            ).start()

    to_group(0, blocks)
    for d, peer in x_peers.items():
        remote(x_buf.at[0], x_buf.at[NX - d], x_send.at[int(d == 2)], x_recv.at[int(d == 2)], peer).start()
    to_group(1, terms)

    row_m[...] = jnp.full(row_m.shape, LOW, F32)
    row_s[...] = jnp.zeros(row_s.shape, F32)

    refs = (blocks, terms)

    def from_group(far):
        return [
            remote(
                ref.at[pl.ds(0, (7, 5)[far])], ref.at[pl.ds(0, (7, 5)[far])],
                one_send.at[i, far], one_recv.at[i, far], sibling,
            )
            for i, ref in enumerate(refs)
        ]

    def to_near(k, far, count, src, dst, peer):
        return [
            remote(
                ref.at[pl.ds(src, count)], ref.at[pl.ds(dst, count)],
                two_send.at[i, k, far], two_recv.at[i, k, far], peer,
            )
            for i, ref in enumerate(refs)
        ]

    def send_near(far):
        count = (8, 5)[far]
        for k in range(2):
            for copy in to_near(k, far, count, 8 * far, (13, 37)[far] + k * count, near[1 - k]):
                copy.start()
        for side, ways in enumerate((NEAR2, FAR2)[far]):
            for dp, dq in ways:
                held = slot_of(dp, dq + 2 * side - 1)
                for copy in to_near(2 + side, far, 1, held, slot_of(dp, dq), near[3 - side]):
                    copy.start()
        if far:
            for (dp, dq), (hp, hq) in HOLDER.items():
                for copy in to_near(4, far, 1, slot_of(dp - hp, dq - hq), slot_of(dp, dq), in_plane(p - hp, q - hq)):
                    copy.start()

    def from_near(k, far):
        return to_near(k, far, (8, 8, 4, 4, 0)[k] if not far else (5, 5, 3, 3, len(REST))[k], 0, 0, sibling)

    def to_sibling(k, start, count):
        return [
            remote(
                ref.at[pl.ds(start, count)], ref.at[pl.ds(CHIPS + start, count)],
                sib_send.at[i, k], sib_recv.at[i, k], sibling,
            )
            for i, ref in enumerate(refs)
        ]

    pieces = ((37, 5), (42, 5), (47, 3), (50, 3), (53, len(REST)))
    passed_on = [to_sibling(0, 0, 8), to_sibling(1, 8, 5), to_sibling(2, 13, 24)]
    last_on = [to_sibling(3 + k, *piece) for k, piece in enumerate(pieces)]
    for far in range(2):
        for copy in from_group(far):
            copy.wait_recv()
        send_near(far)
        for copy in passed_on[far]:
            copy.start()

    gather_x = [
        remote(x_buf.at[pl.ds(0, n)], x_buf.at[pl.ds(0, n)], x_send.at[i], x_recv.at[i], sibling)
        for i, n in enumerate((2, 1))
    ]
    gather_x[0].wait_recv()

    def row_unit(start, count, which=(0, 1, 2, 3)):
        wide = blocks[pl.ds(start, count)].astype(F32)
        first = wide[:, :COLS, :].reshape(count * COLS, HALF)
        second = wide[:, COLS:, :].reshape(count * COLS, HALF)
        cols = jnp.concatenate([first.astype(BF16), second.astype(BF16)], axis=1)
        shape = (count, COLS, 128)
        on_diagonal = lax.broadcasted_iota(jnp.int32, shape, 2) == lax.broadcasted_iota(jnp.int32, shape, 1)
        spread = jnp.where(on_diagonal, jnp.broadcast_to(terms[pl.ds(start, count)], shape), 0.0)
        term_ = jnp.sum(spread, axis=2, keepdims=True).reshape(count * COLS, 1)
        for b in which:
            lanes = slice(b * ROWS, (b + 1) * ROWS)
            cross = jnp.dot(cols, x_buf[b], preferred_element_type=F32)
            scores = cross * (2.0 * KEEP * SCALE) + term_
            stash[pl.ds(start, count), :, lanes] = scores.reshape(count, COLS, ROWS)
            parts = scores.reshape(count * COLS // 8, 8, ROWS)
            old = row_m[:, lanes]
            top = jnp.maximum(old, jnp.max(parts, axis=0))
            row_m[:, lanes] = top
            row_s[:, lanes] = row_s[:, lanes] * jnp.exp2(old - top) + jnp.sum(
                jnp.exp2(parts - top[None]), axis=0
            )

    def first_units(step, _):
        @pl.when(step == 1)
        def _():
            for k in range(4):
                for copy in from_near(k, 0):
                    copy.wait_recv()
            for copy in passed_on[2]:
                copy.start()
            for copy in passed_on[0] + passed_on[1]:
                copy.wait_recv()

        row_unit(CHIPS * step, 13, (0, 1, 3))
        return 0

    def first_opposite(step, _):
        row_unit(CHIPS * step, 13, (2,))
        return 0

    lax.fori_loop(0, 2, first_units, 0)
    gather_x[1].wait_recv()
    lax.fori_loop(0, 2, first_opposite, 0)

    def next_units(step, _):
        @pl.when(step == 1)
        def _():
            for copy in passed_on[2]:
                copy.wait_recv()

        row_unit(13 + CHIPS * step, 24)
        return 0

    lax.fori_loop(0, 2, next_units, 0)

    def last_units(step, _):
        @pl.when(step == 0)
        def _():
            for k in range(5):
                for copy in from_near(k, 1):
                    copy.wait_recv()
                for copy in last_on[k]:
                    copy.start()

        @pl.when(step == 1)
        def _():
            for copy in sum(last_on, []):
                copy.wait_recv()

        row_unit(37 + CHIPS * step, 27)
        return 0

    lax.fori_loop(0, 2, last_units, 0)

    def combined(values):
        top = jnp.max(values, axis=0)
        return top + jnp.log2(jnp.sum(jnp.exp2(values - top[None]), axis=0))

    m = row_m[...]
    top = jnp.max(m, axis=0, keepdims=True)
    total = jnp.sum(row_s[...] * jnp.exp2(m - top), axis=0, keepdims=True)
    local = top + jnp.log2(total)
    for b in range(NX):
        row_l[0, b] = local[:, b * ROWS : (b + 1) * ROWS]
    for d, peer in x_peers.items():
        for b in range(NX):
            remote(row_l.at[0, b], row_l.at[NX - d, (b - d) % NX], row_send, row_recv, peer).start()
    gather_l = remote(row_l.at[pl.ds(0, 3)], row_l.at[pl.ds(0, 3)], row_send, row_recv, sibling)
    gather_l.wait_recv()
    whole = combined(row_l[...])
    lifted = jnp.concatenate([jnp.broadcast_to(whole[b], (8, ROWS)) for b in range(NX)], axis=1)

    lane_tiles = NX * ROWS // 128

    def line_parts(dq, line_ref):
        for h in range(2):
            for j in range(8):
                at = slot_of(j, dq) if h == 0 else CHIPS + slot_of(dq, j)
                scores = stash[at].reshape(COLS // 8, 8, NX * ROWS) - lifted[None]
                pieces = [scores[:, :, i * 128 : (i + 1) * 128] for i in range(lane_tiles)]
                peak = pieces[0]
                for piece in pieces[1:]:
                    peak = jnp.maximum(peak, piece)
                added = jnp.exp2(pieces[0] - peak)
                for piece in pieces[1:]:
                    added = added + jnp.exp2(piece - peak)
                to = (2 * j + h) * COLS
                line_ref[to : to + COLS, :] = (peak + jnp.log2(added)).reshape(COLS, 128)

    def tiles_of(j):
        first = 2 * COLS * j // 128
        return first, (2 * COLS * (j + 1) - 1) // 128 - first + 1

    def line_send(dq, line_ref):
        values = jnp.transpose(line_ref[...])
        top = jnp.max(values, axis=0, keepdims=True)
        sums = top + jnp.log2(jnp.sum(jnp.exp2(values - top), axis=0, keepdims=True))
        for t in range(LINE // 128):
            send_c[dq, t] = sums[:, 128 * t : 128 * (t + 1)]
        for dp in FAR_FIRST:
            first, count = tiles_of(dp)
            if (dp, dq) == (0, 0):
                recv_c[0] = sums[:, :128]
            else:
                seen = 2 * ((-dp % 8) * 8 + -dq % 8)
                remote(
                    send_c.at[dq, pl.ds(first, count)], recv_c.at[pl.ds(seen, count)],
                    col_send, col_recv, in_plane(p + dp, q + dq),
                ).start()

    room = (line_a, line_b)
    line_parts(FAR_FIRST[0], room[0])
    for i in range(8):
        if i < 7:
            line_parts(FAR_FIRST[i + 1], room[(i + 1) % 2])
        line_send(FAR_FIRST[i], room[i % 2])

    f_out[...] = sq_buf[...] * KEEP - (EPS * LN2) * whole[0] + EPS * math.log(float(CHIPS * NX * NC * COLS))

    tiles = 8 * sum(tiles_of(j)[1] for j in range(8)) - 1
    gather_c = remote(recv_c.at[pl.ds(0, tiles)], recv_c.at[pl.ds(0, tiles)], col_send, col_recv, sibling)
    gather_c.wait_recv()

    parts = []
    for dp in range(8):
        j = -dp % 8
        first, count = tiles_of(j)
        tiles = [
            combined(jnp.concatenate([recv_c[pl.ds(2 * (8 * dp + dq) + t, 1)] for dq in range(8)], axis=0))
            for t in range(count)
        ]
        row = jnp.concatenate(tiles, axis=1)
        start = 2 * COLS * j - 128 * first
        parts.append(row[:, start : start + 2 * COLS])
    top = parts[0]
    for part in parts[1:]:
        top = jnp.maximum(top, part)
    both = top + jnp.log2(sum(jnp.exp2(part - top) for part in parts))
    ours, theirs = both[:, :COLS], both[:, COLS:]
    final[0] = jnp.concatenate([theirs, jnp.zeros((1, 128 - COLS), F32)], axis=1)
    swap = remote(final.at[0], final.at[1], fin_send, fin_recv, sibling)
    swap.start()
    swap.wait_recv()
    theirs = final[1][:, :COLS]
    top = jnp.maximum(ours, theirs)
    score = top + jnp.log2(jnp.exp2(ours - top) + jnp.exp2(theirs - top))
    g_out[...] = pot_buf[...] - (EPS * LN2) * score + EPS * (
        math.log(float(CHIPS * NX * NC * ROWS)) - math.log(float(CHIPS * NX * NC * COLS))
    )

    for copy in gather_x + [gather_l, gather_c, swap]:
        copy.wait_send()
    for far in range(2):
        for copy in from_group(far) + sum((from_near(k, far) for k in range(4 + far)), []):
            copy.wait_send()
    for copy in sum(passed_on + last_on, []):
        copy.wait_send()


def per_device(gen_samples, data_samples, data_potential):
    hbm = pl.BlockSpec(memory_space=pltpu.HBM)
    vmem = pl.BlockSpec(memory_space=pltpu.VMEM)
    dma = pltpu.SemaphoreType.DMA
    f, g = pl.pallas_call(
        kernel,
        out_shape=(jax.ShapeDtypeStruct((1, ROWS), F32), jax.ShapeDtypeStruct((1, COLS), F32)),
        in_specs=[hbm, hbm, hbm],
        out_specs=(vmem, vmem),
        scratch_shapes=[
            pltpu.VMEM((NX, WIDTH, ROWS), BF16),
            pltpu.VMEM((ROWS, WIDTH), BF16),
            pltpu.VMEM((COLS, WIDTH), BF16),
            pltpu.VMEM((1, COLS), F32),
            pltpu.VMEM((1, ROWS), F32),
            pltpu.VMEM((2 * CHIPS, 2 * COLS, HALF), BF16),
            pltpu.VMEM((2 * CHIPS, 1, 128), F32),
            pltpu.VMEM((2 * CHIPS, COLS, NX * ROWS), F32),
            pltpu.VMEM((8, NX * ROWS), F32),
            pltpu.VMEM((8, NX * ROWS), F32),
            pltpu.VMEM((NX, NX, 1, ROWS), F32),
            pltpu.VMEM((LINE, 128), F32),
            pltpu.VMEM((LINE, 128), F32),
            pltpu.VMEM((8, LINE // 128, 1, 128), F32),
            pltpu.VMEM((2 * CHIPS, 1, 128), F32),
            pltpu.VMEM((2, 1, 128), F32),
            dma((3,)), dma((2,)), dma((2,)),
            dma((2, 2)), dma((2, 2)), dma((2, 5, 2)), dma((2, 5, 2)), dma((2, 8)), dma((2, 8)),
            dma, dma, dma, dma, dma, dma,
        ],
        compiler_params=pltpu.CompilerParams(
            collective_id=0, has_side_effects=True, vmem_limit_bytes=40 * 2**20
        ),
    )(*[
        pltpu.with_memory_space_constraint(array, pltpu.HBM)
        for array in (gen_samples, data_samples, data_potential.reshape(1, COLS))
    ])
    return f.reshape(ROWS), g.reshape(COLS)


def solution(mesh):
    in_specs = (P(("gen", "dat"), None), P(("dat", "gen"), None), P(("dat", "gen")))
    out_specs = (P(("gen", "dat")), P(("dat", "gen")))
    return jax.shard_map(
        per_device, mesh=mesh, in_specs=in_specs, out_specs=out_specs, check_vma=False
    )
```

```python
import math

import jax
import jax.numpy as jnp
from jax import lax
from jax.experimental import pallas as pl
from jax.experimental.pallas import tpu as pltpu
from jax.sharding import PartitionSpec as P

EPS = 0.05
LOG2E = math.log2(math.e)
LN2 = math.log(2.0)
SCALE = LOG2E / EPS
LOW = -1e30
MESH = pl.DeviceIdType.MESH
F32 = jnp.float32
BF16 = jnp.bfloat16

NX, NY, NZ, NC = 4, 8, 8, 2
CHIPS = NY * NZ
ROWS = 256
COLS = 24
WIDTH = 256
LINE = 8 * NC * COLS
KEEP = 1.0 / WIDTH


def hops(d):
    return min(d % 8, -d % 8)


FAR_FIRST = (4, 3, 5, 2, 6, 1, 7, 0)

NEAR0 = [(0, 0), (0, 2), (0, -2), (2, 1), (2, -1), (-2, 1), (-2, -1), (0, 4)]
FAR0 = [(4, 0), (2, 3), (2, -3), (-2, 3), (-2, -3)]
NEAR2 = ([(0, 1), (2, 2), (-2, 2), (2, 0)], [(0, -1), (2, -2), (-2, -2), (-2, 0)])
FAR2 = ([(0, 3), (4, 1), (2, 4)], [(0, -3), (4, -1), (-2, 4)])


def shifted(offsets, dp, dq):
    return [(a + dp, b + dq) for a, b in offsets]


def folded(offset):
    return tuple((d + 3) % 8 - 3 for d in offset)


FIRST = NEAR0 + FAR0
ORDER = (
    FIRST
    + shifted(NEAR0, 1, 0) + shifted(NEAR0, -1, 0) + NEAR2[0] + NEAR2[1]
    + shifted(FAR0, 1, 0) + shifted(FAR0, -1, 0) + FAR2[0] + FAR2[1]
)
REST = sorted({folded((a, b)) for a in range(8) for b in range(8)} - {folded(o) for o in ORDER})
SLOT = {(a % 8, b % 8): slot for slot, (a, b) in enumerate(ORDER + REST)}


def holders(offsets):
    chosen = {}
    for offset in offsets:
        ways = [folded((offset[0] - a, offset[1] - b)) for a, b in FIRST]
        used = list(chosen.values())
        chosen[offset] = min(ways, key=lambda way: (abs(way[0]) + abs(way[1]), used.count(way), way))
    return chosen


HOLDER = holders(REST)


def slot_of(dp, dq):
    return SLOT[dp % 8, dq % 8]


def squares(values):
    wide = values.astype(F32)
    wide = wide * wide
    high = wide.astype(BF16)
    low = (wide - high.astype(F32)).astype(BF16)
    ones = jnp.ones((8, WIDTH), BF16)
    dims = (((1,), (1,)), ((), ()))
    return lax.dot_general(ones, high, dims, preferred_element_type=F32) + lax.dot_general(
        ones, low, dims, preferred_element_type=F32
    )


def kernel(
    gen_hbm, data_hbm, pot_hbm, f_out, g_out,
    x_buf, pot_buf, sq_buf, blocks, terms, stash, row_m, row_s, row_l,
    line_a, line_b, send_c, recv_c, final,
    local_sem, x_send, x_recv, one_send, one_recv, two_send, two_recv, sib_send, sib_recv,
    row_send, row_recv, col_send, col_recv, fin_send, fin_recv,
):
    gen = lax.axis_index("gen")
    dat = lax.axis_index("dat")
    x, c = (dat // 2) % NX, dat % 2
    y, z = (dat // 8) * 4 + gen % 4, gen // 4

    def device(x_, y_, z_, c_):
        return (z_ * 4 + y_ % 4, (y_ // 4) * 8 + x_ * 2 + c_)

    p, q = y + c * (z - y), z + c * (y - z)

    def in_plane(p_, q_):
        p_, q_ = p_ % 8, q_ % 8
        return device(x, p_ + c * (q_ - p_), q_ + c * (p_ - q_), c)

    sibling = device(x, y, z, 1 - c)
    x_peers = {d: device((x + d) % NX, y, z, c) for d in (1, 3, 2)}
    near = [in_plane(p + 1, q), in_plane(p - 1, q), in_plane(p, q + 1), in_plane(p, q - 1)]
    around = {(1, 0), (-1, 0), (0, 1), (0, -1)}
    others = sorted(({folded(o) for o in FIRST[1:]} | set(HOLDER.values())) - around, key=lambda o: -abs(o[0]) - abs(o[1]))
    group = [in_plane(p + dp, q + dq) for dp, dq in others]

    loads = [
        pltpu.make_async_copy(data_hbm, blocks.at[0], local_sem.at[0]),
        pltpu.make_async_copy(pot_hbm, pot_buf, local_sem.at[1]),
        pltpu.make_async_copy(gen_hbm, x_buf.at[0], local_sem.at[2]),
    ]
    for copy in loads:
        copy.start()

    peers = group + near + list(x_peers.values()) + [sibling]
    barrier = pltpu.get_barrier_semaphore()
    for peer in peers:
        pl.semaphore_signal(barrier, inc=1, device_id=peer, device_id_type=MESH)

    pl.semaphore_wait(barrier, len(peers))

    def remote(src, dst, send, recv, peer):
        return pltpu.make_async_remote_copy(
            src_ref=src, dst_ref=dst, send_sem=send, recv_sem=recv, device_id=peer, device_id_type=MESH
        )

    def to_group(i, ref, source):
        for dp, dq in reversed(FIRST[1:]):
            far = int((dp, dq) in FAR0)
            remote(
                source, ref.at[slot_of(dp, dq)], one_send.at[i, far], one_recv.at[i, far], in_plane(p - dp, q - dq)
            ).start()

    to_group(0, blocks, data_hbm)
    for d, peer in x_peers.items():
        remote(gen_hbm, x_buf.at[NX - d], x_send.at[int(d == 2)], x_recv.at[int(d == 2)], peer).start()

    for copy in loads[:2]:
        copy.wait()
    term = (pot_buf[...] - squares(blocks[0])[0:1, :] * KEEP) * SCALE
    terms[0] = jnp.concatenate([term, jnp.zeros((1, 128 - COLS), F32)], axis=1)
    to_group(1, terms, terms.at[0])

    row_m[...] = jnp.full(row_m.shape, LOW, F32)
    row_s[...] = jnp.zeros(row_s.shape, F32)
    loads[2].wait()
    sq_buf[...] = squares(x_buf[0])[0:1, :]

    refs = (blocks, terms)

    def from_group(far):
        return [
            remote(
                ref.at[pl.ds(0, (7, 5)[far])], ref.at[pl.ds(0, (7, 5)[far])],
                one_send.at[i, far], one_recv.at[i, far], sibling,
            )
            for i, ref in enumerate(refs)
        ]

    def to_near(k, far, count, src, dst, peer):
        return [
            remote(
                ref.at[pl.ds(src, count)], ref.at[pl.ds(dst, count)],
                two_send.at[i, k, far], two_recv.at[i, k, far], peer,
            )
            for i, ref in enumerate(refs)
        ]

    def send_near(i, far):
        count = (8, 5)[far]
        for k in range(2):
            to_near(k, far, count, 8 * far, (13, 37)[far] + k * count, near[1 - k])[i].start()
        for side, ways in enumerate((NEAR2, FAR2)[far]):
            for dp, dq in ways:
                held = slot_of(dp, dq + 2 * side - 1)
                to_near(2 + side, far, 1, held, slot_of(dp, dq), near[3 - side])[i].start()
        if far:
            for (dp, dq), (hp, hq) in HOLDER.items():
                to_near(4, far, 1, slot_of(dp - hp, dq - hq), slot_of(dp, dq), in_plane(p - hp, q - hq))[i].start()

    def from_near(k, far):
        return to_near(k, far, (8, 8, 4, 4, 0)[k] if not far else (5, 5, 3, 3, len(REST))[k], 0, 0, sibling)

    def to_sibling(k, start, count):
        return [
            remote(
                ref.at[pl.ds(start, count)], ref.at[pl.ds(CHIPS + start, count)],
                sib_send.at[i, k], sib_recv.at[i, k], sibling,
            )
            for i, ref in enumerate(refs)
        ]

    pieces = ((37, 5), (42, 5), (47, 3), (50, 3), (53, len(REST)))
    passed_on = [to_sibling(0, 0, 8), to_sibling(1, 8, 5), to_sibling(2, 13, 24)]
    last_on = [to_sibling(3 + k, *piece) for k, piece in enumerate(pieces)]
    for far in range(2):
        for i in range(2):
            from_group(far)[i].wait_recv()
            send_near(i, far)
            passed_on[far][i].start()

    gather_x = [
        remote(x_buf.at[pl.ds(0, n)], x_buf.at[pl.ds(0, n)], x_send.at[i], x_recv.at[i], sibling)
        for i, n in enumerate((2, 1))
    ]
    gather_x[0].wait_recv()

    def row_unit(start, count, which=(0, 1, 2, 3)):
        cols = blocks[pl.ds(start, count)].astype(F32).reshape(count * COLS, WIDTH).astype(BF16)
        shape = (count, COLS, 128)
        on_diagonal = lax.broadcasted_iota(jnp.int32, shape, 2) == lax.broadcasted_iota(jnp.int32, shape, 1)
        spread = jnp.where(on_diagonal, jnp.broadcast_to(terms[pl.ds(start, count)], shape), 0.0)
        term_ = jnp.sum(spread, axis=2, keepdims=True).reshape(count * COLS, 1)
        for b in which:
            lanes = slice(b * ROWS, (b + 1) * ROWS)
            cross = lax.dot_general(cols, x_buf[b], (((1,), (1,)), ((), ())), preferred_element_type=F32)
            scores = cross * (2.0 * KEEP * SCALE) + term_
            stash[pl.ds(start, count), :, lanes] = scores.reshape(count, COLS, ROWS)
            parts = scores.reshape(count * COLS // 8, 8, ROWS)
            old = row_m[:, lanes]
            top = jnp.maximum(old, jnp.max(parts, axis=0))
            row_m[:, lanes] = top
            row_s[:, lanes] = row_s[:, lanes] * jnp.exp2(old - top) + jnp.sum(
                jnp.exp2(parts - top[None]), axis=0
            )

    def first_units(step, _):
        @pl.when(step == 1)
        def _():
            for k in range(4):
                for copy in from_near(k, 0):
                    copy.wait_recv()
            for copy in passed_on[2]:
                copy.start()
            for copy in passed_on[0] + passed_on[1]:
                copy.wait_recv()

        row_unit(CHIPS * step, 13, (0, 1, 3))
        return 0

    def first_opposite(step, _):
        row_unit(CHIPS * step, 13, (2,))
        return 0

    lax.fori_loop(0, 2, first_units, 0)
    gather_x[1].wait_recv()
    lax.fori_loop(0, 2, first_opposite, 0)

    def next_units(step, _):
        @pl.when(step == 1)
        def _():
            for copy in passed_on[2]:
                copy.wait_recv()

        row_unit(13 + CHIPS * step, 24)
        return 0

    lax.fori_loop(0, 2, next_units, 0)

    def last_units(step, _):
        @pl.when(step == 0)
        def _():
            for k in range(5):
                for copy in from_near(k, 1):
                    copy.wait_recv()
                for copy in last_on[k]:
                    copy.start()

        @pl.when(step == 1)
        def _():
            for copy in sum(last_on, []):
                copy.wait_recv()

        row_unit(37 + CHIPS * step, 27)
        return 0

    lax.fori_loop(0, 2, last_units, 0)

    def combined(values):
        top = jnp.max(values, axis=0)
        return top + jnp.log2(jnp.sum(jnp.exp2(values - top[None]), axis=0))

    m = row_m[...]
    top = jnp.max(m, axis=0, keepdims=True)
    total = jnp.sum(row_s[...] * jnp.exp2(m - top), axis=0, keepdims=True)
    local = top + jnp.log2(total)
    for b in range(NX):
        row_l[0, b] = local[:, b * ROWS : (b + 1) * ROWS]
    for d, peer in x_peers.items():
        for b in range(NX):
            remote(row_l.at[0, b], row_l.at[NX - d, (b - d) % NX], row_send, row_recv, peer).start()
    gather_l = remote(row_l.at[pl.ds(0, 3)], row_l.at[pl.ds(0, 3)], row_send, row_recv, sibling)
    gather_l.wait_recv()
    whole = combined(row_l[...])
    lifted = jnp.concatenate([jnp.broadcast_to(whole[b], (8, ROWS)) for b in range(NX)], axis=1)

    lane_tiles = NX * ROWS // 128

    def line_parts(dq, line_ref):
        for h in range(2):
            for j in range(8):
                at = slot_of(j, dq) if h == 0 else CHIPS + slot_of(dq, j)
                scores = stash[at].reshape(COLS // 8, 8, NX * ROWS) - lifted[None]
                pieces = [scores[:, :, i * 128 : (i + 1) * 128] for i in range(lane_tiles)]
                peak = pieces[0]
                for piece in pieces[1:]:
                    peak = jnp.maximum(peak, piece)
                added = jnp.exp2(pieces[0] - peak)
                for piece in pieces[1:]:
                    added = added + jnp.exp2(piece - peak)
                to = (2 * j + h) * COLS
                line_ref[to : to + COLS, :] = (peak + jnp.log2(added)).reshape(COLS, 128)

    def tiles_of(j):
        first = 2 * COLS * j // 128
        return first, (2 * COLS * (j + 1) - 1) // 128 - first + 1

    def line_send(dq, line_ref):
        values = jnp.transpose(line_ref[...])
        top = jnp.max(values, axis=0, keepdims=True)
        sums = top + jnp.log2(jnp.sum(jnp.exp2(values - top), axis=0, keepdims=True))
        for t in range(LINE // 128):
            send_c[dq, t] = sums[:, 128 * t : 128 * (t + 1)]
        for dp in FAR_FIRST:
            first, count = tiles_of(dp)
            if (dp, dq) == (0, 0):
                recv_c[0] = sums[:, :128]
            else:
                seen = 2 * ((-dp % 8) * 8 + -dq % 8)
                remote(
                    send_c.at[dq, pl.ds(first, count)], recv_c.at[pl.ds(seen, count)],
                    col_send, col_recv, in_plane(p + dp, q + dq),
                ).start()

    room = (line_a, line_b)
    line_parts(FAR_FIRST[0], room[0])
    for i in range(8):
        if i < 7:
            line_parts(FAR_FIRST[i + 1], room[(i + 1) % 2])
        line_send(FAR_FIRST[i], room[i % 2])

    f_out[...] = sq_buf[...] * KEEP - (EPS * LN2) * whole[0] + EPS * math.log(float(CHIPS * NX * NC * COLS))

    tiles = 8 * sum(tiles_of(j)[1] for j in range(8)) - 1
    gather_c = remote(recv_c.at[pl.ds(0, tiles)], recv_c.at[pl.ds(0, tiles)], col_send, col_recv, sibling)
    gather_c.wait_recv()

    parts = []
    for dp in range(8):
        j = -dp % 8
        first, count = tiles_of(j)
        tiles = [
            combined(jnp.concatenate([recv_c[pl.ds(2 * (8 * dp + dq) + t, 1)] for dq in range(8)], axis=0))
            for t in range(count)
        ]
        row = jnp.concatenate(tiles, axis=1)
        start = 2 * COLS * j - 128 * first
        parts.append(row[:, start : start + 2 * COLS])
    top = parts[0]
    for part in parts[1:]:
        top = jnp.maximum(top, part)
    both = top + jnp.log2(sum(jnp.exp2(part - top) for part in parts))
    ours, theirs = both[:, :COLS], both[:, COLS:]
    final[0] = jnp.concatenate([theirs, jnp.zeros((1, 128 - COLS), F32)], axis=1)
    swap = remote(final.at[0], final.at[1], fin_send, fin_recv, sibling)
    swap.start()
    swap.wait_recv()
    theirs = final[1][:, :COLS]
    top = jnp.maximum(ours, theirs)
    score = top + jnp.log2(jnp.exp2(ours - top) + jnp.exp2(theirs - top))
    g_out[...] = pot_buf[...] - (EPS * LN2) * score + EPS * (
        math.log(float(CHIPS * NX * NC * ROWS)) - math.log(float(CHIPS * NX * NC * COLS))
    )

    for copy in gather_x + [gather_l, gather_c, swap]:
        copy.wait_send()
    for far in range(2):
        for copy in from_group(far) + sum((from_near(k, far) for k in range(4 + far)), []):
            copy.wait_send()
    for copy in sum(passed_on + last_on, []):
        copy.wait_send()


def per_device(gen_samples, data_samples, data_potential):
    hbm = pl.BlockSpec(memory_space=pltpu.HBM)
    vmem = pl.BlockSpec(memory_space=pltpu.VMEM)
    dma = pltpu.SemaphoreType.DMA
    f, g = pl.pallas_call(
        kernel,
        out_shape=(jax.ShapeDtypeStruct((1, ROWS), F32), jax.ShapeDtypeStruct((1, COLS), F32)),
        in_specs=[hbm, hbm, hbm],
        out_specs=(vmem, vmem),
        scratch_shapes=[
            pltpu.VMEM((NX, ROWS, WIDTH), BF16),
            pltpu.VMEM((1, COLS), F32),
            pltpu.VMEM((1, ROWS), F32),
            pltpu.VMEM((2 * CHIPS, COLS, WIDTH), BF16),
            pltpu.VMEM((2 * CHIPS, 1, 128), F32),
            pltpu.VMEM((2 * CHIPS, COLS, NX * ROWS), F32),
            pltpu.VMEM((8, NX * ROWS), F32),
            pltpu.VMEM((8, NX * ROWS), F32),
            pltpu.VMEM((NX, NX, 1, ROWS), F32),
            pltpu.VMEM((LINE, 128), F32),
            pltpu.VMEM((LINE, 128), F32),
            pltpu.VMEM((8, LINE // 128, 1, 128), F32),
            pltpu.VMEM((2 * CHIPS, 1, 128), F32),
            pltpu.VMEM((2, 1, 128), F32),
            dma((3,)), dma((2,)), dma((2,)),
            dma((2, 2)), dma((2, 2)), dma((2, 5, 2)), dma((2, 5, 2)), dma((2, 8)), dma((2, 8)),
            dma, dma, dma, dma, dma, dma,
        ],
        compiler_params=pltpu.CompilerParams(
            collective_id=0, has_side_effects=True, vmem_limit_bytes=40 * 2**20
        ),
    )(*[
        pltpu.with_memory_space_constraint(array, pltpu.HBM)
        for array in (gen_samples, data_samples, data_potential.reshape(1, COLS))
    ])
    return f.reshape(ROWS), g.reshape(COLS)


def solution(mesh):
    in_specs = (P(("gen", "dat"), None), P(("dat", "gen"), None), P(("dat", "gen")))
    out_specs = (P(("gen", "dat")), P(("dat", "gen")))
    return jax.shard_map(
        per_device, mesh=mesh, in_specs=in_specs, out_specs=out_specs, check_vma=False
    )
```

```python
import math

import jax
import jax.numpy as jnp
from jax import lax
from jax.experimental import pallas as pl
from jax.experimental.pallas import tpu as pltpu
from jax.sharding import PartitionSpec as P

EPS = 0.05
LOG2E = math.log2(math.e)
LN2 = math.log(2.0)
SCALE = LOG2E / EPS
LOW = -1e30
MESH = pl.DeviceIdType.MESH
F32 = jnp.float32
BF16 = jnp.bfloat16

NX, NY, NZ, NC = 4, 8, 8, 2
CHIPS = NY * NZ
ROWS = 256
COLS = 24
WIDTH = 256
BATCH = 8 * NC * COLS
KEEP = 1.0 / WIDTH


def hops(d):
    return min(d % 8, -d % 8)


NEAR0 = [(0, 0), (0, 2), (0, -2), (2, 1), (2, -1), (-2, 1), (-2, -1), (0, 4)]
FAR0 = [(4, 0), (2, 3), (2, -3), (-2, 3), (-2, -3)]
NEAR2 = ([(0, 1), (2, 2), (-2, 2), (2, 0)], [(0, -1), (2, -2), (-2, -2), (-2, 0)])
FAR2 = ([(0, 3), (4, 1), (2, 4)], [(0, -3), (4, -1), (-2, 4)])


def shifted(offsets, dp, dq):
    return [(a + dp, b + dq) for a, b in offsets]


def folded(offset):
    return tuple((d + 3) % 8 - 3 for d in offset)


FIRST = NEAR0 + FAR0
ORDER = (
    FIRST
    + shifted(NEAR0, 1, 0) + shifted(NEAR0, -1, 0) + NEAR2[0] + NEAR2[1]
    + shifted(FAR0, 1, 0) + shifted(FAR0, -1, 0) + FAR2[0] + FAR2[1]
)
REST = sorted({folded((a, b)) for a in range(8) for b in range(8)} - {folded(o) for o in ORDER})
SLOT = {(a % 8, b % 8): slot for slot, (a, b) in enumerate(ORDER + REST)}


def holders(offsets):
    chosen = {}
    for offset in offsets:
        ways = [folded((offset[0] - a, offset[1] - b)) for a, b in FIRST]
        used = list(chosen.values())
        chosen[offset] = min(ways, key=lambda way: (abs(way[0]) + abs(way[1]), used.count(way), way))
    return chosen


HOLDER = holders(REST)
ALL = sorted((folded((a, b)) for a in range(8) for b in range(8)), key=lambda o: (-abs(o[0]) - abs(o[1]), o))
BATCHES = [ALL[i : i + 8] for i in range(0, 56, 8)] + [ALL[:55:-1]]


def slot_of(dp, dq):
    return SLOT[dp % 8, dq % 8]


def squares(values):
    wide = values.astype(F32)
    wide = wide * wide
    high = wide.astype(BF16)
    low = (wide - high.astype(F32)).astype(BF16)
    ones = jnp.ones((8, WIDTH), BF16)
    dims = (((1,), (1,)), ((), ()))
    return lax.dot_general(ones, high, dims, preferred_element_type=F32) + lax.dot_general(
        ones, low, dims, preferred_element_type=F32
    )


def kernel(
    gen_hbm, data_hbm, pot_hbm, f_out, g_out,
    x_buf, pot_buf, sq_buf, blocks, terms, stash, row_m, row_s, row_l,
    batch_a, batch_b, send_c, recv_c, final,
    local_sem, x_send, x_recv, one_send, one_recv, two_send, two_recv, sib_send, sib_recv,
    row_send, row_recv, col_send, col_recv, fin_send, fin_recv,
):
    gen = lax.axis_index("gen")
    dat = lax.axis_index("dat")
    x, c = (dat // 2) % NX, dat % 2
    y, z = (dat // 8) * 4 + gen % 4, gen // 4

    def device(x_, y_, z_, c_):
        return (z_ * 4 + y_ % 4, (y_ // 4) * 8 + x_ * 2 + c_)

    p, q = y + c * (z - y), z + c * (y - z)

    def in_plane(p_, q_):
        p_, q_ = p_ % 8, q_ % 8
        return device(x, p_ + c * (q_ - p_), q_ + c * (p_ - q_), c)

    sibling = device(x, y, z, 1 - c)
    x_peers = {d: device((x + d) % NX, y, z, c) for d in (1, 3, 2)}
    near = [in_plane(p + 1, q), in_plane(p - 1, q), in_plane(p, q + 1), in_plane(p, q - 1)]
    around = {(1, 0), (-1, 0), (0, 1), (0, -1)}
    others = sorted(({folded(o) for o in FIRST[1:]} | set(HOLDER.values())) - around, key=lambda o: -abs(o[0]) - abs(o[1]))
    group = [in_plane(p + dp, q + dq) for dp, dq in others]

    loads = [
        pltpu.make_async_copy(data_hbm, blocks.at[0], local_sem.at[0]),
        pltpu.make_async_copy(pot_hbm, pot_buf, local_sem.at[1]),
        pltpu.make_async_copy(gen_hbm, x_buf.at[0], local_sem.at[2]),
    ]
    for copy in loads:
        copy.start()

    peers = group + near + list(x_peers.values()) + [sibling]
    barrier = pltpu.get_barrier_semaphore()
    for peer in peers:
        pl.semaphore_signal(barrier, inc=1, device_id=peer, device_id_type=MESH)

    pl.semaphore_wait(barrier, len(peers))

    def remote(src, dst, send, recv, peer):
        return pltpu.make_async_remote_copy(
            src_ref=src, dst_ref=dst, send_sem=send, recv_sem=recv, device_id=peer, device_id_type=MESH
        )

    def to_group(i, ref, source):
        for dp, dq in reversed(FIRST[1:]):
            far = int((dp, dq) in FAR0)
            remote(
                source, ref.at[slot_of(dp, dq)], one_send.at[i, far], one_recv.at[i, far], in_plane(p - dp, q - dq)
            ).start()

    to_group(0, blocks, data_hbm)
    for d, peer in x_peers.items():
        remote(gen_hbm, x_buf.at[NX - d], x_send.at[int(d == 2)], x_recv.at[int(d == 2)], peer).start()

    for copy in loads[:2]:
        copy.wait()
    term = (pot_buf[...] - squares(blocks[0])[0:1, :] * KEEP) * SCALE
    terms[0] = jnp.concatenate([term, jnp.zeros((1, 128 - COLS), F32)], axis=1)
    to_group(1, terms, terms.at[0])

    row_m[...] = jnp.full(row_m.shape, LOW, F32)
    row_s[...] = jnp.zeros(row_s.shape, F32)
    loads[2].wait()
    sq_buf[...] = squares(x_buf[0])[0:1, :]

    refs = (blocks, terms)

    def from_group(far):
        return [
            remote(
                ref.at[pl.ds(0, (7, 5)[far])], ref.at[pl.ds(0, (7, 5)[far])],
                one_send.at[i, far], one_recv.at[i, far], sibling,
            )
            for i, ref in enumerate(refs)
        ]

    def to_near(k, far, count, src, dst, peer):
        return [
            remote(
                ref.at[pl.ds(src, count)], ref.at[pl.ds(dst, count)],
                two_send.at[i, k, far], two_recv.at[i, k, far], peer,
            )
            for i, ref in enumerate(refs)
        ]

    def send_near(i, far):
        count = (8, 5)[far]
        for k in range(2):
            to_near(k, far, count, 8 * far, (13, 37)[far] + k * count, near[1 - k])[i].start()
        for side, ways in enumerate((NEAR2, FAR2)[far]):
            for dp, dq in ways:
                held = slot_of(dp, dq + 2 * side - 1)
                to_near(2 + side, far, 1, held, slot_of(dp, dq), near[3 - side])[i].start()
        if far:
            for (dp, dq), (hp, hq) in HOLDER.items():
                to_near(4, far, 1, slot_of(dp - hp, dq - hq), slot_of(dp, dq), in_plane(p - hp, q - hq))[i].start()

    def from_near(k, far):
        return to_near(k, far, (8, 8, 4, 4, 0)[k] if not far else (5, 5, 3, 3, len(REST))[k], 0, 0, sibling)

    def to_sibling(k, start, count):
        return [
            remote(
                ref.at[pl.ds(start, count)], ref.at[pl.ds(CHIPS + start, count)],
                sib_send.at[i, k], sib_recv.at[i, k], sibling,
            )
            for i, ref in enumerate(refs)
        ]

    pieces = ((37, 5), (42, 5), (47, 3), (50, 3), (53, len(REST)))
    passed_on = [to_sibling(0, 0, 8), to_sibling(1, 8, 5), to_sibling(2, 13, 24)]
    last_on = [to_sibling(3 + k, *piece) for k, piece in enumerate(pieces)]
    for far in range(2):
        for i in range(2):
            from_group(far)[i].wait_recv()
            send_near(i, far)
            passed_on[far][i].start()

    gather_x = [
        remote(x_buf.at[pl.ds(0, n)], x_buf.at[pl.ds(0, n)], x_send.at[i], x_recv.at[i], sibling)
        for i, n in enumerate((2, 1))
    ]
    gather_x[0].wait_recv()

    def row_unit(start, count, which=(0, 1, 2, 3)):
        cols = blocks[pl.ds(start, count)].astype(F32).reshape(count * COLS, WIDTH).astype(BF16)
        shape = (count, COLS, 128)
        on_diagonal = lax.broadcasted_iota(jnp.int32, shape, 2) == lax.broadcasted_iota(jnp.int32, shape, 1)
        spread = jnp.where(on_diagonal, jnp.broadcast_to(terms[pl.ds(start, count)], shape), 0.0)
        term_ = jnp.sum(spread, axis=2, keepdims=True).reshape(count * COLS, 1)
        for b in which:
            lanes = slice(b * ROWS, (b + 1) * ROWS)
            cross = lax.dot_general(cols, x_buf[b], (((1,), (1,)), ((), ())), preferred_element_type=F32)
            scores = cross * (2.0 * KEEP * SCALE) + term_
            stash[pl.ds(start, count), :, lanes] = scores.reshape(count, COLS, ROWS)
            parts = scores.reshape(count * COLS // 8, 8, ROWS)
            old = row_m[:, lanes]
            top = jnp.maximum(old, jnp.max(parts, axis=0))
            row_m[:, lanes] = top
            row_s[:, lanes] = row_s[:, lanes] * jnp.exp2(old - top) + jnp.sum(
                jnp.exp2(parts - top[None]), axis=0
            )

    def first_units(step, _):
        @pl.when(step == 1)
        def _():
            for k in range(4):
                for copy in from_near(k, 0):
                    copy.wait_recv()
            for copy in passed_on[2]:
                copy.start()
            for copy in passed_on[0] + passed_on[1]:
                copy.wait_recv()

        row_unit(CHIPS * step, 13, (0, 1, 3))
        return 0

    def first_opposite(step, _):
        row_unit(CHIPS * step, 13, (2,))
        return 0

    lax.fori_loop(0, 2, first_units, 0)
    gather_x[1].wait_recv()
    lax.fori_loop(0, 2, first_opposite, 0)

    def next_units(step, _):
        @pl.when(step == 1)
        def _():
            for copy in passed_on[2]:
                copy.wait_recv()

        row_unit(13 + CHIPS * step, 24)
        return 0

    lax.fori_loop(0, 2, next_units, 0)

    def last_units(step, _):
        @pl.when(step == 0)
        def _():
            for k in range(5):
                for copy in from_near(k, 1):
                    copy.wait_recv()
                for copy in last_on[k]:
                    copy.start()

        @pl.when(step == 1)
        def _():
            for copy in sum(last_on, []):
                copy.wait_recv()

        row_unit(37 + CHIPS * step, 27)
        return 0

    lax.fori_loop(0, 2, last_units, 0)

    def combined(values):
        top = jnp.max(values, axis=0)
        return top + jnp.log2(jnp.sum(jnp.exp2(values - top[None]), axis=0))

    m = row_m[...]
    top = jnp.max(m, axis=0, keepdims=True)
    total = jnp.sum(row_s[...] * jnp.exp2(m - top), axis=0, keepdims=True)
    local = top + jnp.log2(total)
    for b in range(NX):
        row_l[0, b] = local[:, b * ROWS : (b + 1) * ROWS]
    for d, peer in x_peers.items():
        for b in range(NX):
            remote(row_l.at[0, b], row_l.at[NX - d, (b - d) % NX], row_send, row_recv, peer).start()
    gather_l = remote(row_l.at[pl.ds(0, 3)], row_l.at[pl.ds(0, 3)], row_send, row_recv, sibling)
    gather_l.wait_recv()
    whole = combined(row_l[...])
    lifted = jnp.concatenate([jnp.broadcast_to(whole[b], (8, ROWS)) for b in range(NX)], axis=1)

    lane_tiles = NX * ROWS // 128

    def batch_parts(batch, batch_ref):
        for j, (dp, dq) in enumerate(batch):
            for h, at in enumerate((slot_of(dp, dq), CHIPS + slot_of(dq, dp))):
                scores = stash[at].reshape(COLS // 8, 8, NX * ROWS) - lifted[None]
                pieces = [scores[:, :, i * 128 : (i + 1) * 128] for i in range(lane_tiles)]
                peak = pieces[0]
                for piece in pieces[1:]:
                    peak = jnp.maximum(peak, piece)
                added = jnp.exp2(pieces[0] - peak)
                for piece in pieces[1:]:
                    added = added + jnp.exp2(piece - peak)
                to = (2 * j + h) * COLS
                batch_ref[to : to + COLS, :] = (peak + jnp.log2(added)).reshape(COLS, 128)

    def tiles_of(j):
        first = 2 * COLS * j // 128
        return first, (2 * COLS * (j + 1) - 1) // 128 - first + 1

    def batch_send(i, batch_ref):
        values = jnp.transpose(batch_ref[...])
        top = jnp.max(values, axis=0, keepdims=True)
        sums = top + jnp.log2(jnp.sum(jnp.exp2(values - top), axis=0, keepdims=True))
        for t in range(BATCH // 128):
            send_c[i, t] = sums[:, 128 * t : 128 * (t + 1)]
        for j, (dp, dq) in enumerate(BATCHES[i]):
            first, count = tiles_of(j)
            seen = 2 * (8 * j + i)
            if (dp, dq) == (0, 0):
                recv_c[seen] = sums[:, :128]
            else:
                remote(
                    send_c.at[i, pl.ds(first, count)], recv_c.at[pl.ds(seen, count)],
                    col_send, col_recv, in_plane(p + dp, q + dq),
                ).start()

    room = (batch_a, batch_b)
    batch_parts(BATCHES[0], room[0])
    for i in range(8):
        if i < 7:
            batch_parts(BATCHES[i + 1], room[(i + 1) % 2])
        batch_send(i, room[i % 2])

    f_out[...] = sq_buf[...] * KEEP - (EPS * LN2) * whole[0] + EPS * math.log(float(CHIPS * NX * NC * COLS))

    tiles = 8 * sum(tiles_of(j)[1] for j in range(8)) - 1
    gather_c = remote(recv_c.at[pl.ds(0, tiles)], recv_c.at[pl.ds(0, tiles)], col_send, col_recv, sibling)
    for copy in gather_x + [gather_l]:
        copy.wait_send()
    for far in range(2):
        for copy in from_group(far) + sum((from_near(k, far) for k in range(4 + far)), []):
            copy.wait_send()
    for copy in sum(passed_on + last_on, []):
        copy.wait_send()
    gather_c.wait_recv()

    parts = []
    for j in range(8):
        first, count = tiles_of(j)
        tiles = [
            combined(jnp.concatenate([recv_c[pl.ds(2 * (8 * j + i) + t, 1)] for i in range(8)], axis=0))
            for t in range(count)
        ]
        row = jnp.concatenate(tiles, axis=1)
        start = 2 * COLS * j - 128 * first
        parts.append(row[:, start : start + 2 * COLS])
    top = parts[0]
    for part in parts[1:]:
        top = jnp.maximum(top, part)
    both = top + jnp.log2(sum(jnp.exp2(part - top) for part in parts))
    ours, theirs = both[:, :COLS], both[:, COLS:]
    final[0] = jnp.concatenate([theirs, jnp.zeros((1, 128 - COLS), F32)], axis=1)
    swap = remote(final.at[0], final.at[1], fin_send, fin_recv, sibling)
    swap.start()
    swap.wait_recv()
    theirs = final[1][:, :COLS]
    top = jnp.maximum(ours, theirs)
    score = top + jnp.log2(jnp.exp2(ours - top) + jnp.exp2(theirs - top))
    g_out[...] = pot_buf[...] - (EPS * LN2) * score + EPS * (
        math.log(float(CHIPS * NX * NC * ROWS)) - math.log(float(CHIPS * NX * NC * COLS))
    )

    gather_c.wait_send()
    swap.wait_send()


def per_device(gen_samples, data_samples, data_potential):
    hbm = pl.BlockSpec(memory_space=pltpu.HBM)
    vmem = pl.BlockSpec(memory_space=pltpu.VMEM)
    dma = pltpu.SemaphoreType.DMA
    f, g = pl.pallas_call(
        kernel,
        out_shape=(jax.ShapeDtypeStruct((1, ROWS), F32), jax.ShapeDtypeStruct((1, COLS), F32)),
        in_specs=[hbm, hbm, hbm],
        out_specs=(vmem, vmem),
        scratch_shapes=[
            pltpu.VMEM((NX, ROWS, WIDTH), BF16),
            pltpu.VMEM((1, COLS), F32),
            pltpu.VMEM((1, ROWS), F32),
            pltpu.VMEM((2 * CHIPS, COLS, WIDTH), BF16),
            pltpu.VMEM((2 * CHIPS, 1, 128), F32),
            pltpu.VMEM((2 * CHIPS, COLS, NX * ROWS), F32),
            pltpu.VMEM((8, NX * ROWS), F32),
            pltpu.VMEM((8, NX * ROWS), F32),
            pltpu.VMEM((NX, NX, 1, ROWS), F32),
            pltpu.VMEM((BATCH, 128), F32),
            pltpu.VMEM((BATCH, 128), F32),
            pltpu.VMEM((8, BATCH // 128, 1, 128), F32),
            pltpu.VMEM((2 * CHIPS, 1, 128), F32),
            pltpu.VMEM((2, 1, 128), F32),
            dma((3,)), dma((2,)), dma((2,)),
            dma((2, 2)), dma((2, 2)), dma((2, 5, 2)), dma((2, 5, 2)), dma((2, 8)), dma((2, 8)),
            dma, dma, dma, dma, dma, dma,
        ],
        compiler_params=pltpu.CompilerParams(
            collective_id=0, has_side_effects=True, vmem_limit_bytes=40 * 2**20
        ),
    )(*[
        pltpu.with_memory_space_constraint(array, pltpu.HBM)
        for array in (gen_samples, data_samples, data_potential.reshape(1, COLS))
    ])
    return f.reshape(ROWS), g.reshape(COLS)


def solution(mesh):
    in_specs = (P(("gen", "dat"), None), P(("dat", "gen"), None), P(("dat", "gen")))
    out_specs = (P(("gen", "dat")), P(("dat", "gen")))
    return jax.shard_map(
        per_device, mesh=mesh, in_specs=in_specs, out_specs=out_specs, check_vma=False
    )
```

```python
import math

import jax
import jax.numpy as jnp
from jax import lax
from jax.experimental import pallas as pl
from jax.experimental.pallas import tpu as pltpu
from jax.sharding import PartitionSpec as P

EPS = 0.05
LOG2E = math.log2(math.e)
LN2 = math.log(2.0)
SCALE = LOG2E / EPS
LOW = -1e30
MESH = pl.DeviceIdType.MESH
F32 = jnp.float32
BF16 = jnp.bfloat16

NX, NY, NZ, NC = 4, 8, 8, 2
CHIPS = NY * NZ
ROWS = 256
COLS = 24
WIDTH = 256
BATCH = 8 * NC * COLS
KEEP = 1.0 / WIDTH


def hops(d):
    return min(d % 8, -d % 8)


NEAR0 = [(0, 0), (0, 2), (0, -2), (2, 1), (2, -1), (-2, 1), (-2, -1), (0, 4)]
FAR0 = [(4, 0), (2, 3), (2, -3), (-2, 3), (-2, -3)]
NEAR2 = ([(0, 1), (2, 2), (-2, 2), (2, 0)], [(0, -1), (2, -2), (-2, -2), (-2, 0)])
FAR2 = ([(0, 3), (4, 1), (2, 4)], [(0, -3), (4, -1), (-2, 4)])


def shifted(offsets, dp, dq):
    return [(a + dp, b + dq) for a, b in offsets]


def folded(offset):
    return tuple((d + 3) % 8 - 3 for d in offset)


FIRST = NEAR0 + FAR0
NEAR = shifted(NEAR0, 1, 0) + shifted(NEAR0, -1, 0) + NEAR2[0] + NEAR2[1]
FAR = shifted(FAR0, 1, 0) + shifted(FAR0, -1, 0) + FAR2[0] + FAR2[1]
REST = sorted({folded((a, b)) for a in range(8) for b in range(8)} - {folded(o) for o in FIRST + NEAR + FAR})


def holders(offsets):
    chosen = {}
    for offset in offsets:
        ways = [folded((offset[0] - a, offset[1] - b)) for a, b in FIRST]
        used = list(chosen.values())
        chosen[offset] = min(ways, key=lambda way: (abs(way[0]) + abs(way[1]), used.count(way), way))
    return chosen


HOLDER = holders(REST)
NEAR0_SET = {folded(o) for o in NEAR0}
REST_PARTS = ([], [])
for rest in REST:
    held = folded((rest[0] - HOLDER[rest][0], rest[1] - HOLDER[rest][1]))
    REST_PARTS[held not in NEAR0_SET].append(rest)
ORDER = FIRST + NEAR + REST_PARTS[0] + FAR + REST_PARTS[1]
SLOT = {(a % 8, b % 8): slot for slot, (a, b) in enumerate(ORDER)}
FIRST_NEAR, FIRST_FAR = len(FIRST), len(FIRST + NEAR + REST_PARTS[0])
COUNTS = ((8, 8, 4, 4, len(REST_PARTS[0])), (5, 5, 3, 3, len(REST_PARTS[1])))


ALL = sorted((folded((a, b)) for a in range(8) for b in range(8)), key=lambda o: (-abs(o[0]) - abs(o[1]), o))
BATCHES = [ALL[i : i + 8] for i in range(0, 56, 8)] + [ALL[:55:-1]]


def slot_of(dp, dq):
    return SLOT[dp % 8, dq % 8]


def squares(values):
    wide = values.astype(F32)
    wide = wide * wide
    high = wide.astype(BF16)
    low = (wide - high.astype(F32)).astype(BF16)
    ones = jnp.ones((8, WIDTH), BF16)
    dims = (((1,), (1,)), ((), ()))
    return lax.dot_general(ones, high, dims, preferred_element_type=F32) + lax.dot_general(
        ones, low, dims, preferred_element_type=F32
    )


def kernel(
    gen_hbm, data_hbm, pot_hbm, f_out, g_out,
    x_buf, pot_buf, sq_buf, blocks, terms, stash, row_m, row_s, row_l,
    batch_a, batch_b, send_c, recv_c, final,
    local_sem, x_send, x_recv, one_send, one_recv, two_send, two_recv, sib_send, sib_recv,
    row_send, row_recv, col_send, col_recv, fin_send, fin_recv,
):
    gen = lax.axis_index("gen")
    dat = lax.axis_index("dat")
    x, c = (dat // 2) % NX, dat % 2
    y, z = (dat // 8) * 4 + gen % 4, gen // 4

    def device(x_, y_, z_, c_):
        return (z_ * 4 + y_ % 4, (y_ // 4) * 8 + x_ * 2 + c_)

    p, q = y + c * (z - y), z + c * (y - z)

    def in_plane(p_, q_):
        p_, q_ = p_ % 8, q_ % 8
        return device(x, p_ + c * (q_ - p_), q_ + c * (p_ - q_), c)

    sibling = device(x, y, z, 1 - c)
    x_peers = {d: device((x + d) % NX, y, z, c) for d in (1, 3, 2)}
    near = [in_plane(p + 1, q), in_plane(p - 1, q), in_plane(p, q + 1), in_plane(p, q - 1)]
    around = {(1, 0), (-1, 0), (0, 1), (0, -1)}
    others = sorted(({folded(o) for o in FIRST[1:]} | set(HOLDER.values())) - around, key=lambda o: -abs(o[0]) - abs(o[1]))
    group = [in_plane(p + dp, q + dq) for dp, dq in others]

    loads = [
        pltpu.make_async_copy(data_hbm, blocks.at[0], local_sem.at[0]),
        pltpu.make_async_copy(pot_hbm, pot_buf, local_sem.at[1]),
        pltpu.make_async_copy(gen_hbm, x_buf.at[0], local_sem.at[2]),
    ]
    for copy in loads:
        copy.start()

    peers = group + near + list(x_peers.values()) + [sibling]
    barrier = pltpu.get_barrier_semaphore()
    for peer in peers:
        pl.semaphore_signal(barrier, inc=1, device_id=peer, device_id_type=MESH)

    pl.semaphore_wait(barrier, len(peers))

    def remote(src, dst, send, recv, peer):
        return pltpu.make_async_remote_copy(
            src_ref=src, dst_ref=dst, send_sem=send, recv_sem=recv, device_id=peer, device_id_type=MESH
        )

    def to_group(i, ref, source):
        for dp, dq in reversed(FIRST[1:]):
            far = int((dp, dq) in FAR0)
            remote(
                source, ref.at[slot_of(dp, dq)], one_send.at[i, far], one_recv.at[i, far], in_plane(p - dp, q - dq)
            ).start()

    to_group(0, blocks, data_hbm)
    for d, peer in x_peers.items():
        remote(gen_hbm, x_buf.at[NX - d], x_send.at[int(d == 2)], x_recv.at[int(d == 2)], peer).start()

    for copy in loads[:2]:
        copy.wait()
    term = (pot_buf[...] - squares(blocks[0])[0:1, :] * KEEP) * SCALE
    terms[0] = jnp.concatenate([term, jnp.zeros((1, 128 - COLS), F32)], axis=1)
    to_group(1, terms, terms.at[0])

    row_m[...] = jnp.full(row_m.shape, LOW, F32)
    row_s[...] = jnp.zeros(row_s.shape, F32)
    loads[2].wait()
    sq_buf[...] = squares(x_buf[0])[0:1, :]

    refs = (blocks, terms)

    def from_group(far):
        return [
            remote(
                ref.at[pl.ds(0, (7, 5)[far])], ref.at[pl.ds(0, (7, 5)[far])],
                one_send.at[i, far], one_recv.at[i, far], sibling,
            )
            for i, ref in enumerate(refs)
        ]

    def to_near(k, far, count, src, dst, peer):
        return [
            remote(
                ref.at[pl.ds(src, count)], ref.at[pl.ds(dst, count)],
                two_send.at[i, k, far], two_recv.at[i, k, far], peer,
            )
            for i, ref in enumerate(refs)
        ]

    def send_near(i, far):
        count = COUNTS[far][0]
        for dp, dq in REST_PARTS[far]:
            hp, hq = HOLDER[dp, dq]
            to_near(4, far, 1, slot_of(dp - hp, dq - hq), slot_of(dp, dq), in_plane(p - hp, q - hq))[i].start()
        for k in range(2):
            to_near(k, far, count, 8 * far, (FIRST_NEAR, FIRST_FAR)[far] + k * count, near[1 - k])[i].start()
        for side, ways in enumerate((NEAR2, FAR2)[far]):
            for dp, dq in ways:
                held = slot_of(dp, dq + 2 * side - 1)
                to_near(2 + side, far, 1, held, slot_of(dp, dq), near[3 - side])[i].start()

    def from_near(k, far):
        return to_near(k, far, COUNTS[far][k], 0, 0, sibling)

    def to_sibling(k, start, count):
        return [
            remote(
                ref.at[pl.ds(start, count)], ref.at[pl.ds(CHIPS + start, count)],
                sib_send.at[i, k], sib_recv.at[i, k], sibling,
            )
            for i, ref in enumerate(refs)
        ]

    passed_on = [to_sibling(0, 0, 8), to_sibling(1, 8, 5), to_sibling(2, FIRST_NEAR, sum(COUNTS[0]))]
    last_on = [to_sibling(3 + k, FIRST_FAR + sum(COUNTS[1][:k]), COUNTS[1][k]) for k in range(5)]
    for far in range(2):
        for i in range(2):
            from_group(far)[i].wait_recv()
            send_near(i, far)
            passed_on[far][i].start()

    gather_x = [
        remote(x_buf.at[pl.ds(0, n)], x_buf.at[pl.ds(0, n)], x_send.at[i], x_recv.at[i], sibling)
        for i, n in enumerate((2, 1))
    ]
    gather_x[0].wait_recv()

    def row_unit(start, count, which=(0, 1, 2, 3)):
        cols = blocks[pl.ds(start, count)].astype(F32).reshape(count * COLS, WIDTH).astype(BF16)
        shape = (count, COLS, 128)
        on_diagonal = lax.broadcasted_iota(jnp.int32, shape, 2) == lax.broadcasted_iota(jnp.int32, shape, 1)
        spread = jnp.where(on_diagonal, jnp.broadcast_to(terms[pl.ds(start, count)], shape), 0.0)
        term_ = jnp.sum(spread, axis=2, keepdims=True).reshape(count * COLS, 1)
        for b in which:
            lanes = slice(b * ROWS, (b + 1) * ROWS)
            cross = lax.dot_general(cols, x_buf[b], (((1,), (1,)), ((), ())), preferred_element_type=F32)
            scores = cross * (2.0 * KEEP * SCALE) + term_
            stash[pl.ds(start, count), :, lanes] = scores.reshape(count, COLS, ROWS)
            parts = scores.reshape(count * COLS // 8, 8, ROWS)
            old = row_m[:, lanes]
            top = jnp.maximum(old, jnp.max(parts, axis=0))
            row_m[:, lanes] = top
            row_s[:, lanes] = row_s[:, lanes] * jnp.exp2(old - top) + jnp.sum(
                jnp.exp2(parts - top[None]), axis=0
            )

    def first_units(step, _):
        @pl.when(step == 1)
        def _():
            for k in range(5):
                for copy in from_near(k, 0):
                    copy.wait_recv()
            for copy in passed_on[2]:
                copy.start()
            for copy in passed_on[0] + passed_on[1]:
                copy.wait_recv()

        row_unit(CHIPS * step, 13, (0, 1, 3))
        return 0

    def first_opposite(step, _):
        row_unit(CHIPS * step, 13, (2,))
        return 0

    lax.fori_loop(0, 2, first_units, 0)
    gather_x[1].wait_recv()
    lax.fori_loop(0, 2, first_opposite, 0)

    def next_units(step, _):
        @pl.when(step == 1)
        def _():
            for copy in passed_on[2]:
                copy.wait_recv()

        row_unit(FIRST_NEAR + CHIPS * step, sum(COUNTS[0]))
        return 0

    lax.fori_loop(0, 2, next_units, 0)

    def last_units(step, _):
        @pl.when(step == 0)
        def _():
            for k in range(5):
                for copy in from_near(k, 1):
                    copy.wait_recv()
                for copy in last_on[k]:
                    copy.start()

        @pl.when(step == 1)
        def _():
            for copy in sum(last_on, []):
                copy.wait_recv()

        row_unit(FIRST_FAR + CHIPS * step, sum(COUNTS[1]))
        return 0

    lax.fori_loop(0, 2, last_units, 0)

    def combined(values):
        top = jnp.max(values, axis=0)
        return top + jnp.log2(jnp.sum(jnp.exp2(values - top[None]), axis=0))

    m = row_m[...]
    top = jnp.max(m, axis=0, keepdims=True)
    total = jnp.sum(row_s[...] * jnp.exp2(m - top), axis=0, keepdims=True)
    local = top + jnp.log2(total)
    for b in range(NX):
        row_l[0, b] = local[:, b * ROWS : (b + 1) * ROWS]
    for d, peer in x_peers.items():
        for b in range(NX):
            remote(row_l.at[0, b], row_l.at[NX - d, (b - d) % NX], row_send, row_recv, peer).start()
    gather_l = remote(row_l.at[pl.ds(0, 3)], row_l.at[pl.ds(0, 3)], row_send, row_recv, sibling)
    gather_l.wait_recv()
    whole = combined(row_l[...])
    lifted = jnp.concatenate([jnp.broadcast_to(whole[b], (8, ROWS)) for b in range(NX)], axis=1)

    lane_tiles = NX * ROWS // 128

    def batch_parts(batch, batch_ref):
        for j, (dp, dq) in enumerate(batch):
            for h, at in enumerate((slot_of(dp, dq), CHIPS + slot_of(dq, dp))):
                scores = stash[at].reshape(COLS // 8, 8, NX * ROWS) - lifted[None]
                pieces = [scores[:, :, i * 128 : (i + 1) * 128] for i in range(lane_tiles)]
                peak = pieces[0]
                for piece in pieces[1:]:
                    peak = jnp.maximum(peak, piece)
                added = jnp.exp2(pieces[0] - peak)
                for piece in pieces[1:]:
                    added = added + jnp.exp2(piece - peak)
                to = (2 * j + h) * COLS
                batch_ref[to : to + COLS, :] = (peak + jnp.log2(added)).reshape(COLS, 128)

    def tiles_of(j):
        first = 2 * COLS * j // 128
        return first, (2 * COLS * (j + 1) - 1) // 128 - first + 1

    def batch_send(i, batch_ref):
        values = jnp.transpose(batch_ref[...])
        top = jnp.max(values, axis=0, keepdims=True)
        sums = top + jnp.log2(jnp.sum(jnp.exp2(values - top), axis=0, keepdims=True))
        for t in range(BATCH // 128):
            send_c[i, t] = sums[:, 128 * t : 128 * (t + 1)]
        for j, (dp, dq) in enumerate(BATCHES[i]):
            first, count = tiles_of(j)
            seen = 2 * (8 * j + i)
            if (dp, dq) == (0, 0):
                recv_c[seen] = sums[:, :128]
            else:
                remote(
                    send_c.at[i, pl.ds(first, count)], recv_c.at[pl.ds(seen, count)],
                    col_send, col_recv, in_plane(p + dp, q + dq),
                ).start()

    room = (batch_a, batch_b)
    batch_parts(BATCHES[0], room[0])
    for i in range(8):
        if i < 7:
            batch_parts(BATCHES[i + 1], room[(i + 1) % 2])
        batch_send(i, room[i % 2])

    f_out[...] = sq_buf[...] * KEEP - (EPS * LN2) * whole[0] + EPS * math.log(float(CHIPS * NX * NC * COLS))

    tiles = 8 * sum(tiles_of(j)[1] for j in range(8)) - 1
    gather_c = remote(recv_c.at[pl.ds(0, tiles)], recv_c.at[pl.ds(0, tiles)], col_send, col_recv, sibling)
    for copy in gather_x + [gather_l]:
        copy.wait_send()
    for far in range(2):
        for copy in from_group(far) + sum((from_near(k, far) for k in range(5)), []):
            copy.wait_send()
    for copy in sum(passed_on + last_on, []):
        copy.wait_send()
    gather_c.wait_recv()

    parts = []
    for j in range(8):
        first, count = tiles_of(j)
        tiles = [
            combined(jnp.concatenate([recv_c[pl.ds(2 * (8 * j + i) + t, 1)] for i in range(8)], axis=0))
            for t in range(count)
        ]
        row = jnp.concatenate(tiles, axis=1)
        start = 2 * COLS * j - 128 * first
        parts.append(row[:, start : start + 2 * COLS])
    top = parts[0]
    for part in parts[1:]:
        top = jnp.maximum(top, part)
    both = top + jnp.log2(sum(jnp.exp2(part - top) for part in parts))
    ours, theirs = both[:, :COLS], both[:, COLS:]
    final[0] = jnp.concatenate([theirs, jnp.zeros((1, 128 - COLS), F32)], axis=1)
    swap = remote(final.at[0], final.at[1], fin_send, fin_recv, sibling)
    swap.start()
    swap.wait_recv()
    theirs = final[1][:, :COLS]
    top = jnp.maximum(ours, theirs)
    score = top + jnp.log2(jnp.exp2(ours - top) + jnp.exp2(theirs - top))
    g_out[...] = pot_buf[...] - (EPS * LN2) * score + EPS * (
        math.log(float(CHIPS * NX * NC * ROWS)) - math.log(float(CHIPS * NX * NC * COLS))
    )

    gather_c.wait_send()
    swap.wait_send()


def per_device(gen_samples, data_samples, data_potential):
    hbm = pl.BlockSpec(memory_space=pltpu.HBM)
    vmem = pl.BlockSpec(memory_space=pltpu.VMEM)
    dma = pltpu.SemaphoreType.DMA
    f, g = pl.pallas_call(
        kernel,
        out_shape=(jax.ShapeDtypeStruct((1, ROWS), F32), jax.ShapeDtypeStruct((1, COLS), F32)),
        in_specs=[hbm, hbm, hbm],
        out_specs=(vmem, vmem),
        scratch_shapes=[
            pltpu.VMEM((NX, ROWS, WIDTH), BF16),
            pltpu.VMEM((1, COLS), F32),
            pltpu.VMEM((1, ROWS), F32),
            pltpu.VMEM((2 * CHIPS, COLS, WIDTH), BF16),
            pltpu.VMEM((2 * CHIPS, 1, 128), F32),
            pltpu.VMEM((2 * CHIPS, COLS, NX * ROWS), F32),
            pltpu.VMEM((8, NX * ROWS), F32),
            pltpu.VMEM((8, NX * ROWS), F32),
            pltpu.VMEM((NX, NX, 1, ROWS), F32),
            pltpu.VMEM((BATCH, 128), F32),
            pltpu.VMEM((BATCH, 128), F32),
            pltpu.VMEM((8, BATCH // 128, 1, 128), F32),
            pltpu.VMEM((2 * CHIPS, 1, 128), F32),
            pltpu.VMEM((2, 1, 128), F32),
            dma((3,)), dma((2,)), dma((2,)),
            dma((2, 2)), dma((2, 2)), dma((2, 5, 2)), dma((2, 5, 2)), dma((2, 8)), dma((2, 8)),
            dma, dma, dma, dma, dma, dma,
        ],
        compiler_params=pltpu.CompilerParams(
            collective_id=0, has_side_effects=True, vmem_limit_bytes=40 * 2**20
        ),
    )(*[
        pltpu.with_memory_space_constraint(array, pltpu.HBM)
        for array in (gen_samples, data_samples, data_potential.reshape(1, COLS))
    ])
    return f.reshape(ROWS), g.reshape(COLS)


def solution(mesh):
    in_specs = (P(("gen", "dat"), None), P(("dat", "gen"), None), P(("dat", "gen")))
    out_specs = (P(("gen", "dat")), P(("dat", "gen")))
    return jax.shard_map(
        per_device, mesh=mesh, in_specs=in_specs, out_specs=out_specs, check_vma=False
    )
```

```python
import math

import jax
import jax.numpy as jnp
from jax import lax
from jax.experimental import pallas as pl
from jax.experimental.pallas import tpu as pltpu
from jax.sharding import PartitionSpec as P

EPS = 0.05
LOG2E = math.log2(math.e)
LN2 = math.log(2.0)
SCALE = LOG2E / EPS
LOW = -1e30
MESH = pl.DeviceIdType.MESH
F32 = jnp.float32
BF16 = jnp.bfloat16

NX, NY, NZ, NC = 4, 8, 8, 2
CHIPS = NY * NZ
ROWS = 256
COLS = 24
WIDTH = 256
BATCH = 8 * NC * COLS
KEEP = 1.0 / WIDTH


def hops(d):
    return min(d % 8, -d % 8)


NEAR0 = [(0, 0), (0, 2), (0, -2), (2, 1), (2, -1), (-2, 1), (-2, -1), (0, 4)]
FAR0 = [(4, 0), (2, 3), (2, -3), (-2, 3), (-2, -3)]
NEAR2 = ([(0, 1), (2, 2), (-2, 2), (2, 0)], [(0, -1), (2, -2), (-2, -2), (-2, 0)])
FAR2 = ([(0, 3), (4, 1), (2, 4)], [(0, -3), (4, -1), (-2, 4)])


def shifted(offsets, dp, dq):
    return [(a + dp, b + dq) for a, b in offsets]


def folded(offset):
    return tuple((d + 3) % 8 - 3 for d in offset)


FIRST = NEAR0 + FAR0
ORDER = (
    FIRST
    + shifted(NEAR0, 1, 0) + shifted(NEAR0, -1, 0) + NEAR2[0] + NEAR2[1]
    + shifted(FAR0, 1, 0) + shifted(FAR0, -1, 0) + FAR2[0] + FAR2[1]
)
REST = sorted({folded((a, b)) for a in range(8) for b in range(8)} - {folded(o) for o in ORDER})
SLOT = {(a % 8, b % 8): slot for slot, (a, b) in enumerate(ORDER + REST)}


def holders(offsets):
    chosen = {}
    for offset in offsets:
        ways = [folded((offset[0] - a, offset[1] - b)) for a, b in FIRST]
        used = list(chosen.values())
        chosen[offset] = min(ways, key=lambda way: (abs(way[0]) + abs(way[1]), used.count(way), way))
    return chosen


HOLDER = holders(REST)
ALL = sorted((folded((a, b)) for a in range(8) for b in range(8)), key=lambda o: (-abs(o[0]) - abs(o[1]), o))
BATCHES = [ALL[i : i + 8] for i in range(0, 56, 8)] + [ALL[:55:-1]]


def slot_of(dp, dq):
    return SLOT[dp % 8, dq % 8]


def squares(values):
    wide = values.astype(F32)
    wide = wide * wide
    high = wide.astype(BF16)
    low = (wide - high.astype(F32)).astype(BF16)
    ones = jnp.ones((8, WIDTH), BF16)
    dims = (((1,), (1,)), ((), ()))
    return lax.dot_general(ones, high, dims, preferred_element_type=F32) + lax.dot_general(
        ones, low, dims, preferred_element_type=F32
    )


def kernel(
    gen_hbm, data_hbm, pot_hbm, f_out, g_out,
    x_buf, pot_buf, sq_buf, blocks, terms, stash, row_m, row_s, row_l,
    batch_a, batch_b, send_c, recv_c, final,
    local_sem, x_send, x_recv, one_send, one_recv, two_send, two_recv, sib_send, sib_recv,
    row_send, row_recv, col_send, col_recv, fin_send, fin_recv,
):
    gen = lax.axis_index("gen")
    dat = lax.axis_index("dat")
    x, c = (dat // 2) % NX, dat % 2
    y, z = (dat // 8) * 4 + gen % 4, gen // 4

    def device(x_, y_, z_, c_):
        return (z_ * 4 + y_ % 4, (y_ // 4) * 8 + x_ * 2 + c_)

    p, q = y + c * (z - y), z + c * (y - z)

    def in_plane(p_, q_):
        p_, q_ = p_ % 8, q_ % 8
        return device(x, p_ + c * (q_ - p_), q_ + c * (p_ - q_), c)

    sibling = device(x, y, z, 1 - c)
    x_peers = {d: device((x + d) % NX, y, z, c) for d in (1, 3, 2)}
    near = [in_plane(p + 1, q), in_plane(p - 1, q), in_plane(p, q + 1), in_plane(p, q - 1)]
    around = {(1, 0), (-1, 0), (0, 1), (0, -1)}
    others = sorted(({folded(o) for o in FIRST[1:]} | set(HOLDER.values())) - around, key=lambda o: -abs(o[0]) - abs(o[1]))
    group = [in_plane(p + dp, q + dq) for dp, dq in others]

    loads = [
        pltpu.make_async_copy(data_hbm, blocks.at[0], local_sem.at[0]),
        pltpu.make_async_copy(pot_hbm, pot_buf, local_sem.at[1]),
        pltpu.make_async_copy(gen_hbm, x_buf.at[0], local_sem.at[2]),
    ]
    for copy in loads:
        copy.start()

    peers = group + near + list(x_peers.values()) + [sibling]
    barrier = pltpu.get_barrier_semaphore()
    for peer in peers:
        pl.semaphore_signal(barrier, inc=1, device_id=peer, device_id_type=MESH)

    pl.semaphore_wait(barrier, len(peers))

    def remote(src, dst, send, recv, peer):
        return pltpu.make_async_remote_copy(
            src_ref=src, dst_ref=dst, send_sem=send, recv_sem=recv, device_id=peer, device_id_type=MESH
        )

    def to_group(i, ref, source):
        for dp, dq in reversed(FIRST[1:]):
            far = int((dp, dq) in FAR0)
            remote(
                source, ref.at[slot_of(dp, dq)], one_send.at[i, far], one_recv.at[i, far], in_plane(p - dp, q - dq)
            ).start()

    to_group(0, blocks, data_hbm)
    for d, peer in x_peers.items():
        remote(gen_hbm, x_buf.at[NX - d], x_send.at[int(d == 2)], x_recv.at[int(d == 2)], peer).start()

    for copy in loads[:2]:
        copy.wait()
    term = (pot_buf[...] - squares(blocks[0])[0:1, :] * KEEP) * SCALE
    terms[0] = jnp.concatenate([term, jnp.zeros((1, 128 - COLS), F32)], axis=1)
    to_group(1, terms, terms.at[0])

    row_m[...] = jnp.full(row_m.shape, LOW, F32)
    row_s[...] = jnp.zeros(row_s.shape, F32)
    loads[2].wait()
    sq_buf[...] = squares(x_buf[0])[0:1, :]

    refs = (blocks, terms)

    def from_group(far):
        return [
            remote(
                ref.at[pl.ds(0, (7, 5)[far])], ref.at[pl.ds(0, (7, 5)[far])],
                one_send.at[i, far], one_recv.at[i, far], sibling,
            )
            for i, ref in enumerate(refs)
        ]

    def to_near(k, far, count, src, dst, peer):
        return [
            remote(
                ref.at[pl.ds(src, count)], ref.at[pl.ds(dst, count)],
                two_send.at[i, k, far], two_recv.at[i, k, far], peer,
            )
            for i, ref in enumerate(refs)
        ]

    def send_near(i, far):
        count = (8, 5)[far]
        for k in range(2):
            to_near(k, far, count, 8 * far, (13, 37)[far] + k * count, near[1 - k])[i].start()
        for side, ways in enumerate((NEAR2, FAR2)[far]):
            for dp, dq in ways:
                held = slot_of(dp, dq + 2 * side - 1)
                to_near(2 + side, far, 1, held, slot_of(dp, dq), near[3 - side])[i].start()
        if far:
            for (dp, dq), (hp, hq) in HOLDER.items():
                to_near(4, far, 1, slot_of(dp - hp, dq - hq), slot_of(dp, dq), in_plane(p - hp, q - hq))[i].start()

    def from_near(k, far):
        return to_near(k, far, (8, 8, 4, 4, 0)[k] if not far else (5, 5, 3, 3, len(REST))[k], 0, 0, sibling)

    def to_sibling(k, start, count):
        return [
            remote(
                ref.at[pl.ds(start, count)], ref.at[pl.ds(CHIPS + start, count)],
                sib_send.at[i, k], sib_recv.at[i, k], sibling,
            )
            for i, ref in enumerate(refs)
        ]

    pieces = ((37, 5), (42, 5), (47, 3), (50, 3), (53, len(REST)))
    passed_on = [to_sibling(0, 0, 8), to_sibling(1, 8, 5)]
    near_on = [to_sibling(2 + k, *piece) for k, piece in enumerate(((13, 8), (21, 8), (29, 4), (33, 4)))]
    last_on = [to_sibling(6 + k, *piece) for k, piece in enumerate(pieces)]
    for far in range(2):
        for i in range(2):
            from_group(far)[i].wait_recv()
            send_near(i, far)
            passed_on[far][i].start()

    gather_x = [
        remote(x_buf.at[pl.ds(0, n)], x_buf.at[pl.ds(0, n)], x_send.at[i], x_recv.at[i], sibling)
        for i, n in enumerate((2, 1))
    ]
    gather_x[0].wait_recv()

    def row_unit(start, count, which=(0, 1, 2, 3)):
        cols = blocks[pl.ds(start, count)].astype(F32).reshape(count * COLS, WIDTH).astype(BF16)
        shape = (count, COLS, 128)
        on_diagonal = lax.broadcasted_iota(jnp.int32, shape, 2) == lax.broadcasted_iota(jnp.int32, shape, 1)
        spread = jnp.where(on_diagonal, jnp.broadcast_to(terms[pl.ds(start, count)], shape), 0.0)
        term_ = jnp.sum(spread, axis=2, keepdims=True).reshape(count * COLS, 1)
        for b in which:
            lanes = slice(b * ROWS, (b + 1) * ROWS)
            cross = lax.dot_general(cols, x_buf[b], (((1,), (1,)), ((), ())), preferred_element_type=F32)
            scores = cross * (2.0 * KEEP * SCALE) + term_
            stash[pl.ds(start, count), :, lanes] = scores.reshape(count, COLS, ROWS)
            parts = scores.reshape(count * COLS // 8, 8, ROWS)
            old = row_m[:, lanes]
            top = jnp.maximum(old, jnp.max(parts, axis=0))
            row_m[:, lanes] = top
            row_s[:, lanes] = row_s[:, lanes] * jnp.exp2(old - top) + jnp.sum(
                jnp.exp2(parts - top[None]), axis=0
            )

    def first_units(step, _):
        @pl.when(step == 1)
        def _():
            for copy in passed_on[0] + passed_on[1]:
                copy.wait_recv()

        row_unit(CHIPS * step, 13, (0, 1, 3))
        return 0

    def first_opposite(step, _):
        row_unit(CHIPS * step, 13, (2,))
        return 0

    lax.fori_loop(0, 2, first_units, 0)
    gather_x[1].wait_recv()
    lax.fori_loop(0, 2, first_opposite, 0)

    def next_units(step, _):
        @pl.when(step == 0)
        def _():
            for k in range(4):
                for copy in from_near(k, 0):
                    copy.wait_recv()
                for copy in near_on[k]:
                    copy.start()

        @pl.when(step == 1)
        def _():
            for copy in sum(near_on, []):
                copy.wait_recv()

        row_unit(13 + CHIPS * step, 24)
        return 0

    lax.fori_loop(0, 2, next_units, 0)

    def last_units(step, _):
        @pl.when(step == 0)
        def _():
            for k in range(5):
                for copy in from_near(k, 1):
                    copy.wait_recv()
                for copy in last_on[k]:
                    copy.start()

        @pl.when(step == 1)
        def _():
            for copy in sum(last_on, []):
                copy.wait_recv()

        row_unit(37 + CHIPS * step, 27)
        return 0

    lax.fori_loop(0, 2, last_units, 0)

    def combined(values):
        top = jnp.max(values, axis=0)
        return top + jnp.log2(jnp.sum(jnp.exp2(values - top[None]), axis=0))

    m = row_m[...]
    top = jnp.max(m, axis=0, keepdims=True)
    total = jnp.sum(row_s[...] * jnp.exp2(m - top), axis=0, keepdims=True)
    local = top + jnp.log2(total)
    for b in range(NX):
        row_l[0, b] = local[:, b * ROWS : (b + 1) * ROWS]
    for d, peer in x_peers.items():
        for b in range(NX):
            remote(row_l.at[0, b], row_l.at[NX - d, (b - d) % NX], row_send, row_recv, peer).start()
    gather_l = remote(row_l.at[pl.ds(0, 3)], row_l.at[pl.ds(0, 3)], row_send, row_recv, sibling)
    gather_l.wait_recv()
    whole = combined(row_l[...])
    lifted = jnp.concatenate([jnp.broadcast_to(whole[b], (8, ROWS)) for b in range(NX)], axis=1)

    lane_tiles = NX * ROWS // 128

    def batch_parts(batch, batch_ref):
        for j, (dp, dq) in enumerate(batch):
            for h, at in enumerate((slot_of(dp, dq), CHIPS + slot_of(dq, dp))):
                scores = stash[at].reshape(COLS // 8, 8, NX * ROWS) - lifted[None]
                pieces = [scores[:, :, i * 128 : (i + 1) * 128] for i in range(lane_tiles)]
                peak = pieces[0]
                for piece in pieces[1:]:
                    peak = jnp.maximum(peak, piece)
                added = jnp.exp2(pieces[0] - peak)
                for piece in pieces[1:]:
                    added = added + jnp.exp2(piece - peak)
                to = (2 * j + h) * COLS
                batch_ref[to : to + COLS, :] = (peak + jnp.log2(added)).reshape(COLS, 128)

    def tiles_of(j):
        first = 2 * COLS * j // 128
        return first, (2 * COLS * (j + 1) - 1) // 128 - first + 1

    def batch_send(i, batch_ref):
        values = jnp.transpose(batch_ref[...])
        top = jnp.max(values, axis=0, keepdims=True)
        sums = top + jnp.log2(jnp.sum(jnp.exp2(values - top), axis=0, keepdims=True))
        for t in range(BATCH // 128):
            send_c[i, t] = sums[:, 128 * t : 128 * (t + 1)]
        for j, (dp, dq) in enumerate(BATCHES[i]):
            first, count = tiles_of(j)
            seen = 2 * (8 * j + i)
            if (dp, dq) == (0, 0):
                recv_c[seen] = sums[:, :128]
            else:
                remote(
                    send_c.at[i, pl.ds(first, count)], recv_c.at[pl.ds(seen, count)],
                    col_send, col_recv, in_plane(p + dp, q + dq),
                ).start()

    room = (batch_a, batch_b)
    batch_parts(BATCHES[0], room[0])
    for i in range(8):
        if i < 7:
            batch_parts(BATCHES[i + 1], room[(i + 1) % 2])
        batch_send(i, room[i % 2])

    f_out[...] = sq_buf[...] * KEEP - (EPS * LN2) * whole[0] + EPS * math.log(float(CHIPS * NX * NC * COLS))

    tiles = 8 * sum(tiles_of(j)[1] for j in range(8)) - 1
    gather_c = remote(recv_c.at[pl.ds(0, tiles)], recv_c.at[pl.ds(0, tiles)], col_send, col_recv, sibling)
    for copy in gather_x + [gather_l]:
        copy.wait_send()
    for far in range(2):
        for copy in from_group(far) + sum((from_near(k, far) for k in range(4 + far)), []):
            copy.wait_send()
    for copy in sum(passed_on + near_on + last_on, []):
        copy.wait_send()
    gather_c.wait_recv()

    parts = []
    for j in range(8):
        first, count = tiles_of(j)
        tiles = [
            combined(jnp.concatenate([recv_c[pl.ds(2 * (8 * j + i) + t, 1)] for i in range(8)], axis=0))
            for t in range(count)
        ]
        row = jnp.concatenate(tiles, axis=1)
        start = 2 * COLS * j - 128 * first
        parts.append(row[:, start : start + 2 * COLS])
    top = parts[0]
    for part in parts[1:]:
        top = jnp.maximum(top, part)
    both = top + jnp.log2(sum(jnp.exp2(part - top) for part in parts))
    ours, theirs = both[:, :COLS], both[:, COLS:]
    final[0] = jnp.concatenate([theirs, jnp.zeros((1, 128 - COLS), F32)], axis=1)
    swap = remote(final.at[0], final.at[1], fin_send, fin_recv, sibling)
    swap.start()
    swap.wait_recv()
    theirs = final[1][:, :COLS]
    top = jnp.maximum(ours, theirs)
    score = top + jnp.log2(jnp.exp2(ours - top) + jnp.exp2(theirs - top))
    g_out[...] = pot_buf[...] - (EPS * LN2) * score + EPS * (
        math.log(float(CHIPS * NX * NC * ROWS)) - math.log(float(CHIPS * NX * NC * COLS))
    )

    gather_c.wait_send()
    swap.wait_send()


def per_device(gen_samples, data_samples, data_potential):
    hbm = pl.BlockSpec(memory_space=pltpu.HBM)
    vmem = pl.BlockSpec(memory_space=pltpu.VMEM)
    dma = pltpu.SemaphoreType.DMA
    f, g = pl.pallas_call(
        kernel,
        out_shape=(jax.ShapeDtypeStruct((1, ROWS), F32), jax.ShapeDtypeStruct((1, COLS), F32)),
        in_specs=[hbm, hbm, hbm],
        out_specs=(vmem, vmem),
        scratch_shapes=[
            pltpu.VMEM((NX, ROWS, WIDTH), BF16),
            pltpu.VMEM((1, COLS), F32),
            pltpu.VMEM((1, ROWS), F32),
            pltpu.VMEM((2 * CHIPS, COLS, WIDTH), BF16),
            pltpu.VMEM((2 * CHIPS, 1, 128), F32),
            pltpu.VMEM((2 * CHIPS, COLS, NX * ROWS), F32),
            pltpu.VMEM((8, NX * ROWS), F32),
            pltpu.VMEM((8, NX * ROWS), F32),
            pltpu.VMEM((NX, NX, 1, ROWS), F32),
            pltpu.VMEM((BATCH, 128), F32),
            pltpu.VMEM((BATCH, 128), F32),
            pltpu.VMEM((8, BATCH // 128, 1, 128), F32),
            pltpu.VMEM((2 * CHIPS, 1, 128), F32),
            pltpu.VMEM((2, 1, 128), F32),
            dma((3,)), dma((2,)), dma((2,)),
            dma((2, 2)), dma((2, 2)), dma((2, 5, 2)), dma((2, 5, 2)), dma((2, 11)), dma((2, 11)),
            dma, dma, dma, dma, dma, dma,
        ],
        compiler_params=pltpu.CompilerParams(
            collective_id=0, has_side_effects=True, vmem_limit_bytes=40 * 2**20
        ),
    )(*[
        pltpu.with_memory_space_constraint(array, pltpu.HBM)
        for array in (gen_samples, data_samples, data_potential.reshape(1, COLS))
    ])
    return f.reshape(ROWS), g.reshape(COLS)


def solution(mesh):
    in_specs = (P(("gen", "dat"), None), P(("dat", "gen"), None), P(("dat", "gen")))
    out_specs = (P(("gen", "dat")), P(("dat", "gen")))
    return jax.shard_map(
        per_device, mesh=mesh, in_specs=in_specs, out_specs=out_specs, check_vma=False
    )
```

```python
import math

import jax
import jax.numpy as jnp
from jax import lax
from jax.experimental import pallas as pl
from jax.experimental.pallas import tpu as pltpu
from jax.sharding import PartitionSpec as P

EPS = 0.05
LOG2E = math.log2(math.e)
LN2 = math.log(2.0)
SCALE = LOG2E / EPS
LOW = -1e30
MESH = pl.DeviceIdType.MESH
F32 = jnp.float32
BF16 = jnp.bfloat16

NX, NY, NZ, NC = 4, 8, 8, 2
CHIPS = NY * NZ
ROWS = 256
COLS = 24
WIDTH = 256
BATCH = 8 * NC * COLS
KEEP = 1.0 / WIDTH


def hops(d):
    return min(d % 8, -d % 8)


NEAR0 = [(0, 0), (0, 2), (0, -2), (2, 1), (2, -1), (-2, 1), (-2, -1), (0, 4)]
FAR0 = [(4, 0), (2, 3), (2, -3), (-2, 3), (-2, -3)]
NEAR2 = ([(0, 1), (2, 2), (-2, 2), (2, 0)], [(0, -1), (2, -2), (-2, -2), (-2, 0)])
FAR2 = ([(0, 3), (4, 1), (2, 4)], [(0, -3), (4, -1), (-2, 4)])


def shifted(offsets, dp, dq):
    return [(a + dp, b + dq) for a, b in offsets]


def folded(offset):
    return tuple((d + 3) % 8 - 3 for d in offset)


FIRST = NEAR0 + FAR0
ORDER = (
    FIRST
    + shifted(NEAR0, 1, 0) + shifted(NEAR0, -1, 0) + NEAR2[0] + NEAR2[1]
    + shifted(FAR0, 1, 0) + shifted(FAR0, -1, 0) + FAR2[0] + FAR2[1]
)
REST = sorted({folded((a, b)) for a in range(8) for b in range(8)} - {folded(o) for o in ORDER})
SLOT = {(a % 8, b % 8): slot for slot, (a, b) in enumerate(ORDER + REST)}


def holders(offsets):
    chosen = {}
    for offset in offsets:
        ways = [folded((offset[0] - a, offset[1] - b)) for a, b in FIRST]
        used = list(chosen.values())
        chosen[offset] = min(ways, key=lambda way: (abs(way[0]) + abs(way[1]), used.count(way), way))
    return chosen


HOLDER = holders(REST)
ALL = sorted((folded((a, b)) for a in range(8) for b in range(8)), key=lambda o: (-abs(o[0]) - abs(o[1]), o))
BATCHES = [ALL[i : i + 8] for i in range(0, 56, 8)] + [ALL[:55:-1]]


def slot_of(dp, dq):
    return SLOT[dp % 8, dq % 8]


def squares(values):
    wide = values.astype(F32)
    wide = wide * wide
    high = wide.astype(BF16)
    low = (wide - high.astype(F32)).astype(BF16)
    ones = jnp.ones((8, WIDTH), BF16)
    dims = (((1,), (1,)), ((), ()))
    return lax.dot_general(ones, high, dims, preferred_element_type=F32) + lax.dot_general(
        ones, low, dims, preferred_element_type=F32
    )


def kernel(
    gen_hbm, data_hbm, pot_hbm, f_out, g_out,
    x_buf, pot_buf, sq_buf, blocks, terms, stash, row_m, row_s, row_l,
    batch_a, batch_b, send_c, recv_c, final,
    local_sem, x_send, x_recv, one_send, one_recv, two_send, two_recv, sib_send, sib_recv,
    row_send, row_recv, col_send, col_recv, fin_send, fin_recv,
):
    gen = lax.axis_index("gen")
    dat = lax.axis_index("dat")
    x, c = (dat // 2) % NX, dat % 2
    y, z = (dat // 8) * 4 + gen % 4, gen // 4

    def device(x_, y_, z_, c_):
        return (z_ * 4 + y_ % 4, (y_ // 4) * 8 + x_ * 2 + c_)

    p, q = y + c * (z - y), z + c * (y - z)

    def in_plane(p_, q_):
        p_, q_ = p_ % 8, q_ % 8
        return device(x, p_ + c * (q_ - p_), q_ + c * (p_ - q_), c)

    sibling = device(x, y, z, 1 - c)
    x_peers = {d: device((x + d) % NX, y, z, c) for d in (1, 3, 2)}
    near = [in_plane(p + 1, q), in_plane(p - 1, q), in_plane(p, q + 1), in_plane(p, q - 1)]
    around = {(1, 0), (-1, 0), (0, 1), (0, -1)}
    others = sorted(({folded(o) for o in FIRST[1:]} | set(HOLDER.values())) - around, key=lambda o: -abs(o[0]) - abs(o[1]))
    group = [in_plane(p + dp, q + dq) for dp, dq in others]

    loads = [
        pltpu.make_async_copy(data_hbm, blocks.at[0], local_sem.at[0]),
        pltpu.make_async_copy(pot_hbm, pot_buf, local_sem.at[1]),
        pltpu.make_async_copy(gen_hbm, x_buf.at[0], local_sem.at[2]),
    ]
    for copy in loads:
        copy.start()

    peers = group + near + list(x_peers.values()) + [sibling]
    barrier = pltpu.get_barrier_semaphore()
    for peer in peers:
        pl.semaphore_signal(barrier, inc=1, device_id=peer, device_id_type=MESH)

    pl.semaphore_wait(barrier, len(peers))

    def remote(src, dst, send, recv, peer):
        return pltpu.make_async_remote_copy(
            src_ref=src, dst_ref=dst, send_sem=send, recv_sem=recv, device_id=peer, device_id_type=MESH
        )

    def to_group(i, ref, source):
        for dp, dq in reversed(FIRST[1:]):
            far = int((dp, dq) in FAR0)
            remote(
                source, ref.at[slot_of(dp, dq)], one_send.at[i, far], one_recv.at[i, far], in_plane(p - dp, q - dq)
            ).start()

    to_group(0, blocks, data_hbm)
    for d, peer in x_peers.items():
        remote(gen_hbm, x_buf.at[NX - d], x_send.at[int(d == 2)], x_recv.at[int(d == 2)], peer).start()

    for copy in loads[:2]:
        copy.wait()
    term = (pot_buf[...] - squares(blocks[0])[0:1, :] * KEEP) * SCALE
    terms[0] = jnp.concatenate([term, jnp.zeros((1, 128 - COLS), F32)], axis=1)
    to_group(1, terms, terms.at[0])

    row_m[...] = jnp.full(row_m.shape, LOW, F32)
    row_s[...] = jnp.zeros(row_s.shape, F32)
    loads[2].wait()
    sq_buf[...] = squares(x_buf[0])[0:1, :]

    refs = (blocks, terms)

    def from_group(far):
        return [
            remote(
                ref.at[pl.ds(0, (7, 5)[far])], ref.at[pl.ds(0, (7, 5)[far])],
                one_send.at[i, far], one_recv.at[i, far], sibling,
            )
            for i, ref in enumerate(refs)
        ]

    def to_near(k, far, count, src, dst, peer):
        return [
            remote(
                ref.at[pl.ds(src, count)], ref.at[pl.ds(dst, count)],
                two_send.at[i, k, far], two_recv.at[i, k, far], peer,
            )
            for i, ref in enumerate(refs)
        ]

    def send_near(i, far):
        count = (8, 5)[far]
        for k in range(2):
            to_near(k, far, count, 8 * far, (13, 37)[far] + k * count, near[1 - k])[i].start()
        for side, ways in enumerate((NEAR2, FAR2)[far]):
            for dp, dq in ways:
                held = slot_of(dp, dq + 2 * side - 1)
                to_near(2 + side, far, 1, held, slot_of(dp, dq), near[3 - side])[i].start()
        if far:
            for (dp, dq), (hp, hq) in HOLDER.items():
                to_near(4, far, 1, slot_of(dp - hp, dq - hq), slot_of(dp, dq), in_plane(p - hp, q - hq))[i].start()

    def from_near(k, far):
        return to_near(k, far, (8, 8, 4, 4, 0)[k] if not far else (5, 5, 3, 3, len(REST))[k], 0, 0, sibling)

    def to_sibling(k, start, count):
        return [
            remote(
                ref.at[pl.ds(start, count)], ref.at[pl.ds(CHIPS + start, count)],
                sib_send.at[i, k], sib_recv.at[i, k], sibling,
            )
            for i, ref in enumerate(refs)
        ]

    pieces = ((37, 5), (42, 5), (47, 3), (50, 3), (53, len(REST)))
    passed_on = [to_sibling(0, 0, 8), to_sibling(1, 8, 5)]
    near_on = [to_sibling(2 + k, *piece) for k, piece in enumerate(((13, 8), (21, 8), (29, 4), (33, 4)))]
    last_on = [to_sibling(6 + k, *piece) for k, piece in enumerate(pieces)]
    for far in range(2):
        for i in range(2):
            from_group(far)[i].wait_recv()
            send_near(i, far)
            passed_on[far][i].start()

    gather_x = [
        remote(x_buf.at[pl.ds(0, n)], x_buf.at[pl.ds(0, n)], x_send.at[i], x_recv.at[i], sibling)
        for i, n in enumerate((2, 1))
    ]
    gather_x[0].wait_recv()

    def row_unit(start, count, which=(0, 1, 2, 3)):
        cols = blocks[pl.ds(start, count)].astype(F32).reshape(count * COLS, WIDTH).astype(BF16)
        shape = (count, COLS, 128)
        on_diagonal = lax.broadcasted_iota(jnp.int32, shape, 2) == lax.broadcasted_iota(jnp.int32, shape, 1)
        spread = jnp.where(on_diagonal, jnp.broadcast_to(terms[pl.ds(start, count)], shape), 0.0)
        term_ = jnp.sum(spread, axis=2, keepdims=True).reshape(count * COLS, 1)
        for b in which:
            lanes = slice(b * ROWS, (b + 1) * ROWS)
            cross = lax.dot_general(cols, x_buf[b], (((1,), (1,)), ((), ())), preferred_element_type=F32)
            scores = cross * (2.0 * KEEP * SCALE) + term_
            stash[pl.ds(start, count), :, lanes] = scores.reshape(count, COLS, ROWS)
            parts = scores.reshape(count * COLS // 8, 8, ROWS)
            old = row_m[:, lanes]
            top = jnp.maximum(old, jnp.max(parts, axis=0))
            row_m[:, lanes] = top
            row_s[:, lanes] = row_s[:, lanes] * jnp.exp2(old - top) + jnp.sum(
                jnp.exp2(parts - top[None]), axis=0
            )

    def first_units(step, _):
        @pl.when(step == 1)
        def _():
            for copy in passed_on[0] + passed_on[1]:
                copy.wait_recv()

        row_unit(CHIPS * step, 13, (0, 1, 3))
        return 0

    def first_opposite(step, _):
        row_unit(CHIPS * step, 13, (2,))
        return 0

    lax.fori_loop(0, 2, first_units, 0)
    gather_x[1].wait_recv()
    lax.fori_loop(0, 2, first_opposite, 0)

    def next_units(step, _):
        @pl.when(step == 0)
        def _():
            for k in range(4):
                for copy in from_near(k, 0):
                    copy.wait_recv()
                for copy in near_on[k]:
                    copy.start()

        @pl.when(step == 1)
        def _():
            for copy in sum(near_on, []):
                copy.wait_recv()

        row_unit(13 + CHIPS * step, 24)
        return 0

    lax.fori_loop(0, 2, next_units, 0)

    def far_units(step, _):
        @pl.when(step == 0)
        def _():
            for k in range(4):
                for copy in from_near(k, 1):
                    copy.wait_recv()
                for copy in last_on[k]:
                    copy.start()

        @pl.when(step == 1)
        def _():
            for copy in from_near(4, 1):
                copy.wait_recv()
            for copy in last_on[4]:
                copy.start()
            for copy in sum(last_on[:4], []):
                copy.wait_recv()

        row_unit(37 + CHIPS * step, 16)
        return 0

    def rest_units(step, _):
        @pl.when(step == 1)
        def _():
            for copy in last_on[4]:
                copy.wait_recv()

        row_unit(53 + CHIPS * step, len(REST))
        return 0

    lax.fori_loop(0, 2, far_units, 0)
    lax.fori_loop(0, 2, rest_units, 0)

    def combined(values):
        top = jnp.max(values, axis=0)
        return top + jnp.log2(jnp.sum(jnp.exp2(values - top[None]), axis=0))

    m = row_m[...]
    top = jnp.max(m, axis=0, keepdims=True)
    total = jnp.sum(row_s[...] * jnp.exp2(m - top), axis=0, keepdims=True)
    local = top + jnp.log2(total)
    for b in range(NX):
        row_l[0, b] = local[:, b * ROWS : (b + 1) * ROWS]
    for d, peer in x_peers.items():
        for b in range(NX):
            remote(row_l.at[0, b], row_l.at[NX - d, (b - d) % NX], row_send, row_recv, peer).start()
    gather_l = remote(row_l.at[pl.ds(0, 3)], row_l.at[pl.ds(0, 3)], row_send, row_recv, sibling)
    gather_l.wait_recv()
    whole = combined(row_l[...])
    lifted = jnp.concatenate([jnp.broadcast_to(whole[b], (8, ROWS)) for b in range(NX)], axis=1)

    lane_tiles = NX * ROWS // 128

    def batch_parts(batch, batch_ref):
        for j, (dp, dq) in enumerate(batch):
            for h, at in enumerate((slot_of(dp, dq), CHIPS + slot_of(dq, dp))):
                scores = stash[at].reshape(COLS // 8, 8, NX * ROWS) - lifted[None]
                pieces = [scores[:, :, i * 128 : (i + 1) * 128] for i in range(lane_tiles)]
                peak = pieces[0]
                for piece in pieces[1:]:
                    peak = jnp.maximum(peak, piece)
                added = jnp.exp2(pieces[0] - peak)
                for piece in pieces[1:]:
                    added = added + jnp.exp2(piece - peak)
                to = (2 * j + h) * COLS
                batch_ref[to : to + COLS, :] = (peak + jnp.log2(added)).reshape(COLS, 128)

    def tiles_of(j):
        first = 2 * COLS * j // 128
        return first, (2 * COLS * (j + 1) - 1) // 128 - first + 1

    def batch_send(i, batch_ref):
        values = jnp.transpose(batch_ref[...])
        top = jnp.max(values, axis=0, keepdims=True)
        sums = top + jnp.log2(jnp.sum(jnp.exp2(values - top), axis=0, keepdims=True))
        for t in range(BATCH // 128):
            send_c[i, t] = sums[:, 128 * t : 128 * (t + 1)]
        for j, (dp, dq) in enumerate(BATCHES[i]):
            first, count = tiles_of(j)
            seen = 2 * (8 * j + i)
            if (dp, dq) == (0, 0):
                recv_c[seen] = sums[:, :128]
            else:
                remote(
                    send_c.at[i, pl.ds(first, count)], recv_c.at[pl.ds(seen, count)],
                    col_send, col_recv, in_plane(p + dp, q + dq),
                ).start()

    room = (batch_a, batch_b)
    batch_parts(BATCHES[0], room[0])
    for i in range(8):
        if i < 7:
            batch_parts(BATCHES[i + 1], room[(i + 1) % 2])
        batch_send(i, room[i % 2])

    f_out[...] = sq_buf[...] * KEEP - (EPS * LN2) * whole[0] + EPS * math.log(float(CHIPS * NX * NC * COLS))

    tiles = 8 * sum(tiles_of(j)[1] for j in range(8)) - 1
    gather_c = remote(recv_c.at[pl.ds(0, tiles)], recv_c.at[pl.ds(0, tiles)], col_send, col_recv, sibling)
    for copy in gather_x + [gather_l]:
        copy.wait_send()
    for far in range(2):
        for copy in from_group(far) + sum((from_near(k, far) for k in range(4 + far)), []):
            copy.wait_send()
    for copy in sum(passed_on + near_on + last_on, []):
        copy.wait_send()
    gather_c.wait_recv()

    parts = []
    for j in range(8):
        first, count = tiles_of(j)
        tiles = [
            combined(jnp.concatenate([recv_c[pl.ds(2 * (8 * j + i) + t, 1)] for i in range(8)], axis=0))
            for t in range(count)
        ]
        row = jnp.concatenate(tiles, axis=1)
        start = 2 * COLS * j - 128 * first
        parts.append(row[:, start : start + 2 * COLS])
    top = parts[0]
    for part in parts[1:]:
        top = jnp.maximum(top, part)
    both = top + jnp.log2(sum(jnp.exp2(part - top) for part in parts))
    ours, theirs = both[:, :COLS], both[:, COLS:]
    final[0] = jnp.concatenate([theirs, jnp.zeros((1, 128 - COLS), F32)], axis=1)
    swap = remote(final.at[0], final.at[1], fin_send, fin_recv, sibling)
    swap.start()
    swap.wait_recv()
    theirs = final[1][:, :COLS]
    top = jnp.maximum(ours, theirs)
    score = top + jnp.log2(jnp.exp2(ours - top) + jnp.exp2(theirs - top))
    g_out[...] = pot_buf[...] - (EPS * LN2) * score + EPS * (
        math.log(float(CHIPS * NX * NC * ROWS)) - math.log(float(CHIPS * NX * NC * COLS))
    )

    gather_c.wait_send()
    swap.wait_send()


def per_device(gen_samples, data_samples, data_potential):
    hbm = pl.BlockSpec(memory_space=pltpu.HBM)
    vmem = pl.BlockSpec(memory_space=pltpu.VMEM)
    dma = pltpu.SemaphoreType.DMA
    f, g = pl.pallas_call(
        kernel,
        out_shape=(jax.ShapeDtypeStruct((1, ROWS), F32), jax.ShapeDtypeStruct((1, COLS), F32)),
        in_specs=[hbm, hbm, hbm],
        out_specs=(vmem, vmem),
        scratch_shapes=[
            pltpu.VMEM((NX, ROWS, WIDTH), BF16),
            pltpu.VMEM((1, COLS), F32),
            pltpu.VMEM((1, ROWS), F32),
            pltpu.VMEM((2 * CHIPS, COLS, WIDTH), BF16),
            pltpu.VMEM((2 * CHIPS, 1, 128), F32),
            pltpu.VMEM((2 * CHIPS, COLS, NX * ROWS), F32),
            pltpu.VMEM((8, NX * ROWS), F32),
            pltpu.VMEM((8, NX * ROWS), F32),
            pltpu.VMEM((NX, NX, 1, ROWS), F32),
            pltpu.VMEM((BATCH, 128), F32),
            pltpu.VMEM((BATCH, 128), F32),
            pltpu.VMEM((8, BATCH // 128, 1, 128), F32),
            pltpu.VMEM((2 * CHIPS, 1, 128), F32),
            pltpu.VMEM((2, 1, 128), F32),
            dma((3,)), dma((2,)), dma((2,)),
            dma((2, 2)), dma((2, 2)), dma((2, 5, 2)), dma((2, 5, 2)), dma((2, 11)), dma((2, 11)),
            dma, dma, dma, dma, dma, dma,
        ],
        compiler_params=pltpu.CompilerParams(
            collective_id=0, has_side_effects=True, vmem_limit_bytes=40 * 2**20
        ),
    )(*[
        pltpu.with_memory_space_constraint(array, pltpu.HBM)
        for array in (gen_samples, data_samples, data_potential.reshape(1, COLS))
    ])
    return f.reshape(ROWS), g.reshape(COLS)


def solution(mesh):
    in_specs = (P(("gen", "dat"), None), P(("dat", "gen"), None), P(("dat", "gen")))
    out_specs = (P(("gen", "dat")), P(("dat", "gen")))
    return jax.shard_map(
        per_device, mesh=mesh, in_specs=in_specs, out_specs=out_specs, check_vma=False
    )
```

```python
import math

import jax
import jax.numpy as jnp
from jax import lax
from jax.experimental import pallas as pl
from jax.experimental.pallas import tpu as pltpu
from jax.sharding import PartitionSpec as P

EPS = 0.05
LOG2E = math.log2(math.e)
LN2 = math.log(2.0)
SCALE = LOG2E / EPS
LOW = -1e30
MESH = pl.DeviceIdType.MESH
F32 = jnp.float32
BF16 = jnp.bfloat16

NX, NY, NZ, NC = 4, 8, 8, 2
CHIPS = NY * NZ
ROWS = 256
COLS = 24
WIDTH = 256
BATCH = 8 * NC * COLS
KEEP = 1.0 / WIDTH


def hops(d):
    return min(d % 8, -d % 8)


NEAR0 = [(0, 0), (0, 2), (0, -2), (2, 1), (2, -1), (-2, 1), (-2, -1), (0, 4)]
FAR0 = [(4, 0), (2, 3), (2, -3), (-2, 3), (-2, -3), (4, 2), (4, -2)]
NEAR2 = ([(0, 1), (2, 2), (-2, 2), (2, 0)], [(0, -1), (2, -2), (-2, -2), (-2, 0)])
FAR2 = ([(0, 3), (4, 1), (4, 3), (2, 4)], [(0, -3), (4, -1), (4, -3), (-2, 4)])


def shifted(offsets, dp, dq):
    return [(a + dp, b + dq) for a, b in offsets]


def folded(offset):
    return tuple((d + 3) % 8 - 3 for d in offset)


FIRST = NEAR0 + FAR0
ORDER = (
    FIRST
    + shifted(NEAR0, 1, 0) + shifted(NEAR0, -1, 0) + NEAR2[0] + NEAR2[1]
    + shifted(FAR0, 1, 0) + shifted(FAR0, -1, 0) + FAR2[0] + FAR2[1]
)
REST = sorted({folded((a, b)) for a in range(8) for b in range(8)} - {folded(o) for o in ORDER})
SLOT = {(a % 8, b % 8): slot for slot, (a, b) in enumerate(ORDER + REST)}


def holders(offsets):
    chosen = {}
    for offset in offsets:
        ways = [folded((offset[0] - a, offset[1] - b)) for a, b in FIRST]
        used = list(chosen.values())
        chosen[offset] = min(ways, key=lambda way: (abs(way[0]) + abs(way[1]), used.count(way), way))
    return chosen


HOLDER = holders(REST)
ALL = sorted((folded((a, b)) for a in range(8) for b in range(8)), key=lambda o: (-abs(o[0]) - abs(o[1]), o))
BATCHES = [ALL[i : i + 8] for i in range(0, 56, 8)] + [ALL[:55:-1]]


def slot_of(dp, dq):
    return SLOT[dp % 8, dq % 8]


def squares(values):
    wide = values.astype(F32)
    wide = wide * wide
    high = wide.astype(BF16)
    low = (wide - high.astype(F32)).astype(BF16)
    ones = jnp.ones((8, WIDTH), BF16)
    dims = (((1,), (1,)), ((), ()))
    return lax.dot_general(ones, high, dims, preferred_element_type=F32) + lax.dot_general(
        ones, low, dims, preferred_element_type=F32
    )


def kernel(
    gen_hbm, data_hbm, pot_hbm, f_out, g_out,
    x_buf, pot_buf, sq_buf, blocks, terms, stash, row_m, row_s, row_l,
    batch_a, batch_b, send_c, recv_c, final,
    local_sem, x_send, x_recv, one_send, one_recv, two_send, two_recv, sib_send, sib_recv,
    row_send, row_recv, col_send, col_recv, fin_send, fin_recv,
):
    gen = lax.axis_index("gen")
    dat = lax.axis_index("dat")
    x, c = (dat // 2) % NX, dat % 2
    y, z = (dat // 8) * 4 + gen % 4, gen // 4

    def device(x_, y_, z_, c_):
        return (z_ * 4 + y_ % 4, (y_ // 4) * 8 + x_ * 2 + c_)

    p, q = y + c * (z - y), z + c * (y - z)

    def in_plane(p_, q_):
        p_, q_ = p_ % 8, q_ % 8
        return device(x, p_ + c * (q_ - p_), q_ + c * (p_ - q_), c)

    sibling = device(x, y, z, 1 - c)
    x_peers = {d: device((x + d) % NX, y, z, c) for d in (1, 3, 2)}
    near = [in_plane(p + 1, q), in_plane(p - 1, q), in_plane(p, q + 1), in_plane(p, q - 1)]
    around = {(1, 0), (-1, 0), (0, 1), (0, -1)}
    others = sorted(({folded(o) for o in FIRST[1:]} | set(HOLDER.values())) - around, key=lambda o: -abs(o[0]) - abs(o[1]))
    group = [in_plane(p + dp, q + dq) for dp, dq in others]

    loads = [
        pltpu.make_async_copy(data_hbm, blocks.at[0], local_sem.at[0]),
        pltpu.make_async_copy(pot_hbm, pot_buf, local_sem.at[1]),
        pltpu.make_async_copy(gen_hbm, x_buf.at[0], local_sem.at[2]),
    ]
    for copy in loads:
        copy.start()

    peers = group + near + list(x_peers.values()) + [sibling]
    barrier = pltpu.get_barrier_semaphore()
    for peer in peers:
        pl.semaphore_signal(barrier, inc=1, device_id=peer, device_id_type=MESH)

    pl.semaphore_wait(barrier, len(peers))

    def remote(src, dst, send, recv, peer):
        return pltpu.make_async_remote_copy(
            src_ref=src, dst_ref=dst, send_sem=send, recv_sem=recv, device_id=peer, device_id_type=MESH
        )

    def to_group(i, ref, source):
        for dp, dq in reversed(FIRST[1:]):
            far = int((dp, dq) in FAR0)
            remote(
                source, ref.at[slot_of(dp, dq)], one_send.at[i, far], one_recv.at[i, far], in_plane(p - dp, q - dq)
            ).start()

    to_group(0, blocks, data_hbm)
    for d, peer in x_peers.items():
        remote(gen_hbm, x_buf.at[NX - d], x_send.at[int(d == 2)], x_recv.at[int(d == 2)], peer).start()

    for copy in loads[:2]:
        copy.wait()
    term = (pot_buf[...] - squares(blocks[0])[0:1, :] * KEEP) * SCALE
    terms[0] = jnp.concatenate([term, jnp.zeros((1, 128 - COLS), F32)], axis=1)
    to_group(1, terms, terms.at[0])

    row_m[...] = jnp.full(row_m.shape, LOW, F32)
    row_s[...] = jnp.zeros(row_s.shape, F32)
    loads[2].wait()
    sq_buf[...] = squares(x_buf[0])[0:1, :]

    refs = (blocks, terms)

    def from_group(far):
        return [
            remote(
                ref.at[pl.ds(0, (7, 7)[far])], ref.at[pl.ds(0, (7, 7)[far])],
                one_send.at[i, far], one_recv.at[i, far], sibling,
            )
            for i, ref in enumerate(refs)
        ]

    def to_near(k, far, count, src, dst, peer):
        return [
            remote(
                ref.at[pl.ds(src, count)], ref.at[pl.ds(dst, count)],
                two_send.at[i, k, far], two_recv.at[i, k, far], peer,
            )
            for i, ref in enumerate(refs)
        ]

    def send_near(i, far):
        count = (8, 7)[far]
        for k in range(2):
            to_near(k, far, count, 8 * far, (15, 39)[far] + k * count, near[1 - k])[i].start()
        for side, ways in enumerate((NEAR2, FAR2)[far]):
            for dp, dq in ways:
                held = slot_of(dp, dq + 2 * side - 1)
                to_near(2 + side, far, 1, held, slot_of(dp, dq), near[3 - side])[i].start()
        if far:
            for (dp, dq), (hp, hq) in HOLDER.items():
                to_near(4, far, 1, slot_of(dp - hp, dq - hq), slot_of(dp, dq), in_plane(p - hp, q - hq))[i].start()

    def from_near(k, far):
        return to_near(k, far, (8, 8, 4, 4, 0)[k] if not far else (7, 7, 4, 4, len(REST))[k], 0, 0, sibling)

    def to_sibling(k, start, count):
        return [
            remote(
                ref.at[pl.ds(start, count)], ref.at[pl.ds(CHIPS + start, count)],
                sib_send.at[i, k], sib_recv.at[i, k], sibling,
            )
            for i, ref in enumerate(refs)
        ]

    pieces = ((39, 7), (46, 7), (53, 4), (57, 4), (61, len(REST)))
    passed_on = [to_sibling(0, 0, 8), to_sibling(1, 8, 7), to_sibling(2, 15, 24)]
    last_on = [to_sibling(3 + k, *piece) for k, piece in enumerate(pieces)]
    for far in range(2):
        for i in range(2):
            from_group(far)[i].wait_recv()
            send_near(i, far)
            passed_on[far][i].start()

    gather_x = [
        remote(x_buf.at[pl.ds(0, n)], x_buf.at[pl.ds(0, n)], x_send.at[i], x_recv.at[i], sibling)
        for i, n in enumerate((2, 1))
    ]
    gather_x[0].wait_recv()

    def row_unit(start, count, which=(0, 1, 2, 3)):
        cols = blocks[pl.ds(start, count)].astype(F32).reshape(count * COLS, WIDTH).astype(BF16)
        shape = (count, COLS, 128)
        on_diagonal = lax.broadcasted_iota(jnp.int32, shape, 2) == lax.broadcasted_iota(jnp.int32, shape, 1)
        spread = jnp.where(on_diagonal, jnp.broadcast_to(terms[pl.ds(start, count)], shape), 0.0)
        term_ = jnp.sum(spread, axis=2, keepdims=True).reshape(count * COLS, 1)
        for b in which:
            lanes = slice(b * ROWS, (b + 1) * ROWS)
            cross = lax.dot_general(cols, x_buf[b], (((1,), (1,)), ((), ())), preferred_element_type=F32)
            scores = cross * (2.0 * KEEP * SCALE) + term_
            stash[pl.ds(start, count), :, lanes] = scores.reshape(count, COLS, ROWS)
            parts = scores.reshape(count * COLS // 8, 8, ROWS)
            old = row_m[:, lanes]
            top = jnp.maximum(old, jnp.max(parts, axis=0))
            row_m[:, lanes] = top
            row_s[:, lanes] = row_s[:, lanes] * jnp.exp2(old - top) + jnp.sum(
                jnp.exp2(parts - top[None]), axis=0
            )

    def first_units(step, _):
        @pl.when(step == 1)
        def _():
            for k in range(4):
                for copy in from_near(k, 0):
                    copy.wait_recv()
            for copy in passed_on[2]:
                copy.start()
            for copy in passed_on[0] + passed_on[1]:
                copy.wait_recv()

        row_unit(CHIPS * step, 15, (0, 1, 3))
        return 0

    def first_opposite(step, _):
        row_unit(CHIPS * step, 15, (2,))
        return 0

    lax.fori_loop(0, 2, first_units, 0)
    gather_x[1].wait_recv()
    lax.fori_loop(0, 2, first_opposite, 0)

    def next_units(step, _):
        @pl.when(step == 1)
        def _():
            for copy in passed_on[2]:
                copy.wait_recv()

        row_unit(15 + CHIPS * step, 24)
        return 0

    lax.fori_loop(0, 2, next_units, 0)

    def last_units(step, _):
        @pl.when(step == 0)
        def _():
            for k in range(5):
                for copy in from_near(k, 1):
                    copy.wait_recv()
                for copy in last_on[k]:
                    copy.start()

        @pl.when(step == 1)
        def _():
            for copy in sum(last_on, []):
                copy.wait_recv()

        row_unit(39 + CHIPS * step, 25)
        return 0

    lax.fori_loop(0, 2, last_units, 0)

    def combined(values):
        top = jnp.max(values, axis=0)
        return top + jnp.log2(jnp.sum(jnp.exp2(values - top[None]), axis=0))

    m = row_m[...]
    top = jnp.max(m, axis=0, keepdims=True)
    total = jnp.sum(row_s[...] * jnp.exp2(m - top), axis=0, keepdims=True)
    local = top + jnp.log2(total)
    for b in range(NX):
        row_l[0, b] = local[:, b * ROWS : (b + 1) * ROWS]
    for d, peer in x_peers.items():
        for b in range(NX):
            remote(row_l.at[0, b], row_l.at[NX - d, (b - d) % NX], row_send, row_recv, peer).start()
    gather_l = remote(row_l.at[pl.ds(0, 3)], row_l.at[pl.ds(0, 3)], row_send, row_recv, sibling)
    gather_l.wait_recv()
    whole = combined(row_l[...])
    lifted = jnp.concatenate([jnp.broadcast_to(whole[b], (8, ROWS)) for b in range(NX)], axis=1)

    lane_tiles = NX * ROWS // 128

    def batch_parts(batch, batch_ref):
        for j, (dp, dq) in enumerate(batch):
            for h, at in enumerate((slot_of(dp, dq), CHIPS + slot_of(dq, dp))):
                scores = stash[at].reshape(COLS // 8, 8, NX * ROWS) - lifted[None]
                pieces = [scores[:, :, i * 128 : (i + 1) * 128] for i in range(lane_tiles)]
                peak = pieces[0]
                for piece in pieces[1:]:
                    peak = jnp.maximum(peak, piece)
                added = jnp.exp2(pieces[0] - peak)
                for piece in pieces[1:]:
                    added = added + jnp.exp2(piece - peak)
                to = (2 * j + h) * COLS
                batch_ref[to : to + COLS, :] = (peak + jnp.log2(added)).reshape(COLS, 128)

    def tiles_of(j):
        first = 2 * COLS * j // 128
        return first, (2 * COLS * (j + 1) - 1) // 128 - first + 1

    def batch_send(i, batch_ref):
        values = jnp.transpose(batch_ref[...])
        top = jnp.max(values, axis=0, keepdims=True)
        sums = top + jnp.log2(jnp.sum(jnp.exp2(values - top), axis=0, keepdims=True))
        for t in range(BATCH // 128):
            send_c[i, t] = sums[:, 128 * t : 128 * (t + 1)]
        for j, (dp, dq) in enumerate(BATCHES[i]):
            first, count = tiles_of(j)
            seen = 2 * (8 * j + i)
            if (dp, dq) == (0, 0):
                recv_c[seen] = sums[:, :128]
            else:
                remote(
                    send_c.at[i, pl.ds(first, count)], recv_c.at[pl.ds(seen, count)],
                    col_send, col_recv, in_plane(p + dp, q + dq),
                ).start()

    room = (batch_a, batch_b)
    batch_parts(BATCHES[0], room[0])
    for i in range(8):
        if i < 7:
            batch_parts(BATCHES[i + 1], room[(i + 1) % 2])
        batch_send(i, room[i % 2])

    f_out[...] = sq_buf[...] * KEEP - (EPS * LN2) * whole[0] + EPS * math.log(float(CHIPS * NX * NC * COLS))

    tiles = 8 * sum(tiles_of(j)[1] for j in range(8)) - 1
    gather_c = remote(recv_c.at[pl.ds(0, tiles)], recv_c.at[pl.ds(0, tiles)], col_send, col_recv, sibling)
    for copy in gather_x + [gather_l]:
        copy.wait_send()
    for far in range(2):
        for copy in from_group(far) + sum((from_near(k, far) for k in range(4 + far)), []):
            copy.wait_send()
    for copy in sum(passed_on + last_on, []):
        copy.wait_send()
    gather_c.wait_recv()

    parts = []
    for j in range(8):
        first, count = tiles_of(j)
        tiles = [
            combined(jnp.concatenate([recv_c[pl.ds(2 * (8 * j + i) + t, 1)] for i in range(8)], axis=0))
            for t in range(count)
        ]
        row = jnp.concatenate(tiles, axis=1)
        start = 2 * COLS * j - 128 * first
        parts.append(row[:, start : start + 2 * COLS])
    top = parts[0]
    for part in parts[1:]:
        top = jnp.maximum(top, part)
    both = top + jnp.log2(sum(jnp.exp2(part - top) for part in parts))
    ours, theirs = both[:, :COLS], both[:, COLS:]
    final[0] = jnp.concatenate([theirs, jnp.zeros((1, 128 - COLS), F32)], axis=1)
    swap = remote(final.at[0], final.at[1], fin_send, fin_recv, sibling)
    swap.start()
    swap.wait_recv()
    theirs = final[1][:, :COLS]
    top = jnp.maximum(ours, theirs)
    score = top + jnp.log2(jnp.exp2(ours - top) + jnp.exp2(theirs - top))
    g_out[...] = pot_buf[...] - (EPS * LN2) * score + EPS * (
        math.log(float(CHIPS * NX * NC * ROWS)) - math.log(float(CHIPS * NX * NC * COLS))
    )

    gather_c.wait_send()
    swap.wait_send()


def per_device(gen_samples, data_samples, data_potential):
    hbm = pl.BlockSpec(memory_space=pltpu.HBM)
    vmem = pl.BlockSpec(memory_space=pltpu.VMEM)
    dma = pltpu.SemaphoreType.DMA
    f, g = pl.pallas_call(
        kernel,
        out_shape=(jax.ShapeDtypeStruct((1, ROWS), F32), jax.ShapeDtypeStruct((1, COLS), F32)),
        in_specs=[hbm, hbm, hbm],
        out_specs=(vmem, vmem),
        scratch_shapes=[
            pltpu.VMEM((NX, ROWS, WIDTH), BF16),
            pltpu.VMEM((1, COLS), F32),
            pltpu.VMEM((1, ROWS), F32),
            pltpu.VMEM((2 * CHIPS, COLS, WIDTH), BF16),
            pltpu.VMEM((2 * CHIPS, 1, 128), F32),
            pltpu.VMEM((2 * CHIPS, COLS, NX * ROWS), F32),
            pltpu.VMEM((8, NX * ROWS), F32),
            pltpu.VMEM((8, NX * ROWS), F32),
            pltpu.VMEM((NX, NX, 1, ROWS), F32),
            pltpu.VMEM((BATCH, 128), F32),
            pltpu.VMEM((BATCH, 128), F32),
            pltpu.VMEM((8, BATCH // 128, 1, 128), F32),
            pltpu.VMEM((2 * CHIPS, 1, 128), F32),
            pltpu.VMEM((2, 1, 128), F32),
            dma((3,)), dma((2,)), dma((2,)),
            dma((2, 2)), dma((2, 2)), dma((2, 5, 2)), dma((2, 5, 2)), dma((2, 8)), dma((2, 8)),
            dma, dma, dma, dma, dma, dma,
        ],
        compiler_params=pltpu.CompilerParams(
            collective_id=0, has_side_effects=True, vmem_limit_bytes=40 * 2**20
        ),
    )(*[
        pltpu.with_memory_space_constraint(array, pltpu.HBM)
        for array in (gen_samples, data_samples, data_potential.reshape(1, COLS))
    ])
    return f.reshape(ROWS), g.reshape(COLS)


def solution(mesh):
    in_specs = (P(("gen", "dat"), None), P(("dat", "gen"), None), P(("dat", "gen")))
    out_specs = (P(("gen", "dat")), P(("dat", "gen")))
    return jax.shard_map(
        per_device, mesh=mesh, in_specs=in_specs, out_specs=out_specs, check_vma=False
    )
```

```python
import math

import jax
import jax.numpy as jnp
from jax import lax
from jax.experimental import pallas as pl
from jax.experimental.pallas import tpu as pltpu
from jax.sharding import PartitionSpec as P

EPS = 0.05
LOG2E = math.log2(math.e)
LN2 = math.log(2.0)
SCALE = LOG2E / EPS
LOW = -1e30
MESH = pl.DeviceIdType.MESH
F32 = jnp.float32
BF16 = jnp.bfloat16

NX, NY, NZ, NC = 4, 8, 8, 2
CHIPS = NY * NZ
ROWS = 256
COLS = 24
WIDTH = 256
BATCH = 8 * NC * COLS
KEEP = 1.0 / WIDTH


def hops(d):
    return min(d % 8, -d % 8)


NEAR0 = [(0, 0), (0, 2), (0, -2), (2, 1), (2, -1), (-2, 1), (-2, -1), (0, 4)]
FAR0 = [(4, 0), (2, 3), (2, -3), (-2, 3), (-2, -3)]
NEAR2 = ([(0, 1), (2, 2), (-2, 2), (2, 0)], [(0, -1), (2, -2), (-2, -2), (-2, 0)])
FAR2 = ([(0, 3), (4, 1), (2, 4)], [(0, -3), (4, -1), (-2, 4)])


def shifted(offsets, dp, dq):
    return [(a + dp, b + dq) for a, b in offsets]


def folded(offset):
    return tuple((d + 3) % 8 - 3 for d in offset)


FIRST = NEAR0 + FAR0
ORDER = (
    FIRST
    + shifted(NEAR0, 1, 0) + shifted(NEAR0, -1, 0) + NEAR2[0] + NEAR2[1]
    + shifted(FAR0, 1, 0) + shifted(FAR0, -1, 0) + FAR2[0] + FAR2[1]
)
REST = sorted({folded((a, b)) for a in range(8) for b in range(8)} - {folded(o) for o in ORDER})
SLOT = {(a % 8, b % 8): slot for slot, (a, b) in enumerate(ORDER + REST)}


def holders(offsets):
    chosen = {}
    for offset in offsets:
        ways = [folded((offset[0] - a, offset[1] - b)) for a, b in FIRST]
        used = list(chosen.values())
        chosen[offset] = min(ways, key=lambda way: (abs(way[0]) + abs(way[1]), used.count(way), way))
    return chosen


HOLDER = holders(REST)
ALL = sorted((folded((a, b)) for a in range(8) for b in range(8)), key=lambda o: (-abs(o[0]) - abs(o[1]), o))
BATCHES = [ALL[i : i + 8] for i in range(0, 56, 8)] + [ALL[:55:-1]]


def slot_of(dp, dq):
    return SLOT[dp % 8, dq % 8]


def squares(values):
    wide = values.astype(F32)
    wide = wide * wide
    high = wide.astype(BF16)
    low = (wide - high.astype(F32)).astype(BF16)
    ones = jnp.ones((8, WIDTH), BF16)
    dims = (((1,), (1,)), ((), ()))
    return lax.dot_general(ones, high, dims, preferred_element_type=F32) + lax.dot_general(
        ones, low, dims, preferred_element_type=F32
    )


def kernel(
    gen_hbm, data_hbm, pot_hbm, f_out, g_out,
    x_buf, pot_buf, sq_buf, blocks, terms, stash, row_m, row_s, row_l,
    batch_a, batch_b, send_c, recv_c, final,
    local_sem, x_send, x_recv, one_send, one_recv, two_send, two_recv, sib_send, sib_recv,
    row_send, row_recv, col_send, col_recv, fin_send, fin_recv,
):
    gen = lax.axis_index("gen")
    dat = lax.axis_index("dat")
    x, c = (dat // 2) % NX, dat % 2
    y, z = (dat // 8) * 4 + gen % 4, gen // 4

    def device(x_, y_, z_, c_):
        return (z_ * 4 + y_ % 4, (y_ // 4) * 8 + x_ * 2 + c_)

    p, q = y + c * (z - y), z + c * (y - z)

    def in_plane(p_, q_):
        p_, q_ = p_ % 8, q_ % 8
        return device(x, p_ + c * (q_ - p_), q_ + c * (p_ - q_), c)

    sibling = device(x, y, z, 1 - c)
    x_peers = {d: device((x + d) % NX, y, z, c) for d in (1, 3, 2)}
    near = [in_plane(p + 1, q), in_plane(p - 1, q), in_plane(p, q + 1), in_plane(p, q - 1)]
    around = {(1, 0), (-1, 0), (0, 1), (0, -1)}
    others = sorted(({folded(o) for o in FIRST[1:]} | set(HOLDER.values())) - around, key=lambda o: -abs(o[0]) - abs(o[1]))
    group = [in_plane(p + dp, q + dq) for dp, dq in others]

    loads = [
        pltpu.make_async_copy(data_hbm, blocks.at[0], local_sem.at[0]),
        pltpu.make_async_copy(pot_hbm, pot_buf, local_sem.at[1]),
        pltpu.make_async_copy(gen_hbm, x_buf.at[0], local_sem.at[2]),
    ]
    for copy in loads:
        copy.start()

    peers = group + near + list(x_peers.values()) + [sibling]
    barrier = pltpu.get_barrier_semaphore()
    for peer in peers:
        pl.semaphore_signal(barrier, inc=1, device_id=peer, device_id_type=MESH)

    pl.semaphore_wait(barrier, len(peers))

    def remote(src, dst, send, recv, peer):
        return pltpu.make_async_remote_copy(
            src_ref=src, dst_ref=dst, send_sem=send, recv_sem=recv, device_id=peer, device_id_type=MESH
        )

    def to_group(i, ref, source):
        for dp, dq in reversed(FIRST[1:]):
            far = int((dp, dq) in FAR0)
            remote(
                source, ref.at[slot_of(dp, dq)], one_send.at[i, far], one_recv.at[i, far], in_plane(p - dp, q - dq)
            ).start()

    to_group(0, blocks, data_hbm)
    for d, peer in x_peers.items():
        remote(gen_hbm, x_buf.at[NX - d], x_send.at[int(d == 2)], x_recv.at[int(d == 2)], peer).start()

    for copy in loads[:2]:
        copy.wait()
    term = (pot_buf[...] - squares(blocks[0])[0:1, :] * KEEP) * SCALE
    terms[0] = jnp.concatenate([term, jnp.zeros((1, 128 - COLS), F32)], axis=1)
    to_group(1, terms, terms.at[0])

    row_m[...] = jnp.full(row_m.shape, LOW, F32)
    row_s[...] = jnp.zeros(row_s.shape, F32)
    loads[2].wait()
    sq_buf[...] = squares(x_buf[0])[0:1, :]

    refs = (blocks, terms)

    def from_group(far):
        return [
            remote(
                ref.at[pl.ds(0, (7, 5)[far])], ref.at[pl.ds(0, (7, 5)[far])],
                one_send.at[i, far], one_recv.at[i, far], sibling,
            )
            for i, ref in enumerate(refs)
        ]

    def to_near(k, far, count, src, dst, peer):
        return [
            remote(
                ref.at[pl.ds(src, count)], ref.at[pl.ds(dst, count)],
                two_send.at[i, k, far], two_recv.at[i, k, far], peer,
            )
            for i, ref in enumerate(refs)
        ]

    def send_near(i, far):
        count = (8, 5)[far]
        for k in range(2):
            to_near(k, far, count, 8 * far, (13, 37)[far] + k * count, near[1 - k])[i].start()
        for side, ways in enumerate((NEAR2, FAR2)[far]):
            for dp, dq in ways:
                held = slot_of(dp, dq + 2 * side - 1)
                to_near(2 + side, far, 1, held, slot_of(dp, dq), near[3 - side])[i].start()
        if far:
            for (dp, dq), (hp, hq) in HOLDER.items():
                to_near(4, far, 1, slot_of(dp - hp, dq - hq), slot_of(dp, dq), in_plane(p - hp, q - hq))[i].start()

    def from_near(k, far):
        return to_near(k, far, (8, 8, 4, 4, 0)[k] if not far else (5, 5, 3, 3, len(REST))[k], 0, 0, sibling)

    def to_sibling(k, start, count):
        return [
            remote(
                ref.at[pl.ds(start, count)], ref.at[pl.ds(CHIPS + start, count)],
                sib_send.at[i, k], sib_recv.at[i, k], sibling,
            )
            for i, ref in enumerate(refs)
        ]

    pieces = ((37, 5), (42, 5), (47, 3), (50, 3), (53, len(REST)))
    passed_on = [to_sibling(0, 0, 8), to_sibling(1, 8, 5), to_sibling(2, 13, 24)]
    last_on = [to_sibling(3 + k, *piece) for k, piece in enumerate(pieces)]
    for far in range(2):
        for i in range(2):
            from_group(far)[i].wait_recv()
            send_near(i, far)
            passed_on[far][i].start()

    gather_x = [
        remote(x_buf.at[pl.ds(0, n)], x_buf.at[pl.ds(0, n)], x_send.at[i], x_recv.at[i], sibling)
        for i, n in enumerate((2, 1))
    ]
    gather_x[0].wait_recv()

    def row_unit(start, count, which=(0, 1, 2, 3)):
        cols = blocks[pl.ds(start, count)].astype(F32).reshape(count * COLS, WIDTH).astype(BF16)
        shape = (count, COLS, 128)
        on_diagonal = lax.broadcasted_iota(jnp.int32, shape, 2) == lax.broadcasted_iota(jnp.int32, shape, 1)
        spread = jnp.where(on_diagonal, jnp.broadcast_to(terms[pl.ds(start, count)], shape), 0.0)
        term_ = jnp.sum(spread, axis=2, keepdims=True).reshape(count * COLS, 1)
        for b in which:
            lanes = slice(b * ROWS, (b + 1) * ROWS)
            cross = lax.dot_general(cols, x_buf[b], (((1,), (1,)), ((), ())), preferred_element_type=F32)
            scores = cross * (2.0 * KEEP * SCALE) + term_
            stash[pl.ds(start, count), :, lanes] = scores.reshape(count, COLS, ROWS)
            parts = scores.reshape(count * COLS // 8, 8, ROWS)
            old = row_m[:, lanes]
            top = jnp.maximum(old, jnp.max(parts, axis=0))
            row_m[:, lanes] = top
            row_s[:, lanes] = row_s[:, lanes] * jnp.exp2(old - top) + jnp.sum(
                jnp.exp2(parts - top[None]), axis=0
            )

    def first_units(step, _):
        @pl.when(step == 1)
        def _():
            for k in range(4):
                for copy in from_near(k, 0):
                    copy.wait_recv()
            for copy in passed_on[2]:
                copy.start()
            for copy in passed_on[0] + passed_on[1]:
                copy.wait_recv()

        row_unit(CHIPS * step, 13, (0, 1, 3))
        return 0

    def first_opposite(step, _):
        row_unit(CHIPS * step, 13, (2,))
        return 0

    lax.fori_loop(0, 2, first_units, 0)
    gather_x[1].wait_recv()
    lax.fori_loop(0, 2, first_opposite, 0)

    def next_units(step, _):
        @pl.when(step == 1)
        def _():
            for copy in passed_on[2]:
                copy.wait_recv()

        row_unit(13 + CHIPS * step, 24)
        return 0

    lax.fori_loop(0, 2, next_units, 0)

    def last_units(step, _):
        @pl.when(step == 0)
        def _():
            for k in range(5):
                for copy in from_near(k, 1):
                    copy.wait_recv()
                for copy in last_on[k]:
                    copy.start()

        @pl.when(step == 1)
        def _():
            for copy in sum(last_on, []):
                copy.wait_recv()

        row_unit(37 + CHIPS * step, 27)
        return 0

    lax.fori_loop(0, 2, last_units, 0)

    def combined(values):
        top = jnp.max(values, axis=0)
        return top + jnp.log2(jnp.sum(jnp.exp2(values - top[None]), axis=0))

    m = row_m[...]
    top = jnp.max(m, axis=0, keepdims=True)
    total = jnp.sum(row_s[...] * jnp.exp2(m - top), axis=0, keepdims=True)
    local = top + jnp.log2(total)
    for b in range(NX):
        row_l[0, b] = local[:, b * ROWS : (b + 1) * ROWS]
    for d, peer in x_peers.items():
        for b in range(NX):
            remote(row_l.at[0, b], row_l.at[NX - d, (b - d) % NX], row_send, row_recv, peer).start()
    gather_l = remote(row_l.at[pl.ds(0, 3)], row_l.at[pl.ds(0, 3)], row_send, row_recv, sibling)
    gather_l.wait_recv()
    whole = combined(row_l[...])
    lifted = jnp.concatenate([jnp.broadcast_to(whole[b], (8, ROWS)) for b in range(NX)], axis=1)

    lane_tiles = NX * ROWS // 128

    def batch_parts(batch, batch_ref):
        for j, (dp, dq) in enumerate(batch):
            for h, at in enumerate((slot_of(dp, dq), CHIPS + slot_of(dq, dp))):
                scores = stash[at].reshape(COLS // 8, 8, NX * ROWS) - lifted[None]
                pieces = [scores[:, :, i * 128 : (i + 1) * 128] for i in range(lane_tiles)]
                peak = pieces[0]
                for piece in pieces[1:]:
                    peak = jnp.maximum(peak, piece)
                added = jnp.exp2(pieces[0] - peak)
                for piece in pieces[1:]:
                    added = added + jnp.exp2(piece - peak)
                to = (2 * j + h) * COLS
                batch_ref[to : to + COLS, :] = (peak + jnp.log2(added)).reshape(COLS, 128)

    def tiles_of(j):
        first = 2 * COLS * j // 128
        return first, (2 * COLS * (j + 1) - 1) // 128 - first + 1

    def batch_send(i, batch_ref):
        values = jnp.transpose(batch_ref[...])
        top = jnp.max(values, axis=0, keepdims=True)
        sums = top + jnp.log2(jnp.sum(jnp.exp2(values - top), axis=0, keepdims=True))
        for t in range(BATCH // 128):
            send_c[i, t] = sums[:, 128 * t : 128 * (t + 1)]
        for j, (dp, dq) in enumerate(BATCHES[i]):
            first, count = tiles_of(j)
            seen = 2 * (8 * j + i)
            if (dp, dq) == (0, 0):
                recv_c[seen] = sums[:, :128]
            else:
                remote(
                    send_c.at[i, pl.ds(first, count)], recv_c.at[pl.ds(seen, count)],
                    col_send, col_recv, in_plane(p + dp, q + dq),
                ).start()

    room = (batch_a, batch_b)
    batch_parts(BATCHES[0], room[0])
    batch_send(0, room[0])
    batch_parts(BATCHES[1], room[1])
    for i in range(1, 8):
        if i < 7:
            batch_parts(BATCHES[i + 1], room[(i + 1) % 2])
        batch_send(i, room[i % 2])

    f_out[...] = sq_buf[...] * KEEP - (EPS * LN2) * whole[0] + EPS * math.log(float(CHIPS * NX * NC * COLS))

    tiles = 8 * sum(tiles_of(j)[1] for j in range(8)) - 1
    gather_c = remote(recv_c.at[pl.ds(0, tiles)], recv_c.at[pl.ds(0, tiles)], col_send, col_recv, sibling)
    for copy in gather_x + [gather_l]:
        copy.wait_send()
    for far in range(2):
        for copy in from_group(far) + sum((from_near(k, far) for k in range(4 + far)), []):
            copy.wait_send()
    for copy in sum(passed_on + last_on, []):
        copy.wait_send()
    gather_c.wait_recv()

    parts = []
    for j in range(8):
        first, count = tiles_of(j)
        tiles = [
            combined(jnp.concatenate([recv_c[pl.ds(2 * (8 * j + i) + t, 1)] for i in range(8)], axis=0))
            for t in range(count)
        ]
        row = jnp.concatenate(tiles, axis=1)
        start = 2 * COLS * j - 128 * first
        parts.append(row[:, start : start + 2 * COLS])
    top = parts[0]
    for part in parts[1:]:
        top = jnp.maximum(top, part)
    both = top + jnp.log2(sum(jnp.exp2(part - top) for part in parts))
    ours, theirs = both[:, :COLS], both[:, COLS:]
    final[0] = jnp.concatenate([theirs, jnp.zeros((1, 128 - COLS), F32)], axis=1)
    swap = remote(final.at[0], final.at[1], fin_send, fin_recv, sibling)
    swap.start()
    swap.wait_recv()
    theirs = final[1][:, :COLS]
    top = jnp.maximum(ours, theirs)
    score = top + jnp.log2(jnp.exp2(ours - top) + jnp.exp2(theirs - top))
    g_out[...] = pot_buf[...] - (EPS * LN2) * score + EPS * (
        math.log(float(CHIPS * NX * NC * ROWS)) - math.log(float(CHIPS * NX * NC * COLS))
    )

    gather_c.wait_send()
    swap.wait_send()


def per_device(gen_samples, data_samples, data_potential):
    hbm = pl.BlockSpec(memory_space=pltpu.HBM)
    vmem = pl.BlockSpec(memory_space=pltpu.VMEM)
    dma = pltpu.SemaphoreType.DMA
    f, g = pl.pallas_call(
        kernel,
        out_shape=(jax.ShapeDtypeStruct((1, ROWS), F32), jax.ShapeDtypeStruct((1, COLS), F32)),
        in_specs=[hbm, hbm, hbm],
        out_specs=(vmem, vmem),
        scratch_shapes=[
            pltpu.VMEM((NX, ROWS, WIDTH), BF16),
            pltpu.VMEM((1, COLS), F32),
            pltpu.VMEM((1, ROWS), F32),
            pltpu.VMEM((2 * CHIPS, COLS, WIDTH), BF16),
            pltpu.VMEM((2 * CHIPS, 1, 128), F32),
            pltpu.VMEM((2 * CHIPS, COLS, NX * ROWS), F32),
            pltpu.VMEM((8, NX * ROWS), F32),
            pltpu.VMEM((8, NX * ROWS), F32),
            pltpu.VMEM((NX, NX, 1, ROWS), F32),
            pltpu.VMEM((BATCH, 128), F32),
            pltpu.VMEM((BATCH, 128), F32),
            pltpu.VMEM((8, BATCH // 128, 1, 128), F32),
            pltpu.VMEM((2 * CHIPS, 1, 128), F32),
            pltpu.VMEM((2, 1, 128), F32),
            dma((3,)), dma((2,)), dma((2,)),
            dma((2, 2)), dma((2, 2)), dma((2, 5, 2)), dma((2, 5, 2)), dma((2, 8)), dma((2, 8)),
            dma, dma, dma, dma, dma, dma,
        ],
        compiler_params=pltpu.CompilerParams(
            collective_id=0, has_side_effects=True, vmem_limit_bytes=40 * 2**20
        ),
    )(*[
        pltpu.with_memory_space_constraint(array, pltpu.HBM)
        for array in (gen_samples, data_samples, data_potential.reshape(1, COLS))
    ])
    return f.reshape(ROWS), g.reshape(COLS)


def solution(mesh):
    in_specs = (P(("gen", "dat"), None), P(("dat", "gen"), None), P(("dat", "gen")))
    out_specs = (P(("gen", "dat")), P(("dat", "gen")))
    return jax.shard_map(
        per_device, mesh=mesh, in_specs=in_specs, out_specs=out_specs, check_vma=False
    )
```
